128 devices in a mesh: seg: 32 (over x_lo, z, y), pair: 4 (over x_hi, core).
Axes of the slice: x: 4 (x_hi: 2, x_lo: 2; x = x_hi * 2 + x_lo), y: 4, z: 4, core: 2. Of those that a mesh axis runs over, the one named last changes fastest.
Arguments:
- embeddings: bfloat16 [98304, 768], P(('seg', 'pair')), may hold values from -60 to 60
- cluster_id: int32 [98304], P(('seg', 'pair')), may hold values from 0 to 127, as said below
- cluster_rank: int32 [98304], P(('seg', 'pair')), may hold values from 0 to 2687, as said below
- dest_slot: int32 [98304], P(('seg', 'pair')), may hold values from 0 to 98303, as said below
Outputs:
- best_all: float32 [98304], P(('seg', 'pair'))
- best_higher: float32 [98304], P(('seg', 'pair'))
The draws below stay inside these ranges and needn't reach their ends.
Inputs may be any that keep to these rules, and one draw needn't show every extreme that they name: `cluster_id`: rows of one cluster share an id, distinct clusters have distinct ids, and a cluster fills 192 to 2688 consecutive cycle positions (dest_slot, modulo 98304); clusters of both sizes occur. `cluster_rank`: within each cluster the ranks are 0 to its size - 1, each once. `dest_slot`: a permutation of the rows onto cycle positions; the device with seg index a and pair index b holds storage rows a * 4 + b and owns cycle positions (a * 4 + b) * 768 to (a * 4 + b + 1) * 768 - 1; each device's rows fall on at most 9 positions owned by any one device, and on exactly 9 of some device's.
All inputs are finite; a program needn't handle non-finite values.
Results may differ from the reference program's by a relative error of at most 0.00051.
Values may be sent and summed in bfloat16 or wider, within the bound.
No kernel may reach another device: no remote copies, remote signals or barrier semaphores. Data moves between devices by JAX's collectives and lax.ppermute only.
A program may use at most 128 MiB of HBM per device.

```python
import math
import jax
import jax.numpy as jnp
from jax import lax

D = 768
ROWS_DEV = 768
ROWS = 98304
SEG_ROWS = 3072
MINC = 192
N_SEG = 32
N_PAIR = 4


def cycle_layout(key):
    halfway = SEG_ROWS // 2
    pieces = 2 * N_SEG
    device_count = N_SEG * N_PAIR
    subkeys = jax.random.split(key, 10)
    cut_at = jax.random.randint(subkeys[0], (pieces,), MINC, halfway - MINC + 1, dtype=jnp.int32)
    cut_at = cut_at.at[0].set(MINC).at[1].set(halfway - MINC)
    opens = jax.random.randint(subkeys[1], (pieces,), 0, 2, dtype=jnp.int32)
    opens = opens.at[0].set(1).at[1].set(0)
    position = jnp.arange(ROWS, dtype=jnp.int32)
    piece_of = position // halfway
    inside = position - piece_of * halfway
    boundary = (inside == cut_at[piece_of]) | (inside == 0) & (opens[piece_of] == 1)
    ordinal = jnp.cumsum(boundary.astype(jnp.int32)) - 1
    first_at = lax.cummax(jnp.where(boundary, position, 0), axis=0)
    shuffle = jax.random.permutation(subkeys[2], ROWS).astype(jnp.int32)
    sorted_at = jnp.lexsort((shuffle, ordinal)).astype(jnp.int32)
    ranking = jnp.zeros((ROWS,), jnp.int32).at[sorted_at].set(position - first_at[sorted_at])
    final_cluster = ordinal[ROWS - 1]
    ordinal = jnp.where(ordinal == final_cluster, 4 * N_SEG - 1, ordinal).astype(jnp.int32)
    duplicate = (jax.random.randint(subkeys[3], (ROWS,), 0, 3, dtype=jnp.int32) == 0) & jnp.logical_not(boundary)
    offset = jax.random.randint(subkeys[4], (), 0, ROWS, dtype=jnp.int32)
    base_count = ROWS_DEV // device_count
    spread = base_count // 2
    heights = jax.random.randint(subkeys[5], (device_count,), 0, spread + 1, dtype=jnp.int32)
    heights = heights.at[0].set(spread).at[device_count - 1].set(0)
    rises = heights - jnp.roll(heights, 1)
    dest_perm = jax.random.permutation(subkeys[6], device_count).astype(jnp.int32)
    source_perm = jax.random.permutation(subkeys[7], device_count).astype(jnp.int32)
    counts = base_count + rises[(dest_perm[None, :] - source_perm[:, None]) % device_count]
    ends_out = jnp.cumsum(counts, axis=1)
    starts_out = ends_out - counts
    starts_in = jnp.cumsum(counts, axis=0) - counts
    slot_index = jnp.arange(ROWS_DEV, dtype=jnp.int32)
    target = jnp.sum((ends_out[:, None, :] <= slot_index[None, :, None]).astype(jnp.int32), axis=2)
    source_ids = jnp.arange(device_count, dtype=jnp.int32)[:, None]
    within = slot_index[None, :] - starts_out[source_ids, target]
    arrival = starts_in[source_ids, target] + within
    place_perm = jax.vmap(lambda sub_key: jax.random.permutation(sub_key, ROWS_DEV).astype(jnp.int32))(jax.random.split(subkeys[8], device_count))
    landing = target * ROWS_DEV + place_perm[target, arrival]
    store_perm = jax.vmap(lambda sub_key: jax.random.permutation(sub_key, ROWS_DEV).astype(jnp.int32))(jax.random.split(subkeys[9], device_count))
    placed = jnp.zeros((device_count, ROWS_DEV), jnp.int32).at[source_ids, store_perm].set(landing)
    return (ordinal, ranking, duplicate, offset, placed.reshape(-1))


def draw_cluster_id(key, part):
    ordinal, ranking, duplicate, offset, placed = cycle_layout(key)
    return jnp.roll(ordinal, offset)[placed].astype(jnp.int32)


def draw_cluster_rank(key, part):
    ordinal, ranking, duplicate, offset, placed = cycle_layout(key)
    return jnp.roll(ranking, offset)[placed].astype(jnp.int32)


def draw_dest_slot(key, part):
    ordinal, ranking, duplicate, offset, placed = cycle_layout(key)
    return placed.astype(jnp.int32)


def draw_embeddings(key, part):
    ordinal, ranking, duplicate, offset, placed = cycle_layout(key)
    key = jax.random.fold_in(key, 31)
    centre_key, noise_key, scale_key = jax.random.split(key, 3)
    centres = jax.random.normal(centre_key, (4 * N_SEG, D), jnp.float32)
    fresh = jax.random.normal(noise_key, (ROWS, D), jnp.float32)
    scales = jnp.exp(jax.random.uniform(scale_key, (ROWS,), jnp.float32, 0.0, math.log(10.0)))
    earlier = jnp.roll(fresh, 1, axis=0)
    noise = jnp.where(duplicate[:, None], 0.9 * earlier + 0.45 * fresh, fresh)
    values = (centres[ordinal] + noise) * scales[:, None]
    values = jnp.clip(values, -60.0, 60.0)
    return jnp.roll(values, offset, axis=0)[placed].astype(jnp.bfloat16)


def setup_inputs(seed: int = 0) -> dict:
    streams_of = jax.random.split(jax.random.key(seed), 5)
    return {
        "embeddings": draw_embeddings(jax.random.fold_in(streams_of[4], 71), 0),
        "cluster_id": draw_cluster_id(jax.random.fold_in(streams_of[4], 71), 0),
        "cluster_rank": draw_cluster_rank(jax.random.fold_in(streams_of[4], 71), 0),
        "dest_slot": draw_dest_slot(jax.random.fold_in(streams_of[4], 71), 0),
    }


def unit_rows(embeddings):
    values = embeddings.astype(jnp.float32)
    scaling = lax.rsqrt(lax.optimization_barrier(jnp.sum(values * values, axis=1, keepdims=True)) + 1e-06)
    return (values * scaling).astype(jnp.bfloat16)

def masked_best(queries, query_cid, query_rank, key_rows, key_cid, key_rank):
    cosine = jnp.dot(queries, key_rows.T, preferred_element_type=jnp.float32)
    same_cluster = query_cid[:, None] == key_cid[None, :]
    peer_mask = same_cluster & (query_rank[:, None] != key_rank[None, :])
    higher = same_cluster & (key_rank[None, :] < query_rank[:, None])
    lower_mask = same_cluster & (query_rank[:, None] < key_rank[None, :])
    row_all = lax.optimization_barrier(jnp.max(jnp.where(peer_mask, cosine, -1.0), axis=1))
    row_high = lax.optimization_barrier(jnp.max(jnp.where(higher, cosine, -1.0), axis=1))
    col_all = lax.optimization_barrier(jnp.max(jnp.where(peer_mask, cosine, -1.0), axis=0))
    col_high = lax.optimization_barrier(jnp.max(jnp.where(lower_mask, cosine, -1.0), axis=0))
    return (row_all, row_high, col_all, col_high)

def segment_terms(operands):
    queries, query_cid, query_rank, key_rows, key_cid, key_rank = operands
    own_all, own_high, unused_all, unused_high = masked_best(queries, query_cid, query_rank, queries, query_cid, query_rank)
    next_all, next_high, col_all, col_high = masked_best(queries, query_cid, query_rank, key_rows, key_cid, key_rank)
    return (jnp.maximum(own_all, next_all), jnp.maximum(own_high, next_high), col_all, col_high)

def reference(embeddings, cluster_id, cluster_rank, dest_slot):
    normed = unit_rows(embeddings)
    cycle_unit = jnp.zeros_like(normed).at[dest_slot].set(normed)
    cycle_cid = jnp.zeros(cluster_id.shape, jnp.int32).at[dest_slot].set(cluster_id)
    cycle_rank = jnp.zeros(cluster_rank.shape, jnp.int32).at[dest_slot].set(cluster_rank)
    cycle_units = cycle_unit.reshape(N_SEG, SEG_ROWS, normed.shape[1])
    cycle_cids = cycle_cid.reshape(N_SEG, SEG_ROWS)
    cycle_ranks = cycle_rank.reshape(N_SEG, SEG_ROWS)
    row_all, row_high, col_all, col_high = lax.map(segment_terms, (cycle_units, cycle_cids, cycle_ranks, jnp.roll(cycle_units, -1, axis=0), jnp.roll(cycle_cids, -1, axis=0), jnp.roll(cycle_ranks, -1, axis=0)))
    best_all = jnp.maximum(row_all, jnp.roll(col_all, 1, axis=0)).reshape(-1)
    best_higher = jnp.maximum(row_high, jnp.roll(col_high, 1, axis=0)).reshape(-1)
    return (best_all[dest_slot], best_higher[dest_slot])
```

```python
import jax
import jax.numpy as jnp
from jax import lax
from jax.experimental import pallas as pl
from jax.experimental.pallas import tpu as pltpu
from jax.sharding import PartitionSpec as P

AXES = ("seg", "pair")
DEVICES = 128
CHIPS = 64
ROWS = 768
HALF = 384
CAP = 9
SLOTS = DEVICES * CAP
MAIN = DEVICES * 8
META = 16
ROLES = 5
BF = jnp.bfloat16
F32 = jnp.float32
NT = (((1,), (1,)), ((), ()))


def device_of(block):
    block = block & (DEVICES - 1)
    chip, core = block >> 1, block & 1
    high, mid, low = chip >> 4, (chip >> 2) & 3, chip & 3
    x, y, z = (mid - high) & 3, (low - mid) & 3, high
    return ((((x & 1) * 4 + z) * 4 + y) << 2) + ((x >> 1) << 1) + core


def routes(source_of, targets):
    return [(device_of(source_of(t)), device_of(t)) for t in targets]


def iota(shape, dim):
    return lax.broadcasted_iota(jnp.int32, shape, dim)


def dot(a, b):
    return jnp.dot(a, b, preferred_element_type=F32)


def dot_nt(a, b):
    return lax.dot_general(a, b, NT, preferred_element_type=F32)


def split_slot(slot):
    block = ((slot >> 8) * 171) >> 9
    return block, slot - block * ROWS


def place(slot):
    block, local = split_slot(slot)
    device = device_of(block)
    to_device = (iota((DEVICES, ROWS), 0) == device).astype(BF)
    earlier = (iota((ROWS, ROWS), 0) < iota((ROWS, ROWS), 1)).astype(BF)
    before = dot(to_device, earlier)
    within = jnp.sum(to_device.astype(F32) * before, axis=0, keepdims=True).astype(jnp.int32)
    return block, device, local, within, to_device


def pack_kernel(emb_ref, cid_ref, rank_ref, slot_ref, out_ref, unit, extra):
    values = emb_ref[...].astype(F32)
    scaling = lax.rsqrt(jnp.sum(values * values, axis=1, keepdims=True) + 1e-06)
    unit[...] = (values * scaling).astype(BF)
    _, device, local, within, to_device = place(slot_ref[...])
    flat = jnp.where(within < 8, device * 8 + within, -1)
    for start in range(0, MAIN, 256):
        pick = (iota((256, ROWS), 0) + start == flat).astype(BF)
        out_ref[start : start + 256, :ROWS] = dot(pick, unit[...]).astype(BF)
    ninth = jnp.where(within == 8, to_device, jnp.zeros_like(to_device))
    ninth_rows = dot(ninth, unit[...])
    field = iota((DEVICES, ROWS), 0) >> 4
    cid, rank = cid_ref[...], rank_ref[...]
    meta = jnp.where(field == 0, (local >> 8) + 1, jnp.where(field == 1, local & 255, jnp.where(field == 2, cid + 1, 0)))
    meta = jnp.where(field == 3, rank >> 8, jnp.where(field == 4, rank & 255, meta))
    meta = jnp.where((iota((DEVICES, ROWS), 0) & 15) == within, meta, 0).astype(F32).astype(BF)
    extra[...] = jnp.zeros_like(extra)
    for part in range(6):
        extra[pl.ds(part, DEVICES, stride=8), :] = ninth_rows[:, part * 128 : (part + 1) * 128]
    extra[pl.ds(6, DEVICES, stride=8), :] = dot_nt(to_device, meta)
    out_ref[:, ROWS:] = extra[...].astype(BF)


def unpack_kernel(got_ref, out_ref, extra, spread):
    extra[...] = got_ref[:, ROWS:].astype(F32)
    ninth_rows = jnp.concatenate([extra[pl.ds(part, DEVICES, stride=8), :] for part in range(6)], axis=1).astype(BF)
    meta = extra[pl.ds(6, DEVICES, stride=8), :]
    for order in range(8):
        spread[pl.ds(order, DEVICES, stride=8), :] = meta
    lane, row = iota((MAIN, 128), 1), iota((MAIN, 128), 0)
    main = jnp.where((lane & 15) == (row & 7), spread[...], 0.0).astype(BF)
    last = jnp.where((iota((DEVICES, 128), 1) & 15) == 8, meta, 0.0).astype(BF)
    fields = ((iota((META, 128), 1) >> 4) == iota((META, 128), 0)).astype(BF)
    by_slot = jnp.concatenate([dot_nt(fields, main), dot_nt(fields, last)], axis=1)
    slot = ((by_slot[0:1] - 1.0) * 256.0 + by_slot[1:2]).astype(jnp.int32)
    cols = by_slot.astype(BF)
    for start in range(0, ROWS, 256):
        pick = (iota((256, SLOTS), 0) + start == slot).astype(BF)
        rows = dot(pick[:, :MAIN], got_ref[:, :ROWS]) + dot(pick[:, MAIN:], ninth_rows)
        out_ref[start : start + 256, :] = rows.astype(BF)
        placed = dot_nt(cols, pick)
        kept = jnp.concatenate([placed[2:5], jnp.zeros((13, 256), F32)], axis=0)
        out_ref[ROWS:, start : start + 256] = kept.astype(BF)
    out_ref[ROWS + 8 : ROWS + 9, :] = cols[0:1, :ROWS]
    out_ref[ROWS + 9 : ROWS + 10, :] = cols[1:2, :ROWS]
    out_ref[ROWS + 10 : ROWS + 11, :HALF] = cols[0:1, ROWS:]
    out_ref[ROWS + 11 : ROWS + 12, :HALF] = cols[1:2, ROWS:]


def read_meta(block_ref, rows):
    meta = block_ref[rows:, :].astype(F32)
    cid, rank = meta[0:1], meta[1:2] * 256.0 + meta[2:3]
    high = jnp.concatenate([meta[8:9], meta[10:11, :HALF]], axis=1)
    low = jnp.concatenate([meta[9:10], meta[11:12, :HALF]], axis=1)
    slot = ((high - 1.0) * 256.0 + low).astype(jnp.int32)
    return cid, rank, slot


def columns(cid, rank):
    both = jnp.concatenate([cid, rank, jnp.zeros((6, ROWS), F32)], axis=0)
    turned = jnp.transpose(both)
    return turned[:, 0:1], turned[:, 1:2]


def local_kernel(own_ref, other_ref, out_ref):
    own_cid, own_rank, _ = read_meta(own_ref, ROWS)
    best_all = jnp.full((8, ROWS), -1.0, F32)
    best_high = jnp.full((8, ROWS), -1.0, F32)
    for ref in (own_ref, other_ref):
        cid, rank, _ = read_meta(ref, ROWS)
        cid, rank = columns(cid, rank)
        for start in range(0, ROWS, 256):
            cosine = dot_nt(ref[start : start + 256, :], own_ref[:ROWS, :])
            c, r = cid[start : start + 256], rank[start : start + 256]
            near = jnp.where((c == own_cid) & (r != own_rank), cosine, -1.0)
            high = jnp.where(r < own_rank, near, -1.0)
            best_all = jnp.maximum(best_all, jnp.max(near.reshape(32, 8, ROWS), axis=0))
            best_high = jnp.maximum(best_high, jnp.max(high.reshape(32, 8, ROWS), axis=0))
    out_ref[0:1, :] = jnp.max(best_all, axis=0, keepdims=True)
    out_ref[1:2, :] = jnp.max(best_high, axis=0, keepdims=True)
    out_ref[2:, :] = jnp.full((6, ROWS), -1.0, F32)


def against(key_ref, rows, key_cid, key_rank, other_ref, first, count, other_cid, other_rank):
    key_all, key_high = [], []
    best_all = jnp.full((8, count), -1.0, F32)
    best_high = jnp.full((8, count), -1.0, F32)
    for start in range(0, rows, 128):
        cosine = dot_nt(key_ref[start : start + 128, :], other_ref[first : first + count, :])
        near = jnp.where(key_cid[start : start + 128] == other_cid, cosine, -1.0)
        before = other_rank < key_rank[start : start + 128]
        high = jnp.where(before, near, -1.0)
        low = jnp.where(before, -1.0, near)
        best_all = jnp.maximum(best_all, jnp.max(near.reshape(16, 8, count), axis=0))
        best_high = jnp.maximum(best_high, jnp.max(low.reshape(16, 8, count), axis=0))
        wide_all, wide_high = near[:, :128], high[:, :128]
        for lane in range(128, count, 128):
            wide_all = jnp.maximum(wide_all, near[:, lane : lane + 128])
            wide_high = jnp.maximum(wide_high, high[:, lane : lane + 128])
        key_all.append(wide_all)
        key_high.append(wide_high)
    best_all = jnp.max(best_all, axis=0, keepdims=True)
    best_high = jnp.max(best_high, axis=0, keepdims=True)
    return jnp.concatenate(key_all, axis=0), jnp.concatenate(key_high, axis=0), best_all, best_high


def far_kernel(key_ref, own_ref, other_ref, prev_ref, tail_ref, local_ref, out_ref, by_slot):
    key_cid, key_rank, key_slot = read_meta(key_ref, ROWS)
    cid_col, rank_col = columns(key_cid, key_rank)
    key_all = jnp.full((ROWS, 128), -1.0, F32)
    key_high = jnp.full((ROWS, 128), -1.0, F32)
    found = []
    for ref in (own_ref, other_ref, prev_ref):
        cid, rank, slot = read_meta(ref, ROWS)
        wide_all, wide_high, best_all, best_high = against(key_ref, ROWS, cid_col, rank_col, ref, 0, ROWS, cid, rank)
        key_all = jnp.maximum(key_all, wide_all)
        key_high = jnp.maximum(key_high, wide_high)
        found.append((best_all, best_high, slot))
    cid, rank, slot = read_meta(tail_ref, HALF)
    wide_all, wide_high, best_all, best_high = against(
        key_ref, HALF, cid_col, rank_col, tail_ref, 0, HALF, cid[:, HALF:], rank[:, HALF:]
    )
    key_all = jnp.concatenate([jnp.maximum(key_all[:HALF], wide_all), key_all[HALF:]], axis=0)
    key_high = jnp.concatenate([jnp.maximum(key_high[:HALF], wide_high), key_high[HALF:]], axis=0)
    key_all = jnp.max(jnp.transpose(key_all), axis=0, keepdims=True)
    key_high = jnp.max(jnp.transpose(key_high), axis=0, keepdims=True)
    own_all = jnp.maximum(found[0][0], local_ref[0:1, :])
    own_high = jnp.maximum(found[0][1], local_ref[1:2, :])
    parts = [
        (own_all, own_high, found[0][2]),
        found[1],
        (key_all, key_high, key_slot),
        found[2],
        (best_all, best_high, slot - HALF),
    ]
    total = jnp.zeros((128, SLOTS), F32)
    for role, (value_all, value_high, slot) in enumerate(parts):
        count = value_all.shape[1]
        pick = (iota((count, SLOTS), 0) == slot).astype(BF)
        stacked = jnp.zeros((128, count), F32)
        row = iota((128, count), 0)
        for which, value in enumerate((value_all, value_high)):
            rest = value
            for piece in range(3):
                rounded = rest.astype(BF).astype(F32)
                rest = rest - rounded
                stacked = jnp.where(row == piece * 32 + role * 2 + which, rounded, stacked)
        total = total + dot(stacked.astype(BF), pick)
    total = total[0:32] + total[32:64] + total[64:96]
    total = jnp.concatenate([total, jnp.zeros((96, SLOTS), F32)], axis=0)
    by_slot[...] = jnp.transpose(total)
    reply = by_slot[pl.ds(0, DEVICES, stride=8), :]
    for order in range(1, 8):
        reply = reply + pltpu.roll(by_slot[pl.ds(order, DEVICES, stride=8), :], order * 2 * ROLES, 1)
    reply = reply + pltpu.roll(by_slot[MAIN:, :], 16 * ROLES, 1)
    out_ref[...] = reply


def answer_kernel(got_ref, slot_ref, out_ref):
    block, device, local, within, _ = place(slot_ref[...])
    replies = jnp.transpose(got_ref[...])
    pieces = []
    rest = replies
    for piece in range(3):
        rounded = rest.astype(BF)
        pieces.append(rounded)
        rest = rest - rounded.astype(F32)
    pieces = jnp.concatenate(pieces, axis=1)
    senders = (device, device_of(block ^ 1), device_of(block - 2), device_of(block + 1), device_of(block + 2))
    valid = (None, None, None, (block & 1) == 1, local >= HALF)
    lane = iota((128, ROWS), 0)
    result = [None, None]
    for role in range(ROLES):
        sent = (iota((DEVICES, ROWS), 0) == senders[role]).astype(BF)
        lines = dot(pieces, jnp.concatenate([sent, sent, sent], axis=0))
        for which in range(2):
            mine = jnp.where(lane == within * (2 * ROLES) + role * 2 + which, lines, 0.0)
            value = jnp.sum(mine, axis=0, keepdims=True)
            if valid[role] is not None:
                value = jnp.where(valid[role], value, -1.0)
            result[which] = value if result[which] is None else jnp.maximum(result[which], value)
    out_ref[...] = jnp.concatenate([result[0], result[1], jnp.zeros((6, ROWS), F32)], axis=0)


def call(kernel, out, args, scratch=(), flops=0, name=None):
    moved = sum(a.size * a.dtype.itemsize for a in args)
    return pl.pallas_call(
        kernel,
        out_shape=jax.ShapeDtypeStruct(*out),
        in_specs=[pl.BlockSpec(memory_space=pltpu.VMEM)] * len(args),
        out_specs=pl.BlockSpec(memory_space=pltpu.VMEM),
        scratch_shapes=list(scratch),
        compiler_params=pltpu.CompilerParams(vmem_limit_bytes=48 * 1024 * 1024),
        cost_estimate=pl.CostEstimate(flops=flops, bytes_accessed=moved, transcendentals=0),
        name=name,
    )(*args)


def body(embeddings, cluster_id, cluster_rank, dest_slot):
    cid, rank, slot = (a.reshape(1, ROWS) for a in (cluster_id, cluster_rank, dest_slot))
    send = call(
        pack_kernel,
        ((MAIN, ROWS + 128), BF),
        (embeddings, cid, rank, slot),
        (pltpu.VMEM((ROWS, ROWS), BF), pltpu.VMEM((MAIN, 128), F32)),
        name="pack",
    )
    got = lax.all_to_all(send, AXES, split_axis=0, concat_axis=0, tiled=True)
    own = call(
        unpack_kernel,
        ((ROWS + META, ROWS), BF),
        (got,),
        (pltpu.VMEM((MAIN, 128), F32), pltpu.VMEM((MAIN, 128), F32)),
        name="unpack",
    )
    everyone = range(DEVICES)
    other = lax.ppermute(own, AXES, routes(lambda t: t ^ 1, everyone))
    key = lax.ppermute(own, AXES, routes(lambda t: t + 2, everyone))
    prev = lax.ppermute(own, AXES, routes(lambda t: t - 1, range(0, DEVICES, 2)))
    tail = lax.ppermute(own[HALF:], AXES, routes(lambda t: t - 2, everyone))
    tile = 2 * ROWS**3
    local = call(local_kernel, ((8, ROWS), F32), (own, other), flops=2 * tile, name="local")
    reply = call(
        far_kernel,
        ((DEVICES, 128), F32),
        (key, own, other, prev, tail, local),
        (pltpu.VMEM((SLOTS, 128), F32),),
        flops=4 * tile,
        name="far",
    )
    answer = lax.all_to_all(reply.reshape(DEVICES, 1, 128), AXES, split_axis=0, concat_axis=0, tiled=True)
    out = call(answer_kernel, ((8, ROWS), F32), (answer.reshape(DEVICES, 128), slot), name="answer")
    return out[0], out[1]


def solution(mesh):
    rows = P(AXES)
    return jax.shard_map(
        body,
        mesh=mesh,
        in_specs=(P(AXES, None), rows, rows, rows),
        out_specs=(rows, rows),
        check_vma=False,
    )
```

```python
import jax
import jax.numpy as jnp
from jax import lax
from jax.experimental import pallas as pl
from jax.experimental.pallas import tpu as pltpu
from jax.sharding import PartitionSpec as P

AXES = ("seg", "pair")
DEVICES = 128
CHIPS = [
    (2, 0, 1), (2, 1, 1), (2, 1, 2), (2, 1, 3), (2, 2, 3), (1, 2, 3), (1, 2, 0), (0, 2, 0),
    (0, 1, 0), (0, 1, 1), (1, 1, 1), (1, 2, 1), (2, 2, 1), (2, 2, 0), (2, 1, 0), (1, 1, 0),
    (1, 1, 3), (0, 1, 3), (3, 1, 3), (3, 1, 2), (0, 1, 2), (0, 0, 2), (0, 0, 3), (0, 0, 0),
    (1, 0, 0), (2, 0, 0), (2, 0, 3), (3, 0, 3), (3, 3, 3), (3, 2, 3), (3, 2, 0), (3, 2, 1),
    (3, 1, 1), (3, 1, 0), (3, 0, 0), (3, 3, 0), (3, 3, 1), (2, 3, 1), (1, 3, 1), (1, 0, 1),
    (0, 0, 1), (0, 3, 1), (0, 2, 1), (0, 2, 2), (0, 2, 3), (0, 3, 3), (0, 3, 0), (1, 3, 0),
    (2, 3, 0), (2, 3, 3), (1, 3, 3), (1, 0, 3), (1, 0, 2), (1, 1, 2), (1, 2, 2), (1, 3, 2),
    (0, 3, 2), (3, 3, 2), (3, 2, 2), (2, 2, 2), (2, 3, 2), (2, 0, 2), (3, 0, 2), (3, 0, 1),
]
ROWS = 768
HALF = 384
CAP = 9
SLOTS = DEVICES * CAP
MAIN = DEVICES * 8
META = 16
ROLES = 5
BF = jnp.bfloat16
F32 = jnp.float32
NT = (((1,), (1,)), ((), ()))


def chip_device(x, y, z):
    return ((((x & 1) * 4 + z) * 4 + y) << 2) + ((x >> 1) << 1)


WALK = [chip_device(*chip) for chip in CHIPS]


def device_of(block):
    block = block % DEVICES
    return WALK[block >> 1] + (block & 1)


def routes(source_of, targets):
    return [(device_of(source_of(t)), device_of(t)) for t in targets]


def iota(shape, dim):
    return lax.broadcasted_iota(jnp.int32, shape, dim)


def dot(a, b):
    return jnp.dot(a, b, preferred_element_type=F32)


def dot_nt(a, b):
    return lax.dot_general(a, b, NT, preferred_element_type=F32)


def split_slot(slot):
    block = ((slot >> 8) * 171) >> 9
    return block, slot - block * ROWS


def device_table():
    row, lane = iota((8, DEVICES), 0), iota((8, DEVICES), 1)
    step = jnp.where(row == 2, -2, jnp.where(row == 3, 1, jnp.where(row == 4, 2, 0)))
    block = jnp.where(row == 1, lane ^ 1, lane + step) & (DEVICES - 1)
    chip = block >> 1
    found = block & 1
    for index, device in enumerate(WALK):
        found = found + jnp.where(chip == index, device, 0)
    return found.astype(F32).astype(BF)


def pack_kernel(emb_ref, cid_ref, rank_ref, slot_ref, out_ref, route_ref, raw, slots, cids, ranks, unit, extra, sems):
    ids = ((slot_ref, slots), (cid_ref, cids), (rank_ref, ranks))
    small = [pltpu.make_async_copy(*pair, sems.at[3 + i]) for i, pair in enumerate(ids)]
    copies = [
        pltpu.make_async_copy(emb_ref.at[pl.ds(part * 256, 256)], raw.at[pl.ds(part * 256, 256)], sems.at[part])
        for part in range(3)
    ]
    for copy in small + copies:
        copy.start()
    table = device_table()
    earlier = (iota((ROWS, ROWS), 0) < iota((ROWS, ROWS), 1)).astype(BF)
    for copy in small:
        copy.wait()
    slot, cid, rank = (ref[...].reshape(1, ROWS) for _, ref in ids)
    block, local = split_slot(slot)
    to_block = (iota((DEVICES, ROWS), 0) == block).astype(BF)
    within = jnp.sum(to_block.astype(F32) * dot(to_block, earlier), axis=0, keepdims=True).astype(jnp.int32)
    senders = dot(table, to_block).astype(jnp.int32)
    row = iota((8, ROWS), 0)
    dropped = ((row == 3) & ((block & 1) == 0)) | ((row == 4) & (local < HALF))
    route_ref[...] = jnp.where(row == 5, within, jnp.where(dropped, -1, senders))
    device = senders[0:1]
    to_device = (iota((DEVICES, ROWS), 0) == device).astype(BF)
    flat = jnp.where(within < 8, device * 8 + within, -1)
    for part, copy in enumerate(copies):
        copy.wait()
        values = raw[part * 256 : (part + 1) * 256, :].astype(F32)
        scaling = lax.rsqrt(jnp.sum(values * values, axis=1, keepdims=True) + 1e-06)
        unit[part * 256 : (part + 1) * 256, :] = (values * scaling).astype(BF)
    for start in range(0, MAIN, 256):
        pick = (iota((256, ROWS), 0) + start == flat).astype(BF)
        out_ref[start : start + 256, :ROWS] = dot(pick, unit[...]).astype(BF)
    ninth = jnp.where(within == 8, to_device, jnp.zeros_like(to_device))
    ninth_rows = dot(ninth, unit[...])
    field = iota((DEVICES, ROWS), 0) >> 4
    meta = jnp.where(field == 0, (local >> 8) + 1, jnp.where(field == 1, local & 255, jnp.where(field == 2, cid + 1, 0)))
    meta = jnp.where(field == 3, rank >> 8, jnp.where(field == 4, rank & 255, meta))
    meta = jnp.where((iota((DEVICES, ROWS), 0) & 15) == within, meta, 0).astype(F32).astype(BF)
    extra[...] = jnp.zeros_like(extra)
    for part in range(6):
        extra[pl.ds(part, DEVICES, stride=8), :] = ninth_rows[:, part * 128 : (part + 1) * 128]
    extra[pl.ds(6, DEVICES, stride=8), :] = dot_nt(to_device, meta)
    out_ref[:, ROWS:] = extra[...].astype(BF)


def unpack_kernel(got_ref, out_ref, extra, spread):
    extra[...] = got_ref[:, ROWS:].astype(F32)
    ninth_rows = jnp.concatenate([extra[pl.ds(part, DEVICES, stride=8), :] for part in range(6)], axis=1).astype(BF)
    meta = extra[pl.ds(6, DEVICES, stride=8), :]
    for order in range(8):
        spread[pl.ds(order, DEVICES, stride=8), :] = meta
    lane, row = iota((MAIN, 128), 1), iota((MAIN, 128), 0)
    main = jnp.where((lane & 15) == (row & 7), spread[...], 0.0).astype(BF)
    last = jnp.where((iota((DEVICES, 128), 1) & 15) == 8, meta, 0.0).astype(BF)
    fields = ((iota((META, 128), 1) >> 4) == iota((META, 128), 0)).astype(BF)
    by_slot = jnp.concatenate([dot_nt(fields, main), dot_nt(fields, last)], axis=1)
    slot = ((by_slot[0:1] - 1.0) * 256.0 + by_slot[1:2]).astype(jnp.int32)
    cols = by_slot.astype(BF)
    for start in range(0, ROWS, 256):
        pick = (iota((256, SLOTS), 0) + start == slot).astype(BF)
        rows = dot(pick[:, :MAIN], got_ref[:, :ROWS]) + dot(pick[:, MAIN:], ninth_rows)
        out_ref[start : start + 256, :] = rows.astype(BF)
        placed = dot_nt(cols, pick)
        kept = jnp.concatenate([placed[2:5], jnp.zeros((13, 256), F32)], axis=0)
        out_ref[ROWS:, start : start + 256] = kept.astype(BF)
    out_ref[ROWS + 8 : ROWS + 9, :] = cols[0:1, :ROWS]
    out_ref[ROWS + 9 : ROWS + 10, :] = cols[1:2, :ROWS]
    out_ref[ROWS + 10 : ROWS + 11, :HALF] = cols[0:1, ROWS:]
    out_ref[ROWS + 11 : ROWS + 12, :HALF] = cols[1:2, ROWS:]


def read_meta(block_ref, rows):
    meta = block_ref[rows:, :].astype(F32)
    cid, rank = meta[0:1], meta[1:2] * 256.0 + meta[2:3]
    high = jnp.concatenate([meta[8:9], meta[10:11, :HALF]], axis=1)
    low = jnp.concatenate([meta[9:10], meta[11:12, :HALF]], axis=1)
    slot = ((high - 1.0) * 256.0 + low).astype(jnp.int32)
    return cid, rank, slot


def columns(cid, rank):
    both = jnp.concatenate([cid, rank, jnp.zeros((6, ROWS), F32)], axis=0)
    turned = jnp.transpose(both)
    return turned[:, 0:1], turned[:, 1:2]


def local_kernel(own_ref, other_ref, out_ref):
    own_cid, own_rank, _ = read_meta(own_ref, ROWS)
    best_all = jnp.full((8, ROWS), -1.0, F32)
    best_high = jnp.full((8, ROWS), -1.0, F32)
    for ref in (own_ref, other_ref):
        cid, rank, _ = read_meta(ref, ROWS)
        cid, rank = columns(cid, rank)
        for start in range(0, ROWS, 256):
            cosine = dot_nt(ref[start : start + 256, :], own_ref[:ROWS, :])
            c, r = cid[start : start + 256], rank[start : start + 256]
            near = jnp.where((c == own_cid) & (r != own_rank), cosine, -1.0)
            high = jnp.where(r < own_rank, near, -1.0)
            best_all = jnp.maximum(best_all, jnp.max(near.reshape(32, 8, ROWS), axis=0))
            best_high = jnp.maximum(best_high, jnp.max(high.reshape(32, 8, ROWS), axis=0))
    out_ref[0:1, :] = jnp.max(best_all, axis=0, keepdims=True)
    out_ref[1:2, :] = jnp.max(best_high, axis=0, keepdims=True)
    out_ref[2:, :] = jnp.full((6, ROWS), -1.0, F32)


def against(key, key_cid, key_rank, other_ref, count, other_cid, other_rank):
    cosine = dot_nt(key, other_ref[:count, :])
    near = jnp.where(key_cid == other_cid, cosine, -1.0)
    before = other_rank < key_rank
    high = jnp.where(before, near, -1.0)
    low = jnp.where(before, -1.0, near)
    wide_all, wide_high = near[:, :128], high[:, :128]
    for lane in range(128, count, 128):
        wide_all = jnp.maximum(wide_all, near[:, lane : lane + 128])
        wide_high = jnp.maximum(wide_high, high[:, lane : lane + 128])
    return wide_all, wide_high, jnp.max(near, axis=0, keepdims=True), jnp.max(low, axis=0, keepdims=True)


def reply_rows(value, slot):
    groups = value.shape[1] // 128
    rows = [value[:, g * 128 : (g + 1) * 128] for g in range(groups)]
    rest = jnp.concatenate(rows + [jnp.zeros((8 - groups, 128), F32)], axis=0)
    pieces = []
    for _ in range(3):
        pieces.append(rest.astype(BF))
        rest = rest - pieces[-1].astype(F32)
    pieces = jnp.concatenate(pieces, axis=0).astype(F32)
    return pieces, jnp.where((slot >> 7) == iota((8, SLOTS), 0), 1.0, 0.0)


def reply_to(value_all, value_high, slot):
    pieces_all, group = reply_rows(value_all, slot)
    pieces_high, _ = reply_rows(value_high, slot)
    pieces = jnp.concatenate([pieces_all, pieces_high], axis=0).astype(BF)
    pick = (iota((128, SLOTS), 0) == (slot & 127)).astype(BF)
    lines = dot(pieces, pick)
    row = iota((8, SLOTS), 0)
    out = []
    for which in range(2):
        line = lines[which * 24 : which * 24 + 8] + lines[which * 24 + 8 : which * 24 + 16] + lines[which * 24 + 16 : which * 24 + 24]
        found = jnp.sum(line * group, axis=0, keepdims=True)
        out.append(jnp.where(row == 4 * which, found, 0.0))
    return out + [jnp.zeros((8, SLOTS), F32)]


def far_kernel(key_ref, own_ref, other_ref, prev_ref, tail_ref, local_ref, out_ref, by_slot):
    key_cid, key_rank, key_slot = read_meta(key_ref, ROWS)
    cid_col, rank_col = columns(key_cid, key_rank)
    key_all = [jnp.full((HALF, 128), -1.0, F32)] * 2
    key_high = [jnp.full((HALF, 128), -1.0, F32)] * 2
    found = []
    cid, rank, slot = read_meta(tail_ref, HALF)
    work = [(tail_ref, HALF, 1, cid[:, HALF:], rank[:, HALF:], slot - HALF)]
    for ref in (prev_ref, own_ref, other_ref):
        cid, rank, slot = read_meta(ref, ROWS)
        work.append((ref, ROWS, 2, cid, rank, slot))
    for ref, count, halves, cid, rank, slot in work:
        best_all = best_high = None
        for half in range(halves):
            col = slice(half * HALF, (half + 1) * HALF)
            wide_all, wide_high, row_all, row_high = against(key_ref[col, :], cid_col[col], rank_col[col], ref, count, cid, rank)
            key_all[half] = jnp.maximum(key_all[half], wide_all)
            key_high[half] = jnp.maximum(key_high[half], wide_high)
            best_all = row_all if best_all is None else jnp.maximum(best_all, row_all)
            best_high = row_high if best_high is None else jnp.maximum(best_high, row_high)
        found.append((best_all, best_high, slot))
    key_all = jnp.max(jnp.transpose(jnp.concatenate(key_all, axis=0)), axis=0, keepdims=True)
    key_high = jnp.max(jnp.transpose(jnp.concatenate(key_high, axis=0)), axis=0, keepdims=True)
    tail, prev, own, other = found
    own = (jnp.maximum(own[0], local_ref[0:1, :]), jnp.maximum(own[1], local_ref[1:2, :]), own[2])
    rows = []
    for part in (own, other, (key_all, key_high, key_slot), prev, tail):
        rows += reply_to(*part)
    rows.append(jnp.zeros((8, SLOTS), F32))
    by_slot[...] = jnp.transpose(jnp.concatenate(rows, axis=0))
    reply = by_slot[pl.ds(0, DEVICES, stride=8), :]
    for order in range(1, 8):
        reply = reply + pltpu.roll(by_slot[pl.ds(order, DEVICES, stride=8), :], order, 1)
    out_ref[...] = reply + pltpu.roll(by_slot[MAIN:, :], 8, 1)


def answer_kernel(got_ref, route_ref, all_ref, high_ref):
    within = route_ref[5:6, :]
    replies = jnp.transpose(got_ref[...])
    row = iota((24, ROWS), 0)
    best = None
    for role in range(ROLES):
        rest = replies[role * 24 : role * 24 + 24]
        pieces = []
        for _ in range(3):
            pieces.append(rest.astype(BF).astype(F32))
            rest = rest - pieces[-1]
        sender = route_ref[role : role + 1, :]
        lines = dot(jnp.concatenate(pieces, axis=0).astype(BF), (iota((DEVICES, ROWS), 0) == sender).astype(BF))
        lines = jnp.where(sender >= 0, lines[0:24] + lines[24:48] + lines[48:72], -1.0)
        best = lines if best is None else jnp.maximum(best, lines)
    all_ref[...] = jnp.sum(jnp.where(row == within, best, 0.0), axis=0, keepdims=True).reshape(ROWS)
    high_ref[...] = jnp.sum(jnp.where(row == within + 12, best, 0.0), axis=0, keepdims=True).reshape(ROWS)


def call(kernel, out, args, scratch=(), flops=0, name=None, left=(), grant=48):
    moved = sum(a.size * a.dtype.itemsize for a in args)
    many = isinstance(out, list)
    shapes = [jax.ShapeDtypeStruct(*o) for o in (out if many else [out])]
    out_specs = [pl.BlockSpec(memory_space=pltpu.VMEM)] * len(shapes)
    return pl.pallas_call(
        kernel,
        out_shape=shapes if many else shapes[0],
        in_specs=[pl.BlockSpec(memory_space=pl.ANY if i in left else pltpu.VMEM) for i in range(len(args))],
        out_specs=out_specs if many else out_specs[0],
        scratch_shapes=list(scratch),
        compiler_params=pltpu.CompilerParams(vmem_limit_bytes=grant * 1024 * 1024),
        cost_estimate=pl.CostEstimate(flops=flops, bytes_accessed=moved, transcendentals=0),
        name=name,
    )(*args)


def body(embeddings, cluster_id, cluster_rank, dest_slot):
    send, route = call(
        pack_kernel,
        [((MAIN, ROWS + 128), BF), ((8, ROWS), jnp.int32)],
        (embeddings, cluster_id, cluster_rank, dest_slot),
        (
            pltpu.VMEM((ROWS, ROWS), BF),
            pltpu.VMEM((ROWS,), jnp.int32),
            pltpu.VMEM((ROWS,), jnp.int32),
            pltpu.VMEM((ROWS,), jnp.int32),
            pltpu.VMEM((ROWS, ROWS), BF),
            pltpu.VMEM((MAIN, 128), F32),
            pltpu.SemaphoreType.DMA((6,)),
        ),
        name="pack",
        left=(0, 1, 2, 3),
        grant=60,
    )
    got = lax.all_to_all(send, AXES, split_axis=0, concat_axis=0, tiled=True)
    own = call(
        unpack_kernel,
        ((ROWS + META, ROWS), BF),
        (got,),
        (pltpu.VMEM((MAIN, 128), F32), pltpu.VMEM((MAIN, 128), F32)),
        name="unpack",
    )
    everyone = range(DEVICES)
    other = lax.ppermute(own, AXES, routes(lambda t: t ^ 1, everyone))
    key = lax.ppermute(own, AXES, routes(lambda t: t + 2, everyone))
    prev = lax.ppermute(own, AXES, routes(lambda t: t - 1, range(0, DEVICES, 2)))
    tail = lax.ppermute(own[HALF:], AXES, routes(lambda t: t - 2, everyone))
    tile = 2 * ROWS**3
    local = call(local_kernel, ((8, ROWS), F32), (own, other), flops=2 * tile, name="local")
    reply = call(
        far_kernel,
        ((DEVICES, 128), F32),
        (key, own, other, prev, tail, local),
        (pltpu.VMEM((SLOTS, 128), F32),),
        flops=4 * tile,
        name="far",
    )
    answer = lax.all_to_all(reply.reshape(DEVICES, 1, 128), AXES, split_axis=0, concat_axis=0, tiled=True)
    return call(answer_kernel, [((ROWS,), F32)] * 2, (answer.reshape(DEVICES, 128), route), name="answer")


def solution(mesh):
    rows = P(AXES)
    return jax.shard_map(
        body,
        mesh=mesh,
        in_specs=(P(AXES, None), rows, rows, rows),
        out_specs=(rows, rows),
        check_vma=False,
    )
```

```python
import jax
import jax.numpy as jnp
from jax import lax
from jax.experimental import pallas as pl
from jax.experimental.pallas import tpu as pltpu
from jax.sharding import PartitionSpec as P

AXES = ("seg", "pair")
DEVICES = 128
PLACES = [
    (3, 3, 3, 0), (2, 3, 3, 0), (3, 3, 0, 0), (2, 3, 0, 0), (3, 0, 0, 0), (2, 0, 0, 0), (3, 0, 1, 0), (2, 0, 1, 0),
    (3, 0, 2, 0), (2, 0, 2, 0), (3, 0, 3, 0), (2, 0, 3, 0), (3, 1, 3, 0), (2, 1, 3, 0), (3, 1, 0, 0), (2, 1, 0, 0),
    (3, 1, 1, 0), (2, 1, 1, 0), (3, 1, 2, 0), (2, 1, 2, 0), (3, 2, 2, 0), (2, 2, 2, 0), (3, 2, 3, 0), (2, 2, 3, 0),
    (3, 2, 0, 0), (2, 2, 0, 0), (3, 2, 1, 0), (2, 2, 1, 0), (3, 3, 1, 0), (2, 3, 1, 0), (3, 3, 2, 0), (2, 3, 2, 0),
    (2, 3, 2, 1), (1, 3, 2, 1), (2, 2, 2, 1), (1, 2, 2, 1), (2, 2, 1, 1), (1, 2, 1, 1), (2, 1, 1, 1), (1, 1, 1, 1),
    (2, 0, 1, 1), (1, 0, 1, 1), (2, 3, 1, 1), (1, 3, 1, 1), (2, 3, 0, 1), (1, 3, 0, 1), (2, 2, 0, 1), (1, 2, 0, 1),
    (2, 1, 0, 1), (1, 1, 0, 1), (2, 0, 0, 1), (1, 0, 0, 1), (2, 0, 3, 1), (1, 0, 3, 1), (2, 3, 3, 1), (1, 3, 3, 1),
    (2, 2, 3, 1), (1, 2, 3, 1), (2, 1, 3, 1), (1, 1, 3, 1), (2, 1, 2, 1), (1, 1, 2, 1), (2, 0, 2, 1), (1, 0, 2, 1),
    (1, 0, 2, 0), (0, 0, 2, 0), (1, 0, 1, 0), (0, 0, 1, 0), (1, 0, 0, 0), (0, 0, 0, 0), (1, 3, 0, 0), (0, 3, 0, 0),
    (1, 3, 3, 0), (0, 3, 3, 0), (1, 3, 2, 0), (0, 3, 2, 0), (1, 3, 1, 0), (0, 3, 1, 0), (1, 2, 1, 0), (0, 2, 1, 0),
    (1, 2, 0, 0), (0, 2, 0, 0), (1, 2, 3, 0), (0, 2, 3, 0), (1, 2, 2, 0), (0, 2, 2, 0), (1, 1, 2, 0), (0, 1, 2, 0),
    (1, 1, 1, 0), (0, 1, 1, 0), (1, 1, 0, 0), (0, 1, 0, 0), (1, 1, 3, 0), (0, 1, 3, 0), (1, 0, 3, 0), (0, 0, 3, 0),
    (0, 0, 3, 1), (3, 0, 3, 1), (0, 0, 0, 1), (3, 0, 0, 1), (0, 1, 0, 1), (3, 1, 0, 1), (0, 2, 0, 1), (3, 2, 0, 1),
    (0, 3, 0, 1), (3, 3, 0, 1), (0, 3, 1, 1), (3, 3, 1, 1), (0, 0, 1, 1), (3, 0, 1, 1), (0, 1, 1, 1), (3, 1, 1, 1),
    (0, 2, 1, 1), (3, 2, 1, 1), (0, 2, 2, 1), (3, 2, 2, 1), (0, 3, 2, 1), (3, 3, 2, 1), (0, 0, 2, 1), (3, 0, 2, 1),
    (0, 1, 2, 1), (3, 1, 2, 1), (0, 1, 3, 1), (3, 1, 3, 1), (0, 2, 3, 1), (3, 2, 3, 1), (0, 3, 3, 1), (3, 3, 3, 1),
]
ROWS = 768
HALF = 384
CAP = 9
SLOTS = DEVICES * CAP
MAIN = DEVICES * 8
META = 16
ROLES = 4
BF = jnp.bfloat16
F32 = jnp.float32
NT = (((1,), (1,)), ((), ()))


HOLDERS = [((((x & 1) * 4 + z) * 4 + y) << 2) + ((x >> 1) << 1) + core for x, y, z, core in PLACES]


def device_of(block):
    return HOLDERS[block % DEVICES]


def shift(step):
    return [(device_of(block + step), device_of(block)) for block in range(DEVICES)]


def iota(shape, dim):
    return lax.broadcasted_iota(jnp.int32, shape, dim)


def dot(a, b):
    return jnp.dot(a, b, preferred_element_type=F32)


def dot_nt(a, b):
    return lax.dot_general(a, b, NT, preferred_element_type=F32)


def split_slot(slot):
    block = ((slot >> 8) * 171) >> 9
    return block, slot - block * ROWS


def device_table():
    row, lane = iota((8, DEVICES), 0), iota((8, DEVICES), 1)
    step = jnp.where(row == 1, 1, jnp.where(row == 2, -2, jnp.where(row == 3, 2, 0)))
    block = (lane + step) & (DEVICES - 1)
    found = jnp.zeros_like(block)
    for index, device in enumerate(HOLDERS):
        found = jnp.where(block == index, device, found)
    return found.astype(F32).astype(BF)


def pack_kernel(emb_ref, cid_ref, rank_ref, slot_ref, out_ref, route_ref, raw, slots, cids, ranks, unit, extra, sems):
    ids = ((slot_ref, slots), (cid_ref, cids), (rank_ref, ranks))
    small = [pltpu.make_async_copy(*pair, sems.at[3 + i]) for i, pair in enumerate(ids)]
    copies = [
        pltpu.make_async_copy(emb_ref.at[pl.ds(part * 256, 256)], raw.at[pl.ds(part * 256, 256)], sems.at[part])
        for part in range(3)
    ]
    for copy in small + copies:
        copy.start()
    table = device_table()
    earlier = (iota((ROWS, ROWS), 0) < iota((ROWS, ROWS), 1)).astype(BF)
    for copy in small:
        copy.wait()
    slot, cid, rank = (ref[...].reshape(1, ROWS) for _, ref in ids)
    block, local = split_slot(slot)
    to_block = (iota((DEVICES, ROWS), 0) == block).astype(BF)
    within = jnp.sum(to_block.astype(F32) * dot(to_block, earlier), axis=0, keepdims=True).astype(jnp.int32)
    senders = dot(table, to_block).astype(jnp.int32)
    row = iota((8, ROWS), 0)
    dropped = (row == 3) & (local < HALF)
    route_ref[...] = jnp.where(row == 4, within, jnp.where(dropped, -1, senders))
    device = senders[0:1]
    to_device = (iota((DEVICES, ROWS), 0) == device).astype(BF)
    flat = jnp.where(within < 8, device * 8 + within, -1)
    for part, copy in enumerate(copies):
        copy.wait()
        values = raw[part * 256 : (part + 1) * 256, :].astype(F32)
        scaling = lax.rsqrt(jnp.sum(values * values, axis=1, keepdims=True) + 1e-06)
        unit[part * 256 : (part + 1) * 256, :] = (values * scaling).astype(BF)
    for start in range(0, MAIN, 256):
        pick = (iota((256, ROWS), 0) + start == flat).astype(BF)
        out_ref[start : start + 256, :ROWS] = dot(pick, unit[...]).astype(BF)
    ninth = jnp.where(within == 8, to_device, jnp.zeros_like(to_device))
    ninth_rows = dot(ninth, unit[...])
    field = iota((DEVICES, ROWS), 0) >> 4
    meta = jnp.where(field == 0, (local >> 8) + 1, jnp.where(field == 1, local & 255, jnp.where(field == 2, cid + 1, 0)))
    meta = jnp.where(field == 3, rank >> 8, jnp.where(field == 4, rank & 255, meta))
    meta = jnp.where((iota((DEVICES, ROWS), 0) & 15) == within, meta, 0).astype(F32).astype(BF)
    extra[...] = jnp.zeros_like(extra)
    for part in range(6):
        extra[pl.ds(part, DEVICES, stride=8), :] = ninth_rows[:, part * 128 : (part + 1) * 128]
    extra[pl.ds(6, DEVICES, stride=8), :] = dot_nt(to_device, meta)
    out_ref[:, ROWS:] = extra[...].astype(BF)


def unpack_kernel(got_ref, out_ref, extra, spread):
    extra[...] = got_ref[:, ROWS:].astype(F32)
    ninth_rows = jnp.concatenate([extra[pl.ds(part, DEVICES, stride=8), :] for part in range(6)], axis=1).astype(BF)
    meta = extra[pl.ds(6, DEVICES, stride=8), :]
    for order in range(8):
        spread[pl.ds(order, DEVICES, stride=8), :] = meta
    lane, row = iota((MAIN, 128), 1), iota((MAIN, 128), 0)
    main = jnp.where((lane & 15) == (row & 7), spread[...], 0.0).astype(BF)
    last = jnp.where((iota((DEVICES, 128), 1) & 15) == 8, meta, 0.0).astype(BF)
    fields = ((iota((META, 128), 1) >> 4) == iota((META, 128), 0)).astype(BF)
    by_slot = jnp.concatenate([dot_nt(fields, main), dot_nt(fields, last)], axis=1)
    slot = ((by_slot[0:1] - 1.0) * 256.0 + by_slot[1:2]).astype(jnp.int32)
    cols = by_slot.astype(BF)
    for start in range(0, ROWS, 256):
        pick = (iota((256, SLOTS), 0) + start == slot).astype(BF)
        rows = dot(pick[:, :MAIN], got_ref[:, :ROWS]) + dot(pick[:, MAIN:], ninth_rows)
        out_ref[start : start + 256, :] = rows.astype(BF)
        placed = dot_nt(cols, pick)
        kept = jnp.concatenate([placed[2:5], jnp.zeros((13, 256), F32)], axis=0)
        out_ref[ROWS:, start : start + 256] = kept.astype(BF)
    out_ref[ROWS + 8 : ROWS + 9, :] = cols[0:1, :ROWS]
    out_ref[ROWS + 9 : ROWS + 10, :] = cols[1:2, :ROWS]
    out_ref[ROWS + 10 : ROWS + 11, :HALF] = cols[0:1, ROWS:]
    out_ref[ROWS + 11 : ROWS + 12, :HALF] = cols[1:2, ROWS:]


def read_meta(block_ref, rows):
    meta = block_ref[rows:, :].astype(F32)
    cid, rank = meta[0:1], meta[1:2] * 256.0 + meta[2:3]
    high = jnp.concatenate([meta[8:9], meta[10:11, :HALF]], axis=1)
    low = jnp.concatenate([meta[9:10], meta[11:12, :HALF]], axis=1)
    slot = ((high - 1.0) * 256.0 + low).astype(jnp.int32)
    return cid, rank, slot


def columns(cid, rank):
    both = jnp.concatenate([cid, rank, jnp.zeros((6, ROWS), F32)], axis=0)
    turned = jnp.transpose(both)
    return turned[:, 0:1], turned[:, 1:2]


def local_kernel(own_ref, out_ref):
    own_cid, own_rank, _ = read_meta(own_ref, ROWS)
    cid, rank = columns(own_cid, own_rank)
    best_all = jnp.full((8, ROWS), -1.0, F32)
    best_high = jnp.full((8, ROWS), -1.0, F32)
    for start in range(0, ROWS, HALF):
        cosine = dot_nt(own_ref[start : start + HALF, :], own_ref[:ROWS, :])
        c, r = cid[start : start + HALF], rank[start : start + HALF]
        near = jnp.where((c == own_cid) & (r != own_rank), cosine, -1.0)
        high = jnp.where(r < own_rank, near, -1.0)
        best_all = jnp.maximum(best_all, jnp.max(near.reshape(HALF // 8, 8, ROWS), axis=0))
        best_high = jnp.maximum(best_high, jnp.max(high.reshape(HALF // 8, 8, ROWS), axis=0))
    out_ref[0:1, :] = jnp.max(best_all, axis=0, keepdims=True)
    out_ref[1:2, :] = jnp.max(best_high, axis=0, keepdims=True)
    out_ref[2:, :] = jnp.full((6, ROWS), -1.0, F32)


def meet(key_ref, key, others):
    cid, rank = columns(*key)
    key_all = [jnp.full((HALF, 128), -1.0, F32)] * 2
    key_high = [jnp.full((HALF, 128), -1.0, F32)] * 2
    found = []
    for ref, count, other_cid, other_rank in others:
        best = None
        for half in range(count // HALF):
            part = slice(half * HALF, (half + 1) * HALF)
            wide_all, wide_high, row_all, row_high = against(
                key_ref[part, :], cid[part], rank[part], ref, count, other_cid, other_rank
            )
            key_all[half] = jnp.maximum(key_all[half], wide_all)
            key_high[half] = jnp.maximum(key_high[half], wide_high)
            best = (row_all, row_high) if best is None else (jnp.maximum(best[0], row_all), jnp.maximum(best[1], row_high))
        found.append(best)
    key = tuple(
        jnp.max(jnp.transpose(jnp.concatenate(wide, axis=0)), axis=0, keepdims=True) for wide in (key_all, key_high)
    )
    return key, found


def both(left, right):
    return tuple(jnp.maximum(a, b) for a, b in zip(left, right))


def against(key, key_cid, key_rank, other_ref, count, other_cid, other_rank):
    cosine = dot_nt(key, other_ref[:count, :])
    near = jnp.where(key_cid == other_cid, cosine, -1.0)
    before = other_rank < key_rank
    high = jnp.where(before, near, -1.0)
    low = jnp.where(before, -1.0, near)
    wide_all, wide_high = near[:, :128], high[:, :128]
    for lane in range(128, count, 128):
        wide_all = jnp.maximum(wide_all, near[:, lane : lane + 128])
        wide_high = jnp.maximum(wide_high, high[:, lane : lane + 128])
    return wide_all, wide_high, jnp.max(near, axis=0, keepdims=True), jnp.max(low, axis=0, keepdims=True)


def reply_rows(value, slot):
    groups = value.shape[1] // 128
    rows = [value[:, g * 128 : (g + 1) * 128] for g in range(groups)]
    rest = jnp.concatenate(rows + [jnp.zeros((8 - groups, 128), F32)], axis=0)
    pieces = []
    for _ in range(3):
        pieces.append(rest.astype(BF))
        rest = rest - pieces[-1].astype(F32)
    pieces = jnp.concatenate(pieces, axis=0).astype(F32)
    return pieces, jnp.where((slot >> 7) == iota((8, SLOTS), 0), 1.0, 0.0)


def reply_to(value_all, value_high, slot):
    pieces_all, group = reply_rows(value_all, slot)
    pieces_high, _ = reply_rows(value_high, slot)
    pieces = jnp.concatenate([pieces_all, pieces_high], axis=0).astype(BF)
    pick = (iota((128, SLOTS), 0) == (slot & 127)).astype(BF)
    lines = dot(pieces, pick)
    row = iota((8, SLOTS), 0)
    out = []
    for which in range(2):
        line = lines[which * 24 : which * 24 + 8] + lines[which * 24 + 8 : which * 24 + 16] + lines[which * 24 + 16 : which * 24 + 24]
        found = jnp.sum(line * group, axis=0, keepdims=True)
        out.append(jnp.where(row == 4 * which, found, 0.0))
    return out + [jnp.zeros((8, SLOTS), F32)]


def mate_kernel(own_ref, mate_ref, local_ref, out_ref):
    own, mate = read_meta(own_ref, ROWS), read_meta(mate_ref, ROWS)
    mine, (theirs,) = meet(own_ref, own[:2], [(mate_ref, ROWS, *mate[:2])])
    mine = both(mine, (local_ref[0:1, :], local_ref[1:2, :]))
    out_ref[...] = jnp.concatenate([*mine, *theirs, jnp.full((4, ROWS), -1.0, F32)], axis=0)


def far_kernel(key_ref, own_ref, mate_ref, tail_ref, near_ref, out_ref, by_slot):
    own, mate, key = (read_meta(ref, ROWS) for ref in (own_ref, mate_ref, key_ref))
    cid, rank, tail_slot = read_meta(tail_ref, HALF)
    keys, (tails, mates, owns) = meet(
        key_ref,
        key[:2],
        [(tail_ref, HALF, cid[:, HALF:], rank[:, HALF:]), (mate_ref, ROWS, *mate[:2]), (own_ref, ROWS, *own[:2])],
    )
    owns = both(owns, (near_ref[0:1, :], near_ref[1:2, :]))
    mates = both(mates, (near_ref[2:3, :], near_ref[3:4, :]))
    rows = []
    for part, slot in ((owns, own[2]), (mates, mate[2]), (keys, key[2]), (tails, tail_slot - HALF)):
        rows += reply_to(*part, slot)
    rows.append(jnp.zeros((32, SLOTS), F32))
    by_slot[...] = jnp.transpose(jnp.concatenate(rows, axis=0))
    reply = by_slot[pl.ds(0, DEVICES, stride=8), :]
    for order in range(1, 8):
        reply = reply + pltpu.roll(by_slot[pl.ds(order, DEVICES, stride=8), :], order, 1)
    out_ref[...] = reply + pltpu.roll(by_slot[MAIN:, :], 8, 1)


def answer_kernel(got_ref, route_ref, all_ref, high_ref):
    within = route_ref[4:5, :]
    replies = jnp.transpose(got_ref[...])
    row = iota((24, ROWS), 0)
    best = None
    for role in range(ROLES):
        rest = replies[role * 24 : role * 24 + 24]
        pieces = []
        for _ in range(3):
            pieces.append(rest.astype(BF).astype(F32))
            rest = rest - pieces[-1]
        sender = route_ref[role : role + 1, :]
        lines = dot(jnp.concatenate(pieces, axis=0).astype(BF), (iota((DEVICES, ROWS), 0) == sender).astype(BF))
        lines = jnp.where(sender >= 0, lines[0:24] + lines[24:48] + lines[48:72], -1.0)
        best = lines if best is None else jnp.maximum(best, lines)
    all_ref[...] = jnp.sum(jnp.where(row == within, best, 0.0), axis=0, keepdims=True).reshape(ROWS)
    high_ref[...] = jnp.sum(jnp.where(row == within + 12, best, 0.0), axis=0, keepdims=True).reshape(ROWS)


def call(kernel, out, args, scratch=(), flops=0, name=None, left=(), grant=48):
    moved = sum(a.size * a.dtype.itemsize for a in args)
    many = isinstance(out, list)
    shapes = [jax.ShapeDtypeStruct(*o) for o in (out if many else [out])]
    out_specs = [pl.BlockSpec(memory_space=pltpu.VMEM)] * len(shapes)
    return pl.pallas_call(
        kernel,
        out_shape=shapes if many else shapes[0],
        in_specs=[pl.BlockSpec(memory_space=pl.ANY if i in left else pltpu.VMEM) for i in range(len(args))],
        out_specs=out_specs if many else out_specs[0],
        scratch_shapes=list(scratch),
        compiler_params=pltpu.CompilerParams(vmem_limit_bytes=grant * 1024 * 1024),
        cost_estimate=pl.CostEstimate(flops=flops, bytes_accessed=moved, transcendentals=0),
        name=name,
    )(*args)


def body(embeddings, cluster_id, cluster_rank, dest_slot):
    send, route = call(
        pack_kernel,
        [((MAIN, ROWS + 128), BF), ((8, ROWS), jnp.int32)],
        (embeddings, cluster_id, cluster_rank, dest_slot),
        (
            pltpu.VMEM((ROWS, ROWS), BF),
            pltpu.VMEM((ROWS,), jnp.int32),
            pltpu.VMEM((ROWS,), jnp.int32),
            pltpu.VMEM((ROWS,), jnp.int32),
            pltpu.VMEM((ROWS, ROWS), BF),
            pltpu.VMEM((MAIN, 128), F32),
            pltpu.SemaphoreType.DMA((6,)),
        ),
        name="pack",
        left=(0, 1, 2, 3),
        grant=60,
    )
    got = lax.all_to_all(send, AXES, split_axis=0, concat_axis=0, tiled=True)
    own = call(
        unpack_kernel,
        ((ROWS + META, ROWS), BF),
        (got,),
        (pltpu.VMEM((MAIN, 128), F32), pltpu.VMEM((MAIN, 128), F32)),
        name="unpack",
    )
    mate = lax.ppermute(own, AXES, shift(-1))
    key = lax.ppermute(own, AXES, shift(2))
    tail = lax.ppermute(own[HALF:], AXES, shift(-2))
    tile = 2 * ROWS**3
    local = call(local_kernel, ((8, ROWS), F32), (own,), flops=tile, name="local")
    near = call(mate_kernel, ((8, ROWS), F32), (own, mate, local), flops=tile, name="mate")
    reply = call(
        far_kernel,
        ((DEVICES, 128), F32),
        (key, own, mate, tail, near),
        (pltpu.VMEM((SLOTS, 128), F32),),
        flops=3 * tile,
        name="far",
    )
    answer = lax.all_to_all(reply.reshape(DEVICES, 1, 128), AXES, split_axis=0, concat_axis=0, tiled=True)
    return call(answer_kernel, [((ROWS,), F32)] * 2, (answer.reshape(DEVICES, 128), route), name="answer")


def solution(mesh):
    rows = P(AXES)
    return jax.shard_map(
        body,
        mesh=mesh,
        in_specs=(P(AXES, None), rows, rows, rows),
        out_specs=(rows, rows),
        check_vma=False,
    )
```

```python
import jax
import jax.numpy as jnp
from jax import lax
from jax.experimental import pallas as pl
from jax.experimental.pallas import tpu as pltpu
from jax.sharding import PartitionSpec as P

AXES = ("seg", "pair")
DEVICES = 128
PLACES = [
    (3, 0, 1, 1), (0, 0, 1, 1), (3, 1, 1, 1), (0, 1, 1, 1), (3, 2, 1, 1), (0, 2, 1, 1), (3, 2, 2, 1), (0, 2, 2, 1),
    (3, 3, 2, 1), (0, 3, 2, 1), (3, 0, 2, 1), (0, 0, 2, 1), (3, 1, 2, 1), (0, 1, 2, 1), (3, 1, 3, 1), (0, 1, 3, 1),
    (3, 2, 3, 1), (0, 2, 3, 1), (3, 3, 3, 1), (0, 3, 3, 1), (3, 0, 3, 1), (0, 0, 3, 1), (3, 0, 0, 1), (0, 0, 0, 1),
    (3, 1, 0, 1), (0, 1, 0, 1), (3, 2, 0, 1), (0, 2, 0, 1), (3, 3, 0, 1), (0, 3, 0, 1), (3, 3, 1, 1), (0, 3, 1, 1),
    (0, 3, 1, 0), (1, 3, 1, 0), (0, 2, 1, 0), (1, 2, 1, 0), (0, 2, 0, 0), (1, 2, 0, 0), (0, 2, 3, 0), (1, 2, 3, 0),
    (0, 2, 2, 0), (1, 2, 2, 0), (0, 1, 2, 0), (1, 1, 2, 0), (0, 1, 1, 0), (1, 1, 1, 0), (0, 1, 0, 0), (1, 1, 0, 0),
    (0, 1, 3, 0), (1, 1, 3, 0), (0, 0, 3, 0), (1, 0, 3, 0), (0, 0, 2, 0), (1, 0, 2, 0), (0, 0, 1, 0), (1, 0, 1, 0),
    (0, 0, 0, 0), (1, 0, 0, 0), (0, 3, 0, 0), (1, 3, 0, 0), (0, 3, 3, 0), (1, 3, 3, 0), (0, 3, 2, 0), (1, 3, 2, 0),
    (1, 3, 2, 1), (2, 3, 2, 1), (1, 2, 2, 1), (2, 2, 2, 1), (1, 2, 1, 1), (2, 2, 1, 1), (1, 1, 1, 1), (2, 1, 1, 1),
    (1, 0, 1, 1), (2, 0, 1, 1), (1, 3, 1, 1), (2, 3, 1, 1), (1, 3, 0, 1), (2, 3, 0, 1), (1, 2, 0, 1), (2, 2, 0, 1),
    (1, 1, 0, 1), (2, 1, 0, 1), (1, 0, 0, 1), (2, 0, 0, 1), (1, 0, 3, 1), (2, 0, 3, 1), (1, 3, 3, 1), (2, 3, 3, 1),
    (1, 2, 3, 1), (2, 2, 3, 1), (1, 1, 3, 1), (2, 1, 3, 1), (1, 1, 2, 1), (2, 1, 2, 1), (1, 0, 2, 1), (2, 0, 2, 1),
    (2, 0, 2, 0), (3, 0, 2, 0), (2, 0, 3, 0), (3, 0, 3, 0), (2, 1, 3, 0), (3, 1, 3, 0), (2, 1, 0, 0), (3, 1, 0, 0),
    (2, 1, 1, 0), (3, 1, 1, 0), (2, 1, 2, 0), (3, 1, 2, 0), (2, 2, 2, 0), (3, 2, 2, 0), (2, 2, 3, 0), (3, 2, 3, 0),
    (2, 2, 0, 0), (3, 2, 0, 0), (2, 2, 1, 0), (3, 2, 1, 0), (2, 3, 1, 0), (3, 3, 1, 0), (2, 3, 2, 0), (3, 3, 2, 0),
    (2, 3, 3, 0), (3, 3, 3, 0), (2, 3, 0, 0), (3, 3, 0, 0), (2, 0, 0, 0), (3, 0, 0, 0), (2, 0, 1, 0), (3, 0, 1, 0),
]
ROWS = 768
HALF = 384
CAP = 9
SLOTS = DEVICES * CAP
MAIN = DEVICES * 8
META = 16
ROLES = 4
BF = jnp.bfloat16
F32 = jnp.float32
NT = (((1,), (1,)), ((), ()))


HOLDERS = [((((x & 1) * 4 + z) * 4 + y) << 2) + ((x >> 1) << 1) + core for x, y, z, core in PLACES]


def device_of(block):
    return HOLDERS[block % DEVICES]


def shift(step):
    return [(device_of(block + step), device_of(block)) for block in range(DEVICES)]


def iota(shape, dim):
    return lax.broadcasted_iota(jnp.int32, shape, dim)


def dot(a, b):
    return jnp.dot(a, b, preferred_element_type=F32)


def dot_nt(a, b):
    return lax.dot_general(a, b, NT, preferred_element_type=F32)


def split_slot(slot):
    block = ((slot >> 8) * 171) >> 9
    return block, slot - block * ROWS


def device_table():
    row, lane = iota((8, DEVICES), 0), iota((8, DEVICES), 1)
    step = jnp.where(row == 1, 1, jnp.where(row == 2, -2, jnp.where(row == 3, 2, 0)))
    block = (lane + step) & (DEVICES - 1)
    found = jnp.zeros_like(block)
    for index, device in enumerate(HOLDERS):
        found = jnp.where(block == index, device, found)
    return found.astype(F32).astype(BF)


def pack_kernel(emb_ref, cid_ref, rank_ref, slot_ref, out_ref, route_ref, raw, slots, cids, ranks, unit, extra, sems):
    ids = ((slot_ref, slots), (cid_ref, cids), (rank_ref, ranks))
    small = [pltpu.make_async_copy(*pair, sems.at[3 + i]) for i, pair in enumerate(ids)]
    copies = [
        pltpu.make_async_copy(emb_ref.at[pl.ds(part * 256, 256)], raw.at[pl.ds(part * 256, 256)], sems.at[part])
        for part in range(3)
    ]
    for copy in small + copies:
        copy.start()
    table = device_table()
    earlier = (iota((ROWS, ROWS), 0) < iota((ROWS, ROWS), 1)).astype(BF)
    for copy in small:
        copy.wait()
    slot, cid, rank = (ref[...].reshape(1, ROWS) for _, ref in ids)
    block, local = split_slot(slot)
    to_block = (iota((DEVICES, ROWS), 0) == block).astype(BF)
    within = jnp.sum(to_block.astype(F32) * dot(to_block, earlier), axis=0, keepdims=True).astype(jnp.int32)
    senders = dot(table, to_block).astype(jnp.int32)
    row = iota((8, ROWS), 0)
    dropped = (row == 3) & (local < HALF)
    route_ref[...] = jnp.where(row == 4, within, jnp.where(dropped, -1, senders))
    device = senders[0:1]
    to_device = (iota((DEVICES, ROWS), 0) == device).astype(BF)
    flat = jnp.where(within < 8, device * 8 + within, -1)
    for part, copy in enumerate(copies):
        copy.wait()
        values = raw[part * 256 : (part + 1) * 256, :].astype(F32)
        scaling = lax.rsqrt(jnp.sum(values * values, axis=1, keepdims=True) + 1e-06)
        unit[part * 256 : (part + 1) * 256, :] = (values * scaling).astype(BF)
    for start in range(0, MAIN, 256):
        pick = (iota((256, ROWS), 0) + start == flat).astype(BF)
        out_ref[start : start + 256, :ROWS] = dot(pick, unit[...]).astype(BF)
    ninth = jnp.where(within == 8, to_device, jnp.zeros_like(to_device))
    ninth_rows = dot(ninth, unit[...])
    field = iota((DEVICES, ROWS), 0) >> 4
    meta = jnp.where(field == 0, (local >> 8) + 1, jnp.where(field == 1, local & 255, jnp.where(field == 2, cid + 1, 0)))
    meta = jnp.where(field == 3, rank >> 8, jnp.where(field == 4, rank & 255, meta))
    meta = jnp.where((iota((DEVICES, ROWS), 0) & 15) == within, meta, 0).astype(F32).astype(BF)
    extra[...] = jnp.zeros_like(extra)
    for part in range(6):
        extra[pl.ds(part, DEVICES, stride=8), :] = ninth_rows[:, part * 128 : (part + 1) * 128]
    extra[pl.ds(6, DEVICES, stride=8), :] = dot_nt(to_device, meta)
    out_ref[:, ROWS:] = extra[...].astype(BF)


def unpack_kernel(got_ref, out_ref, first_ref, extra, spread):
    extra[...] = got_ref[:, ROWS:].astype(F32)
    ninth_rows = jnp.concatenate([extra[pl.ds(part, DEVICES, stride=8), :] for part in range(6)], axis=1).astype(BF)
    meta = extra[pl.ds(6, DEVICES, stride=8), :]
    for order in range(8):
        spread[pl.ds(order, DEVICES, stride=8), :] = meta
    lane, row = iota((MAIN, 128), 1), iota((MAIN, 128), 0)
    main = jnp.where((lane & 15) == (row & 7), spread[...], 0.0).astype(BF)
    last = jnp.where((iota((DEVICES, 128), 1) & 15) == 8, meta, 0.0).astype(BF)
    fields = ((iota((META, 128), 1) >> 4) == iota((META, 128), 0)).astype(BF)
    by_slot = jnp.concatenate([dot_nt(fields, main), dot_nt(fields, last)], axis=1)
    slot = ((by_slot[0:1] - 1.0) * 256.0 + by_slot[1:2]).astype(jnp.int32)
    cols = by_slot.astype(BF)
    for start in range(0, ROWS, 256):
        pick = (iota((256, SLOTS), 0) + start == slot).astype(BF)
        rows = dot(pick[:, :MAIN], got_ref[:, :ROWS]) + dot(pick[:, MAIN:], ninth_rows)
        out_ref[start : start + 256, :] = rows.astype(BF)
        placed = dot_nt(cols, pick)
        kept = jnp.concatenate([placed[2:5], jnp.zeros((13, 256), F32)], axis=0)
        out_ref[ROWS:, start : start + 256] = kept.astype(BF)
    out_ref[ROWS + 8 : ROWS + 9, :] = cols[0:1, :ROWS]
    out_ref[ROWS + 9 : ROWS + 10, :] = cols[1:2, :ROWS]
    out_ref[ROWS + 10 : ROWS + 11, :HALF] = cols[0:1, ROWS:]
    out_ref[ROWS + 11 : ROWS + 12, :HALF] = cols[1:2, ROWS:]
    first_ref[:HALF, :] = out_ref[:HALF, :]
    first_ref[HALF:, :] = out_ref[ROWS:, :]


def read_meta(block_ref, rows):
    meta = block_ref[rows:, :].astype(F32)
    cid, rank = meta[0:1], meta[1:2] * 256.0 + meta[2:3]
    high = jnp.concatenate([meta[8:9], meta[10:11, :HALF]], axis=1)
    low = jnp.concatenate([meta[9:10], meta[11:12, :HALF]], axis=1)
    slot = ((high - 1.0) * 256.0 + low).astype(jnp.int32)
    return cid, rank, slot


def columns(cid, rank):
    both = jnp.concatenate([cid, rank, jnp.zeros((6, cid.shape[1]), F32)], axis=0)
    turned = jnp.transpose(both)
    return turned[:, 0:1], turned[:, 1:2]


def local_kernel(own_ref, out_ref):
    own_cid, own_rank, _ = read_meta(own_ref, ROWS)
    cid, rank = columns(own_cid, own_rank)
    best_all = jnp.full((8, ROWS), -1.0, F32)
    best_high = jnp.full((8, ROWS), -1.0, F32)
    for start in range(0, ROWS, HALF):
        cosine = dot_nt(own_ref[start : start + HALF, :], own_ref[:ROWS, :])
        c, r = cid[start : start + HALF], rank[start : start + HALF]
        near = jnp.where((c == own_cid) & (r != own_rank), cosine, -1.0)
        high = jnp.where(r < own_rank, near, -1.0)
        best_all = jnp.maximum(best_all, jnp.max(near.reshape(HALF // 8, 8, ROWS), axis=0))
        best_high = jnp.maximum(best_high, jnp.max(high.reshape(HALF // 8, 8, ROWS), axis=0))
    out_ref[0:1, :] = jnp.max(best_all, axis=0, keepdims=True)
    out_ref[1:2, :] = jnp.max(best_high, axis=0, keepdims=True)
    out_ref[2:, :] = jnp.full((6, ROWS), -1.0, F32)


def meet(key, ids, others):
    cid, rank = columns(*ids)
    key_all = jnp.full((HALF, 128), -1.0, F32)
    key_high, found = key_all, []
    for ref, count, other_cid, other_rank in others:
        wide_all, wide_high, row_all, row_high = against(key, cid, rank, ref, count, other_cid, other_rank)
        key_all, key_high = jnp.maximum(key_all, wide_all), jnp.maximum(key_high, wide_high)
        found.append((row_all, row_high))
    return tuple(jnp.max(jnp.transpose(wide), axis=0, keepdims=True) for wide in (key_all, key_high)), found


def half_ids(ids, half):
    part = slice(half * HALF, (half + 1) * HALF)
    return ids[0][:, part], ids[1][:, part]


def both(left, right):
    return tuple(jnp.maximum(a, b) for a, b in zip(left, right))


def against(key, key_cid, key_rank, other_ref, count, other_cid, other_rank):
    cosine = dot_nt(key, other_ref[:count, :])
    near = jnp.where(key_cid == other_cid, cosine, -1.0)
    before = other_rank < key_rank
    high = jnp.where(before, near, -1.0)
    low = jnp.where(before, -1.0, near)
    wide_all, wide_high = near[:, :128], high[:, :128]
    for lane in range(128, count, 128):
        wide_all = jnp.maximum(wide_all, near[:, lane : lane + 128])
        wide_high = jnp.maximum(wide_high, high[:, lane : lane + 128])
    return wide_all, wide_high, jnp.max(near, axis=0, keepdims=True), jnp.max(low, axis=0, keepdims=True)


def reply_rows(value, slot):
    groups = value.shape[1] // 128
    rows = [value[:, g * 128 : (g + 1) * 128] for g in range(groups)]
    rest = jnp.concatenate(rows + [jnp.zeros((8 - groups, 128), F32)], axis=0)
    pieces = []
    for _ in range(3):
        pieces.append(rest.astype(BF))
        rest = rest - pieces[-1].astype(F32)
    pieces = jnp.concatenate(pieces, axis=0).astype(F32)
    return pieces, jnp.where((slot >> 7) == iota((8, SLOTS), 0), 1.0, 0.0)


def reply_to(value_all, value_high, slot):
    pieces_all, group = reply_rows(value_all, slot)
    pieces_high, _ = reply_rows(value_high, slot)
    pieces = jnp.concatenate([pieces_all, pieces_high], axis=0).astype(BF)
    pick = (iota((128, SLOTS), 0) == (slot & 127)).astype(BF)
    lines = dot(pieces, pick)
    row = iota((8, SLOTS), 0)
    out = []
    for which in range(2):
        line = lines[which * 24 : which * 24 + 8] + lines[which * 24 + 8 : which * 24 + 16] + lines[which * 24 + 16 : which * 24 + 24]
        found = jnp.sum(line * group, axis=0, keepdims=True)
        out.append(jnp.where(row == 4 * which, found, 0.0))
    return out + [jnp.zeros((8, SLOTS), F32)]


def mate_kernel(own_ref, mate_ref, local_ref, out_ref):
    own, mate = read_meta(own_ref, ROWS), read_meta(mate_ref, ROWS)
    mine, theirs = [], None
    for half in range(2):
        rows = own_ref[half * HALF : (half + 1) * HALF, :]
        keys, (found,) = meet(rows, half_ids(own, half), [(mate_ref, ROWS, *mate[:2])])
        mine.append(keys)
        theirs = found if theirs is None else both(theirs, found)
    mine = [jnp.concatenate([mine[0][i], mine[1][i]], axis=1) for i in range(2)]
    mine = both(mine, (local_ref[0:1, :], local_ref[1:2, :]))
    out_ref[...] = jnp.concatenate([*mine, *theirs, jnp.full((4, ROWS), -1.0, F32)], axis=0)


def far_first_kernel(key_ref, own_ref, mate_ref, tail_ref, near_ref, out_ref):
    own, mate = read_meta(own_ref, ROWS), read_meta(mate_ref, ROWS)
    key, tail = read_meta(key_ref, HALF), read_meta(tail_ref, HALF)
    keys, (tails, mates, owns) = meet(
        key_ref[:HALF, :],
        half_ids(key, 0),
        [(tail_ref, HALF, *half_ids(tail, 1)), (mate_ref, ROWS, *mate[:2]), (own_ref, ROWS, *own[:2])],
    )
    owns = both(owns, (near_ref[0:1, :], near_ref[1:2, :]))
    mates = both(mates, (near_ref[2:3, :], near_ref[3:4, :]))
    ends = [jnp.concatenate([keys[i], tails[i]], axis=1) for i in range(2)]
    out_ref[...] = jnp.concatenate([*owns, *mates, *ends, jnp.zeros((2, ROWS), F32)], axis=0)


def far_second_kernel(key_ref, own_ref, mate_ref, tail_ref, first_ref, out_ref, by_slot):
    own, mate = read_meta(own_ref, ROWS), read_meta(mate_ref, ROWS)
    key, tail = read_meta(key_ref, HALF), read_meta(tail_ref, HALF)
    keys, (mates, owns) = meet(
        key_ref[:HALF, :], half_ids(key, 1), [(mate_ref, ROWS, *mate[:2]), (own_ref, ROWS, *own[:2])]
    )
    line = [first_ref[i : i + 1, :] for i in range(6)]
    owns, mates = both(owns, line[0:2]), both(mates, line[2:4])
    keys = [jnp.concatenate([line[4 + i][:, :HALF], keys[i]], axis=1) for i in range(2)]
    tails = [line[4 + i][:, HALF:] for i in range(2)]
    rows = []
    for part, slot in ((owns, own[2]), (mates, mate[2]), (keys, key[2]), (tails, tail[2] - HALF)):
        rows += reply_to(*part, slot)
    rows.append(jnp.zeros((32, SLOTS), F32))
    by_slot[...] = jnp.transpose(jnp.concatenate(rows, axis=0))
    reply = by_slot[pl.ds(0, DEVICES, stride=8), :]
    for order in range(1, 8):
        reply = reply + pltpu.roll(by_slot[pl.ds(order, DEVICES, stride=8), :], order, 1)
    out_ref[...] = reply + pltpu.roll(by_slot[MAIN:, :], 8, 1)


def answer_kernel(got_ref, route_ref, all_ref, high_ref):
    within = route_ref[4:5, :]
    replies = jnp.transpose(got_ref[...])
    row = iota((24, ROWS), 0)
    best = None
    for role in range(ROLES):
        rest = replies[role * 24 : role * 24 + 24]
        pieces = []
        for _ in range(3):
            pieces.append(rest.astype(BF).astype(F32))
            rest = rest - pieces[-1]
        sender = route_ref[role : role + 1, :]
        lines = dot(jnp.concatenate(pieces, axis=0).astype(BF), (iota((DEVICES, ROWS), 0) == sender).astype(BF))
        lines = jnp.where(sender >= 0, lines[0:24] + lines[24:48] + lines[48:72], -1.0)
        best = lines if best is None else jnp.maximum(best, lines)
    all_ref[...] = jnp.sum(jnp.where(row == within, best, 0.0), axis=0, keepdims=True).reshape(ROWS)
    high_ref[...] = jnp.sum(jnp.where(row == within + 12, best, 0.0), axis=0, keepdims=True).reshape(ROWS)


def call(kernel, out, args, scratch=(), flops=0, name=None, left=(), grant=48):
    moved = sum(a.size * a.dtype.itemsize for a in args)
    many = isinstance(out, list)
    shapes = [jax.ShapeDtypeStruct(*o) for o in (out if many else [out])]
    out_specs = [pl.BlockSpec(memory_space=pltpu.VMEM)] * len(shapes)
    return pl.pallas_call(
        kernel,
        out_shape=shapes if many else shapes[0],
        in_specs=[pl.BlockSpec(memory_space=pl.ANY if i in left else pltpu.VMEM) for i in range(len(args))],
        out_specs=out_specs if many else out_specs[0],
        scratch_shapes=list(scratch),
        compiler_params=pltpu.CompilerParams(vmem_limit_bytes=grant * 1024 * 1024),
        cost_estimate=pl.CostEstimate(flops=flops, bytes_accessed=moved, transcendentals=0),
        name=name,
    )(*args)


def body(embeddings, cluster_id, cluster_rank, dest_slot):
    send, route = call(
        pack_kernel,
        [((MAIN, ROWS + 128), BF), ((8, ROWS), jnp.int32)],
        (embeddings, cluster_id, cluster_rank, dest_slot),
        (
            pltpu.VMEM((ROWS, ROWS), BF),
            pltpu.VMEM((ROWS,), jnp.int32),
            pltpu.VMEM((ROWS,), jnp.int32),
            pltpu.VMEM((ROWS,), jnp.int32),
            pltpu.VMEM((ROWS, ROWS), BF),
            pltpu.VMEM((MAIN, 128), F32),
            pltpu.SemaphoreType.DMA((6,)),
        ),
        name="pack",
        left=(0, 1, 2, 3),
        grant=60,
    )
    got = lax.all_to_all(send, AXES, split_axis=0, concat_axis=0, tiled=True)
    own, first = call(
        unpack_kernel,
        [((ROWS + META, ROWS), BF), ((HALF + META, ROWS), BF)],
        (got,),
        (pltpu.VMEM((MAIN, 128), F32), pltpu.VMEM((MAIN, 128), F32)),
        name="unpack",
    )
    second = own[HALF:]
    mate = lax.ppermute(own, AXES, shift(-1))
    key1 = lax.ppermute(first, AXES, shift(2))
    tail = lax.ppermute(second, AXES, shift(-2))
    key2 = lax.ppermute(second, AXES, shift(2))
    tile = 2 * ROWS**3
    local = call(local_kernel, ((8, ROWS), F32), (own,), flops=tile, name="local")
    near = call(mate_kernel, ((8, ROWS), F32), (own, mate, local), flops=tile, name="mate")
    lines = call(far_first_kernel, ((8, ROWS), F32), (key1, own, mate, tail, near), flops=tile, name="far_first")
    reply = call(
        far_second_kernel,
        ((DEVICES, 128), F32),
        (key2, own, mate, tail, lines),
        (pltpu.VMEM((SLOTS, 128), F32),),
        flops=tile,
        name="far_second",
    )
    answer = lax.all_to_all(reply.reshape(DEVICES, 1, 128), AXES, split_axis=0, concat_axis=0, tiled=True)
    return call(answer_kernel, [((ROWS,), F32)] * 2, (answer.reshape(DEVICES, 128), route), name="answer")


def solution(mesh):
    rows = P(AXES)
    return jax.shard_map(
        body,
        mesh=mesh,
        in_specs=(P(AXES, None), rows, rows, rows),
        out_specs=(rows, rows),
        check_vma=False,
    )
```

```python
import jax
import jax.numpy as jnp
from jax import lax
from jax.experimental import pallas as pl
from jax.experimental.pallas import tpu as pltpu
from jax.sharding import PartitionSpec as P

AXES = ("seg", "pair")
DEVICES = 128
PLACES = [
    (3, 0, 1, 1), (0, 0, 1, 1), (3, 1, 1, 1), (0, 1, 1, 1), (3, 2, 1, 1), (0, 2, 1, 1), (3, 2, 2, 1), (0, 2, 2, 1),
    (3, 3, 2, 1), (0, 3, 2, 1), (3, 0, 2, 1), (0, 0, 2, 1), (3, 1, 2, 1), (0, 1, 2, 1), (3, 1, 3, 1), (0, 1, 3, 1),
    (3, 2, 3, 1), (0, 2, 3, 1), (3, 3, 3, 1), (0, 3, 3, 1), (3, 0, 3, 1), (0, 0, 3, 1), (3, 0, 0, 1), (0, 0, 0, 1),
    (3, 1, 0, 1), (0, 1, 0, 1), (3, 2, 0, 1), (0, 2, 0, 1), (3, 3, 0, 1), (0, 3, 0, 1), (3, 3, 1, 1), (0, 3, 1, 1),
    (0, 3, 1, 0), (1, 3, 1, 0), (0, 2, 1, 0), (1, 2, 1, 0), (0, 2, 0, 0), (1, 2, 0, 0), (0, 2, 3, 0), (1, 2, 3, 0),
    (0, 2, 2, 0), (1, 2, 2, 0), (0, 1, 2, 0), (1, 1, 2, 0), (0, 1, 1, 0), (1, 1, 1, 0), (0, 1, 0, 0), (1, 1, 0, 0),
    (0, 1, 3, 0), (1, 1, 3, 0), (0, 0, 3, 0), (1, 0, 3, 0), (0, 0, 2, 0), (1, 0, 2, 0), (0, 0, 1, 0), (1, 0, 1, 0),
    (0, 0, 0, 0), (1, 0, 0, 0), (0, 3, 0, 0), (1, 3, 0, 0), (0, 3, 3, 0), (1, 3, 3, 0), (0, 3, 2, 0), (1, 3, 2, 0),
    (1, 3, 2, 1), (2, 3, 2, 1), (1, 2, 2, 1), (2, 2, 2, 1), (1, 2, 1, 1), (2, 2, 1, 1), (1, 1, 1, 1), (2, 1, 1, 1),
    (1, 0, 1, 1), (2, 0, 1, 1), (1, 3, 1, 1), (2, 3, 1, 1), (1, 3, 0, 1), (2, 3, 0, 1), (1, 2, 0, 1), (2, 2, 0, 1),
    (1, 1, 0, 1), (2, 1, 0, 1), (1, 0, 0, 1), (2, 0, 0, 1), (1, 0, 3, 1), (2, 0, 3, 1), (1, 3, 3, 1), (2, 3, 3, 1),
    (1, 2, 3, 1), (2, 2, 3, 1), (1, 1, 3, 1), (2, 1, 3, 1), (1, 1, 2, 1), (2, 1, 2, 1), (1, 0, 2, 1), (2, 0, 2, 1),
    (2, 0, 2, 0), (3, 0, 2, 0), (2, 0, 3, 0), (3, 0, 3, 0), (2, 1, 3, 0), (3, 1, 3, 0), (2, 1, 0, 0), (3, 1, 0, 0),
    (2, 1, 1, 0), (3, 1, 1, 0), (2, 1, 2, 0), (3, 1, 2, 0), (2, 2, 2, 0), (3, 2, 2, 0), (2, 2, 3, 0), (3, 2, 3, 0),
    (2, 2, 0, 0), (3, 2, 0, 0), (2, 2, 1, 0), (3, 2, 1, 0), (2, 3, 1, 0), (3, 3, 1, 0), (2, 3, 2, 0), (3, 3, 2, 0),
    (2, 3, 3, 0), (3, 3, 3, 0), (2, 3, 0, 0), (3, 3, 0, 0), (2, 0, 0, 0), (3, 0, 0, 0), (2, 0, 1, 0), (3, 0, 1, 0),
]
ROWS = 768
HALF = 384
EARLY = 512
CAP = 9
SLOTS = DEVICES * CAP
MAIN = DEVICES * 8
META = 16
ROLES = 4
BF = jnp.bfloat16
F32 = jnp.float32
NT = (((1,), (1,)), ((), ()))


HOLDERS = [((((x & 1) * 4 + z) * 4 + y) << 2) + ((x >> 1) << 1) + core for x, y, z, core in PLACES]


def device_of(block):
    return HOLDERS[block % DEVICES]


def shift(step):
    return [(device_of(block + step), device_of(block)) for block in range(DEVICES)]


def iota(shape, dim):
    return lax.broadcasted_iota(jnp.int32, shape, dim)


def dot(a, b):
    return jnp.dot(a, b, preferred_element_type=F32)


def dot_nt(a, b):
    return lax.dot_general(a, b, NT, preferred_element_type=F32)


def split_slot(slot):
    block = ((slot >> 8) * 171) >> 9
    return block, slot - block * ROWS


def device_table():
    row, lane = iota((8, DEVICES), 0), iota((8, DEVICES), 1)
    step = jnp.where(row == 1, 1, jnp.where(row == 2, -2, jnp.where(row == 3, 2, 0)))
    block = (lane + step) & (DEVICES - 1)
    found = jnp.zeros_like(block)
    for index, device in enumerate(HOLDERS):
        found = jnp.where(block == index, device, found)
    return found.astype(F32).astype(BF)


def pack_kernel(emb_ref, cid_ref, rank_ref, slot_ref, out_ref, route_ref, raw, slots, cids, ranks, unit, extra, sems):
    ids = ((slot_ref, slots), (cid_ref, cids), (rank_ref, ranks))
    small = [pltpu.make_async_copy(*pair, sems.at[3 + i]) for i, pair in enumerate(ids)]
    copies = [
        pltpu.make_async_copy(emb_ref.at[pl.ds(part * 256, 256)], raw.at[pl.ds(part * 256, 256)], sems.at[part])
        for part in range(3)
    ]
    for copy in small + copies:
        copy.start()
    table = device_table()
    earlier = (iota((ROWS, ROWS), 0) < iota((ROWS, ROWS), 1)).astype(BF)
    for copy in small:
        copy.wait()
    slot, cid, rank = (ref[...].reshape(1, ROWS) for _, ref in ids)
    block, local = split_slot(slot)
    to_block = (iota((DEVICES, ROWS), 0) == block).astype(BF)
    within = jnp.sum(to_block.astype(F32) * dot(to_block, earlier), axis=0, keepdims=True).astype(jnp.int32)
    senders = dot(table, to_block).astype(jnp.int32)
    row = iota((8, ROWS), 0)
    dropped = (row == 3) & (local < HALF)
    route_ref[...] = jnp.where(row == 4, within, jnp.where(dropped, -1, senders))
    device = senders[0:1]
    to_device = (iota((DEVICES, ROWS), 0) == device).astype(BF)
    flat = jnp.where(within < 8, device * 8 + within, -1)
    for part, copy in enumerate(copies):
        copy.wait()
        values = raw[part * 256 : (part + 1) * 256, :].astype(F32)
        scaling = lax.rsqrt(jnp.sum(values * values, axis=1, keepdims=True) + 1e-06)
        unit[part * 256 : (part + 1) * 256, :] = (values * scaling).astype(BF)
    for start in range(0, MAIN, 256):
        pick = (iota((256, ROWS), 0) + start == flat).astype(BF)
        out_ref[start : start + 256, :ROWS] = dot(pick, unit[...]).astype(BF)
    ninth = jnp.where(within == 8, to_device, jnp.zeros_like(to_device))
    ninth_rows = dot(ninth, unit[...])
    field = iota((DEVICES, ROWS), 0) >> 4
    meta = jnp.where(field == 0, (local >> 8) + 1, jnp.where(field == 1, local & 255, jnp.where(field == 2, cid + 1, 0)))
    meta = jnp.where(field == 3, rank >> 8, jnp.where(field == 4, rank & 255, meta))
    meta = jnp.where((iota((DEVICES, ROWS), 0) & 15) == within, meta, 0).astype(F32).astype(BF)
    extra[...] = jnp.zeros_like(extra)
    for part in range(6):
        extra[pl.ds(part, DEVICES, stride=8), :] = ninth_rows[:, part * 128 : (part + 1) * 128]
    extra[pl.ds(6, DEVICES, stride=8), :] = dot_nt(to_device, meta)
    out_ref[:, ROWS:] = extra[...].astype(BF)


def unpack_kernel(got_ref, out_ref, first_ref, extra, spread):
    extra[...] = got_ref[:, ROWS:].astype(F32)
    ninth_rows = jnp.concatenate([extra[pl.ds(part, DEVICES, stride=8), :] for part in range(6)], axis=1).astype(BF)
    meta = extra[pl.ds(6, DEVICES, stride=8), :]
    for order in range(8):
        spread[pl.ds(order, DEVICES, stride=8), :] = meta
    lane, row = iota((MAIN, 128), 1), iota((MAIN, 128), 0)
    main = jnp.where((lane & 15) == (row & 7), spread[...], 0.0).astype(BF)
    last = jnp.where((iota((DEVICES, 128), 1) & 15) == 8, meta, 0.0).astype(BF)
    fields = ((iota((META, 128), 1) >> 4) == iota((META, 128), 0)).astype(BF)
    by_slot = jnp.concatenate([dot_nt(fields, main), dot_nt(fields, last)], axis=1)
    slot = ((by_slot[0:1] - 1.0) * 256.0 + by_slot[1:2]).astype(jnp.int32)
    cols = by_slot.astype(BF)
    for start in range(0, ROWS, 256):
        pick = (iota((256, SLOTS), 0) + start == slot).astype(BF)
        rows = dot(pick[:, :MAIN], got_ref[:, :ROWS]) + dot(pick[:, MAIN:], ninth_rows)
        out_ref[start : start + 256, :] = rows.astype(BF)
        placed = dot_nt(cols, pick)
        kept = jnp.concatenate([placed[2:5], jnp.zeros((13, 256), F32)], axis=0)
        out_ref[ROWS:, start : start + 256] = kept.astype(BF)
    out_ref[ROWS + 8 : ROWS + 9, :] = cols[0:1, :ROWS]
    out_ref[ROWS + 9 : ROWS + 10, :] = cols[1:2, :ROWS]
    out_ref[ROWS + 10 : ROWS + 11, :HALF] = cols[0:1, ROWS:]
    out_ref[ROWS + 11 : ROWS + 12, :HALF] = cols[1:2, ROWS:]
    first_ref[:EARLY, :] = out_ref[:EARLY, :]
    first_ref[EARLY:, :] = out_ref[ROWS:, :]


def read_meta(block_ref, rows):
    meta = block_ref[rows:, :].astype(F32)
    cid, rank = meta[0:1], meta[1:2] * 256.0 + meta[2:3]
    high = jnp.concatenate([meta[8:9], meta[10:11, :HALF]], axis=1)
    low = jnp.concatenate([meta[9:10], meta[11:12, :HALF]], axis=1)
    slot = ((high - 1.0) * 256.0 + low).astype(jnp.int32)
    return cid, rank, slot


def columns(cid, rank):
    both = jnp.concatenate([cid, rank, jnp.zeros((6, cid.shape[1]), F32)], axis=0)
    turned = jnp.transpose(both)
    return turned[:, 0:1], turned[:, 1:2]


def local_kernel(own_ref, out_ref):
    own_cid, own_rank, _ = read_meta(own_ref, ROWS)
    cid, rank = columns(own_cid, own_rank)
    best_all = jnp.full((8, ROWS), -1.0, F32)
    best_high = jnp.full((8, ROWS), -1.0, F32)
    for start in range(0, ROWS, HALF):
        cosine = dot_nt(own_ref[start : start + HALF, :], own_ref[:ROWS, :])
        c, r = cid[start : start + HALF], rank[start : start + HALF]
        near = jnp.where((c == own_cid) & (r != own_rank), cosine, -1.0)
        high = jnp.where(r < own_rank, near, -1.0)
        best_all = jnp.maximum(best_all, jnp.max(near.reshape(HALF // 8, 8, ROWS), axis=0))
        best_high = jnp.maximum(best_high, jnp.max(high.reshape(HALF // 8, 8, ROWS), axis=0))
    out_ref[0:1, :] = jnp.max(best_all, axis=0, keepdims=True)
    out_ref[1:2, :] = jnp.max(best_high, axis=0, keepdims=True)
    out_ref[2:, :] = jnp.full((6, ROWS), -1.0, F32)


def meet(key, ids, others):
    cid, rank = columns(*ids)
    rows = key.shape[0]
    key_all = jnp.full((rows, 128), -1.0, F32)
    key_high, found = key_all, []
    for ref, count, other_cid, other_rank in others:
        near = HALF if count == HALF else rows
        wide_all, wide_high, row_all, row_high = against(key[:near], cid[:near], rank[:near], ref, count, other_cid, other_rank)
        if near < rows:
            rest = jnp.full((rows - near, 128), -1.0, F32)
            wide_all, wide_high = jnp.concatenate([wide_all, rest], axis=0), jnp.concatenate([wide_high, rest], axis=0)
        key_all, key_high = jnp.maximum(key_all, wide_all), jnp.maximum(key_high, wide_high)
        found.append((row_all, row_high))
    return tuple(jnp.max(jnp.transpose(wide), axis=0, keepdims=True) for wide in (key_all, key_high)), found


def ids_of(ids, start, stop):
    return ids[0][:, start:stop], ids[1][:, start:stop]


def both(left, right):
    return tuple(jnp.maximum(a, b) for a, b in zip(left, right))


def against(key, key_cid, key_rank, other_ref, count, other_cid, other_rank):
    cosine = dot_nt(key, other_ref[:count, :])
    near = jnp.where(key_cid == other_cid, cosine, -1.0)
    before = other_rank < key_rank
    high = jnp.where(before, near, -1.0)
    low = jnp.where(before, -1.0, near)
    wide_all, wide_high = near[:, :128], high[:, :128]
    for lane in range(128, count, 128):
        wide_all = jnp.maximum(wide_all, near[:, lane : lane + 128])
        wide_high = jnp.maximum(wide_high, high[:, lane : lane + 128])
    return wide_all, wide_high, jnp.max(near, axis=0, keepdims=True), jnp.max(low, axis=0, keepdims=True)


def reply_rows(value, slot):
    groups = value.shape[1] // 128
    rows = [value[:, g * 128 : (g + 1) * 128] for g in range(groups)]
    rest = jnp.concatenate(rows + [jnp.zeros((8 - groups, 128), F32)], axis=0)
    pieces = []
    for _ in range(3):
        pieces.append(rest.astype(BF))
        rest = rest - pieces[-1].astype(F32)
    pieces = jnp.concatenate(pieces, axis=0).astype(F32)
    return pieces, jnp.where((slot >> 7) == iota((8, SLOTS), 0), 1.0, 0.0)


def reply_to(value_all, value_high, slot):
    pieces_all, group = reply_rows(value_all, slot)
    pieces_high, _ = reply_rows(value_high, slot)
    pieces = jnp.concatenate([pieces_all, pieces_high], axis=0).astype(BF)
    pick = (iota((128, SLOTS), 0) == (slot & 127)).astype(BF)
    lines = dot(pieces, pick)
    row = iota((8, SLOTS), 0)
    out = []
    for which in range(2):
        line = lines[which * 24 : which * 24 + 8] + lines[which * 24 + 8 : which * 24 + 16] + lines[which * 24 + 16 : which * 24 + 24]
        found = jnp.sum(line * group, axis=0, keepdims=True)
        out.append(jnp.where(row == 4 * which, found, 0.0))
    return out + [jnp.zeros((8, SLOTS), F32)]


def mate_kernel(own_ref, mate_ref, local_ref, out_ref):
    own, mate = read_meta(own_ref, ROWS), read_meta(mate_ref, ROWS)
    mine, theirs = [], None
    for half in range(2):
        rows = own_ref[half * HALF : (half + 1) * HALF, :]
        keys, (found,) = meet(rows, ids_of(own, half * HALF, half * HALF + HALF), [(mate_ref, ROWS, *mate[:2])])
        mine.append(keys)
        theirs = found if theirs is None else both(theirs, found)
    mine = [jnp.concatenate([mine[0][i], mine[1][i]], axis=1) for i in range(2)]
    mine = both(mine, (local_ref[0:1, :], local_ref[1:2, :]))
    out_ref[...] = jnp.concatenate([*mine, *theirs, jnp.full((4, ROWS), -1.0, F32)], axis=0)


def far_first_kernel(key_ref, own_ref, mate_ref, tail_ref, near_ref, out_ref):
    own, mate = read_meta(own_ref, ROWS), read_meta(mate_ref, ROWS)
    key, tail = read_meta(key_ref, EARLY), read_meta(tail_ref, HALF)
    keys, (tails, mates, owns) = meet(
        key_ref[:EARLY, :],
        ids_of(key, 0, EARLY),
        [(tail_ref, HALF, *ids_of(tail, HALF, ROWS)), (mate_ref, ROWS, *mate[:2]), (own_ref, ROWS, *own[:2])],
    )
    owns = both(owns, (near_ref[0:1, :], near_ref[1:2, :]))
    mates = both(mates, (near_ref[2:3, :], near_ref[3:4, :]))
    lines = [jnp.concatenate([keys[i], jnp.zeros((1, ROWS - EARLY), F32)], axis=1) for i in range(2)]
    lines += [jnp.concatenate([tails[i], jnp.zeros((1, HALF), F32)], axis=1) for i in range(2)]
    out_ref[...] = jnp.concatenate([*owns, *mates, *lines], axis=0)


def far_second_kernel(key_ref, own_ref, mate_ref, early_ref, tail_ref, first_ref, out_ref, by_slot):
    own, mate = read_meta(own_ref, ROWS), read_meta(mate_ref, ROWS)
    key, tail = read_meta(early_ref, EARLY), read_meta(tail_ref, HALF)
    keys, (mates, owns) = meet(
        key_ref[...], ids_of(key, EARLY, ROWS), [(mate_ref, ROWS, *mate[:2]), (own_ref, ROWS, *own[:2])]
    )
    line = [first_ref[i : i + 1, :] for i in range(8)]
    owns, mates = both(owns, line[0:2]), both(mates, line[2:4])
    keys = [jnp.concatenate([line[4 + i][:, :EARLY], keys[i]], axis=1) for i in range(2)]
    tails = [line[6 + i][:, :HALF] for i in range(2)]
    rows = []
    for part, slot in ((owns, own[2]), (mates, mate[2]), (keys, key[2]), (tails, tail[2] - HALF)):
        rows += reply_to(*part, slot)
    rows.append(jnp.zeros((32, SLOTS), F32))
    by_slot[...] = jnp.transpose(jnp.concatenate(rows, axis=0))
    reply = by_slot[pl.ds(0, DEVICES, stride=8), :]
    for order in range(1, 8):
        reply = reply + pltpu.roll(by_slot[pl.ds(order, DEVICES, stride=8), :], order, 1)
    out_ref[...] = reply + pltpu.roll(by_slot[MAIN:, :], 8, 1)


def answer_kernel(got_ref, route_ref, all_ref, high_ref):
    within = route_ref[4:5, :]
    replies = jnp.transpose(got_ref[...])
    row = iota((24, ROWS), 0)
    best = None
    for role in range(ROLES):
        rest = replies[role * 24 : role * 24 + 24]
        pieces = []
        for _ in range(3):
            pieces.append(rest.astype(BF).astype(F32))
            rest = rest - pieces[-1]
        sender = route_ref[role : role + 1, :]
        lines = dot(jnp.concatenate(pieces, axis=0).astype(BF), (iota((DEVICES, ROWS), 0) == sender).astype(BF))
        lines = jnp.where(sender >= 0, lines[0:24] + lines[24:48] + lines[48:72], -1.0)
        best = lines if best is None else jnp.maximum(best, lines)
    all_ref[...] = jnp.sum(jnp.where(row == within, best, 0.0), axis=0, keepdims=True).reshape(ROWS)
    high_ref[...] = jnp.sum(jnp.where(row == within + 12, best, 0.0), axis=0, keepdims=True).reshape(ROWS)


def call(kernel, out, args, scratch=(), flops=0, name=None, left=(), grant=48):
    moved = sum(a.size * a.dtype.itemsize for a in args)
    many = isinstance(out, list)
    shapes = [jax.ShapeDtypeStruct(*o) for o in (out if many else [out])]
    out_specs = [pl.BlockSpec(memory_space=pltpu.VMEM)] * len(shapes)
    return pl.pallas_call(
        kernel,
        out_shape=shapes if many else shapes[0],
        in_specs=[pl.BlockSpec(memory_space=pl.ANY if i in left else pltpu.VMEM) for i in range(len(args))],
        out_specs=out_specs if many else out_specs[0],
        scratch_shapes=list(scratch),
        compiler_params=pltpu.CompilerParams(vmem_limit_bytes=grant * 1024 * 1024),
        cost_estimate=pl.CostEstimate(flops=flops, bytes_accessed=moved, transcendentals=0),
        name=name,
    )(*args)


def body(embeddings, cluster_id, cluster_rank, dest_slot):
    send, route = call(
        pack_kernel,
        [((MAIN, ROWS + 128), BF), ((8, ROWS), jnp.int32)],
        (embeddings, cluster_id, cluster_rank, dest_slot),
        (
            pltpu.VMEM((ROWS, ROWS), BF),
            pltpu.VMEM((ROWS,), jnp.int32),
            pltpu.VMEM((ROWS,), jnp.int32),
            pltpu.VMEM((ROWS,), jnp.int32),
            pltpu.VMEM((ROWS, ROWS), BF),
            pltpu.VMEM((MAIN, 128), F32),
            pltpu.SemaphoreType.DMA((6,)),
        ),
        name="pack",
        left=(0, 1, 2, 3),
        grant=60,
    )
    got = lax.all_to_all(send, AXES, split_axis=0, concat_axis=0, tiled=True)
    own, first = call(
        unpack_kernel,
        [((ROWS + META, ROWS), BF), ((EARLY + META, ROWS), BF)],
        (got,),
        (pltpu.VMEM((MAIN, 128), F32), pltpu.VMEM((MAIN, 128), F32)),
        name="unpack",
    )
    mate = lax.ppermute(own, AXES, shift(-1))
    key1 = lax.ppermute(first, AXES, shift(2))
    tail = lax.ppermute(own[HALF:], AXES, shift(-2))
    key2 = lax.ppermute(own[EARLY:ROWS], AXES, shift(2))
    tile = 2 * ROWS**3
    local = call(local_kernel, ((8, ROWS), F32), (own,), flops=tile, name="local")
    near = call(mate_kernel, ((8, ROWS), F32), (own, mate, local), flops=tile, name="mate")
    lines = call(far_first_kernel, ((8, ROWS), F32), (key1, own, mate, tail, near), flops=tile, name="far_first")
    reply = call(
        far_second_kernel,
        ((DEVICES, 128), F32),
        (key2, own, mate, key1, tail, lines),
        (pltpu.VMEM((SLOTS, 128), F32),),
        flops=tile,
        name="far_second",
    )
    answer = lax.all_to_all(reply.reshape(DEVICES, 1, 128), AXES, split_axis=0, concat_axis=0, tiled=True)
    return call(answer_kernel, [((ROWS,), F32)] * 2, (answer.reshape(DEVICES, 128), route), name="answer")


def solution(mesh):
    rows = P(AXES)
    return jax.shard_map(
        body,
        mesh=mesh,
        in_specs=(P(AXES, None), rows, rows, rows),
        out_specs=(rows, rows),
        check_vma=False,
    )
```

```python
import jax
import jax.numpy as jnp
from jax import lax
from jax.experimental import pallas as pl
from jax.experimental.pallas import tpu as pltpu
from jax.sharding import PartitionSpec as P

AXES = ("seg", "pair")
DEVICES = 128
PLACES = [
    (3, 0, 1, 1), (0, 0, 1, 1), (3, 1, 1, 1), (0, 1, 1, 1), (3, 2, 1, 1), (0, 2, 1, 1), (3, 2, 2, 1), (0, 2, 2, 1),
    (3, 3, 2, 1), (0, 3, 2, 1), (3, 0, 2, 1), (0, 0, 2, 1), (3, 1, 2, 1), (0, 1, 2, 1), (3, 1, 3, 1), (0, 1, 3, 1),
    (3, 2, 3, 1), (0, 2, 3, 1), (3, 3, 3, 1), (0, 3, 3, 1), (3, 0, 3, 1), (0, 0, 3, 1), (3, 0, 0, 1), (0, 0, 0, 1),
    (3, 1, 0, 1), (0, 1, 0, 1), (3, 2, 0, 1), (0, 2, 0, 1), (3, 3, 0, 1), (0, 3, 0, 1), (3, 3, 1, 1), (0, 3, 1, 1),
    (0, 3, 1, 0), (1, 3, 1, 0), (0, 2, 1, 0), (1, 2, 1, 0), (0, 2, 0, 0), (1, 2, 0, 0), (0, 2, 3, 0), (1, 2, 3, 0),
    (0, 2, 2, 0), (1, 2, 2, 0), (0, 1, 2, 0), (1, 1, 2, 0), (0, 1, 1, 0), (1, 1, 1, 0), (0, 1, 0, 0), (1, 1, 0, 0),
    (0, 1, 3, 0), (1, 1, 3, 0), (0, 0, 3, 0), (1, 0, 3, 0), (0, 0, 2, 0), (1, 0, 2, 0), (0, 0, 1, 0), (1, 0, 1, 0),
    (0, 0, 0, 0), (1, 0, 0, 0), (0, 3, 0, 0), (1, 3, 0, 0), (0, 3, 3, 0), (1, 3, 3, 0), (0, 3, 2, 0), (1, 3, 2, 0),
    (1, 3, 2, 1), (2, 3, 2, 1), (1, 2, 2, 1), (2, 2, 2, 1), (1, 2, 1, 1), (2, 2, 1, 1), (1, 1, 1, 1), (2, 1, 1, 1),
    (1, 0, 1, 1), (2, 0, 1, 1), (1, 3, 1, 1), (2, 3, 1, 1), (1, 3, 0, 1), (2, 3, 0, 1), (1, 2, 0, 1), (2, 2, 0, 1),
    (1, 1, 0, 1), (2, 1, 0, 1), (1, 0, 0, 1), (2, 0, 0, 1), (1, 0, 3, 1), (2, 0, 3, 1), (1, 3, 3, 1), (2, 3, 3, 1),
    (1, 2, 3, 1), (2, 2, 3, 1), (1, 1, 3, 1), (2, 1, 3, 1), (1, 1, 2, 1), (2, 1, 2, 1), (1, 0, 2, 1), (2, 0, 2, 1),
    (2, 0, 2, 0), (3, 0, 2, 0), (2, 0, 3, 0), (3, 0, 3, 0), (2, 1, 3, 0), (3, 1, 3, 0), (2, 1, 0, 0), (3, 1, 0, 0),
    (2, 1, 1, 0), (3, 1, 1, 0), (2, 1, 2, 0), (3, 1, 2, 0), (2, 2, 2, 0), (3, 2, 2, 0), (2, 2, 3, 0), (3, 2, 3, 0),
    (2, 2, 0, 0), (3, 2, 0, 0), (2, 2, 1, 0), (3, 2, 1, 0), (2, 3, 1, 0), (3, 3, 1, 0), (2, 3, 2, 0), (3, 3, 2, 0),
    (2, 3, 3, 0), (3, 3, 3, 0), (2, 3, 0, 0), (3, 3, 0, 0), (2, 0, 0, 0), (3, 0, 0, 0), (2, 0, 1, 0), (3, 0, 1, 0),
]
ROWS = 768
HALF = 384
EARLY = 512
CAP = 9
SLOTS = DEVICES * CAP
MAIN = DEVICES * 8
META = 16
ROLES = 4
BF = jnp.bfloat16
F32 = jnp.float32
NT = (((1,), (1,)), ((), ()))


HOLDERS = [((((x & 1) * 4 + z) * 4 + y) << 2) + ((x >> 1) << 1) + core for x, y, z, core in PLACES]


def device_of(block):
    return HOLDERS[block % DEVICES]


def shift(step):
    return [(device_of(block + step), device_of(block)) for block in range(DEVICES)]


def iota(shape, dim):
    return lax.broadcasted_iota(jnp.int32, shape, dim)


def dot(a, b):
    return jnp.dot(a, b, preferred_element_type=F32)


def dot_nt(a, b):
    return lax.dot_general(a, b, NT, preferred_element_type=F32)


def split_slot(slot):
    block = ((slot >> 8) * 171) >> 9
    return block, slot - block * ROWS


def device_table():
    row, lane = iota((8, DEVICES), 0), iota((8, DEVICES), 1)
    step = jnp.where(row == 1, 1, jnp.where(row == 2, -2, jnp.where(row == 3, 2, 0)))
    block = (lane + step) & (DEVICES - 1)
    found = jnp.zeros_like(block)
    for index, device in enumerate(HOLDERS):
        found = jnp.where(block == index, device, found)
    return found.astype(F32).astype(BF)


def pack_kernel(emb_ref, cid_ref, rank_ref, slot_ref, out_ref, route_ref, raw, slots, cids, ranks, unit, extra, sems):
    ids = ((slot_ref, slots), (cid_ref, cids), (rank_ref, ranks))
    small = [pltpu.make_async_copy(*pair, sems.at[3 + i]) for i, pair in enumerate(ids)]
    copies = [
        pltpu.make_async_copy(emb_ref.at[pl.ds(part * 256, 256)], raw.at[pl.ds(part * 256, 256)], sems.at[part])
        for part in range(3)
    ]
    for copy in small + copies:
        copy.start()
    table = device_table()
    earlier = (iota((ROWS, ROWS), 0) < iota((ROWS, ROWS), 1)).astype(BF)
    for copy in small:
        copy.wait()
    slot, cid, rank = (ref[...].reshape(1, ROWS) for _, ref in ids)
    block, local = split_slot(slot)
    to_block = (iota((DEVICES, ROWS), 0) == block).astype(BF)
    within = jnp.sum(to_block.astype(F32) * dot(to_block, earlier), axis=0, keepdims=True).astype(jnp.int32)
    senders = dot(table, to_block).astype(jnp.int32)
    row = iota((8, ROWS), 0)
    dropped = (row == 3) & (local < HALF)
    route_ref[...] = jnp.where(row == 4, within, jnp.where(dropped, -1, senders))
    device = senders[0:1]
    to_device = (iota((DEVICES, ROWS), 0) == device).astype(BF)
    flat = jnp.where(within < 8, device * 8 + within, -1)
    for part, copy in enumerate(copies):
        copy.wait()
        values = raw[part * 256 : (part + 1) * 256, :].astype(F32)
        scaling = lax.rsqrt(jnp.sum(values * values, axis=1, keepdims=True) + 1e-06)
        unit[part * 256 : (part + 1) * 256, :] = (values * scaling).astype(BF)
    for start in range(0, MAIN, 256):
        pick = (iota((256, ROWS), 0) + start == flat).astype(BF)
        out_ref[start : start + 256, :ROWS] = dot(pick, unit[...]).astype(BF)
    ninth = jnp.where(within == 8, to_device, jnp.zeros_like(to_device))
    ninth_rows = dot(ninth, unit[...])
    field = iota((DEVICES, ROWS), 0) >> 4
    meta = jnp.where(field == 0, (local >> 8) + 1, jnp.where(field == 1, local & 255, jnp.where(field == 2, cid + 1, 0)))
    meta = jnp.where(field == 3, rank >> 8, jnp.where(field == 4, rank & 255, meta))
    meta = jnp.where((iota((DEVICES, ROWS), 0) & 15) == within, meta, 0).astype(F32).astype(BF)
    extra[...] = jnp.zeros_like(extra)
    for part in range(6):
        extra[pl.ds(part, DEVICES, stride=8), :] = ninth_rows[:, part * 128 : (part + 1) * 128]
    extra[pl.ds(6, DEVICES, stride=8), :] = dot_nt(to_device, meta)
    out_ref[:, ROWS:] = extra[...].astype(BF)


def unpack_kernel(got_ref, out_ref, first_ref, extra, spread):
    extra[...] = got_ref[:, ROWS:].astype(F32)
    ninth_rows = jnp.concatenate([extra[pl.ds(part, DEVICES, stride=8), :] for part in range(6)], axis=1).astype(BF)
    meta = extra[pl.ds(6, DEVICES, stride=8), :]
    for order in range(8):
        spread[pl.ds(order, DEVICES, stride=8), :] = meta
    lane, row = iota((MAIN, 128), 1), iota((MAIN, 128), 0)
    main = jnp.where((lane & 15) == (row & 7), spread[...], 0.0).astype(BF)
    last = jnp.where((iota((DEVICES, 128), 1) & 15) == 8, meta, 0.0).astype(BF)
    fields = ((iota((META, 128), 1) >> 4) == iota((META, 128), 0)).astype(BF)
    by_slot = jnp.concatenate([dot_nt(fields, main), dot_nt(fields, last)], axis=1)
    slot = ((by_slot[0:1] - 1.0) * 256.0 + by_slot[1:2]).astype(jnp.int32)
    cols = by_slot.astype(BF)
    for start in range(0, ROWS, 256):
        pick = (iota((256, SLOTS), 0) + start == slot).astype(BF)
        rows = dot(pick[:, :MAIN], got_ref[:, :ROWS]) + dot(pick[:, MAIN:], ninth_rows)
        out_ref[start : start + 256, :] = rows.astype(BF)
        placed = dot_nt(cols, pick)
        kept = jnp.concatenate([placed[2:5], jnp.zeros((13, 256), F32)], axis=0)
        out_ref[ROWS:, start : start + 256] = kept.astype(BF)
    out_ref[ROWS + 8 : ROWS + 9, :] = cols[0:1, :ROWS]
    out_ref[ROWS + 9 : ROWS + 10, :] = cols[1:2, :ROWS]
    out_ref[ROWS + 10 : ROWS + 11, :HALF] = cols[0:1, ROWS:]
    out_ref[ROWS + 11 : ROWS + 12, :HALF] = cols[1:2, ROWS:]
    first_ref[:EARLY, :] = out_ref[:EARLY, :]
    first_ref[EARLY:, :] = out_ref[ROWS:, :]


def read_meta(block_ref, rows):
    meta = block_ref[rows:, :].astype(F32)
    cid, rank = meta[0:1], meta[1:2] * 256.0 + meta[2:3]
    high = jnp.concatenate([meta[8:9], meta[10:11, :HALF]], axis=1)
    low = jnp.concatenate([meta[9:10], meta[11:12, :HALF]], axis=1)
    slot = ((high - 1.0) * 256.0 + low).astype(jnp.int32)
    return cid, rank, slot


def columns(cid, rank):
    both = jnp.concatenate([cid, rank, jnp.zeros((6, cid.shape[1]), F32)], axis=0)
    turned = jnp.transpose(both)
    return turned[:, 0:1], turned[:, 1:2]


def local_kernel(own_ref, out_ref):
    own_cid, own_rank, _ = read_meta(own_ref, ROWS)
    cid, rank = columns(own_cid, own_rank)
    best_all = jnp.full((8, ROWS), -1.0, F32)
    best_high = jnp.full((8, ROWS), -1.0, F32)
    for start in range(0, ROWS, HALF):
        cosine = dot_nt(own_ref[start : start + HALF, :], own_ref[:ROWS, :])
        c, r = cid[start : start + HALF], rank[start : start + HALF]
        near = jnp.where((c == own_cid) & (r != own_rank), cosine, -1.0)
        high = jnp.where(r < own_rank, near, -1.0)
        best_all = jnp.maximum(best_all, jnp.max(near.reshape(HALF // 8, 8, ROWS), axis=0))
        best_high = jnp.maximum(best_high, jnp.max(high.reshape(HALF // 8, 8, ROWS), axis=0))
    out_ref[0:1, :] = jnp.max(best_all, axis=0, keepdims=True)
    out_ref[1:2, :] = jnp.max(best_high, axis=0, keepdims=True)
    out_ref[2:, :] = jnp.full((6, ROWS), -1.0, F32)


def meet(key, ids, others):
    cid, rank = columns(*ids)
    rows = key.shape[0]
    key_all = jnp.full((rows, 128), -1.0, F32)
    key_high, found = key_all, []
    for ref, count, other_cid, other_rank in others:
        near = HALF if count == HALF else rows
        wide_all, wide_high, row_all, row_high = against(key[:near], cid[:near], rank[:near], ref, count, other_cid, other_rank)
        if near < rows:
            rest = jnp.full((rows - near, 128), -1.0, F32)
            wide_all, wide_high = jnp.concatenate([wide_all, rest], axis=0), jnp.concatenate([wide_high, rest], axis=0)
        key_all, key_high = jnp.maximum(key_all, wide_all), jnp.maximum(key_high, wide_high)
        found.append((row_all, row_high))
    return tuple(jnp.max(jnp.transpose(wide), axis=0, keepdims=True) for wide in (key_all, key_high)), found


def ids_of(ids, start, stop):
    return ids[0][:, start:stop], ids[1][:, start:stop]


def both(left, right):
    return tuple(jnp.maximum(a, b) for a, b in zip(left, right))


def against(key, key_cid, key_rank, other_ref, count, other_cid, other_rank):
    cosine = dot_nt(key, other_ref[:count, :])
    near = jnp.where(key_cid == other_cid, cosine, -1.0)
    before = other_rank < key_rank
    high = jnp.where(before, near, -1.0)
    low = jnp.where(before, -1.0, near)
    wide_all, wide_high = near[:, :128], high[:, :128]
    for lane in range(128, count, 128):
        wide_all = jnp.maximum(wide_all, near[:, lane : lane + 128])
        wide_high = jnp.maximum(wide_high, high[:, lane : lane + 128])
    return wide_all, wide_high, jnp.max(near, axis=0, keepdims=True), jnp.max(low, axis=0, keepdims=True)


def reply_rows(value, slot):
    groups = value.shape[1] // 128
    rows = [value[:, g * 128 : (g + 1) * 128] for g in range(groups)]
    rest = jnp.concatenate(rows + [jnp.zeros((8 - groups, 128), F32)], axis=0)
    pieces = []
    for _ in range(3):
        pieces.append(rest.astype(BF))
        rest = rest - pieces[-1].astype(F32)
    pieces = jnp.concatenate(pieces, axis=0).astype(F32)
    return pieces, jnp.where((slot >> 7) == iota((8, SLOTS), 0), 1.0, 0.0)


def reply_to(value_all, value_high, slot):
    pieces_all, group = reply_rows(value_all, slot)
    pieces_high, _ = reply_rows(value_high, slot)
    pieces = jnp.concatenate([pieces_all, pieces_high], axis=0).astype(BF)
    pick = (iota((128, SLOTS), 0) == (slot & 127)).astype(BF)
    lines = dot(pieces, pick)
    row = iota((8, SLOTS), 0)
    out = []
    for which in range(2):
        line = lines[which * 24 : which * 24 + 8] + lines[which * 24 + 8 : which * 24 + 16] + lines[which * 24 + 16 : which * 24 + 24]
        found = jnp.sum(line * group, axis=0, keepdims=True)
        out.append(jnp.where(row == 4 * which, found, 0.0))
    return out + [jnp.zeros((8, SLOTS), F32)]


def mate_kernel(own_ref, mate_ref, local_ref, out_ref):
    own, mate = read_meta(own_ref, ROWS), read_meta(mate_ref, ROWS)
    mine, theirs = [], None
    for half in range(2):
        rows = own_ref[half * HALF : (half + 1) * HALF, :]
        keys, (found,) = meet(rows, ids_of(own, half * HALF, half * HALF + HALF), [(mate_ref, ROWS, *mate[:2])])
        mine.append(keys)
        theirs = found if theirs is None else both(theirs, found)
    mine = [jnp.concatenate([mine[0][i], mine[1][i]], axis=1) for i in range(2)]
    mine = both(mine, (local_ref[0:1, :], local_ref[1:2, :]))
    out_ref[...] = jnp.concatenate([*mine, *theirs, jnp.full((4, ROWS), -1.0, F32)], axis=0)


def far_first_kernel(key_ref, own_ref, mate_ref, tail_ref, near_ref, out_ref, tail_rows_ref):
    own, mate = read_meta(own_ref, ROWS), read_meta(mate_ref, ROWS)
    key, tail = read_meta(key_ref, EARLY), read_meta(tail_ref, HALF)
    keys, (tails, mates, owns) = meet(
        key_ref[:EARLY, :],
        ids_of(key, 0, EARLY),
        [(tail_ref, HALF, *ids_of(tail, HALF, ROWS)), (mate_ref, ROWS, *mate[:2]), (own_ref, ROWS, *own[:2])],
    )
    owns = both(owns, (near_ref[0:1, :], near_ref[1:2, :]))
    mates = both(mates, (near_ref[2:3, :], near_ref[3:4, :]))
    lines = [jnp.concatenate([keys[i], jnp.zeros((1, ROWS - EARLY), F32)], axis=1) for i in range(2)]
    out_ref[...] = jnp.concatenate([*owns, *mates, *lines, jnp.zeros((2, ROWS), F32)], axis=0)
    tail_rows_ref[...] = jnp.concatenate(reply_to(*tails, tail[2] - HALF), axis=0)


def far_second_kernel(key_ref, own_ref, mate_ref, early_ref, first_ref, tail_rows_ref, out_ref, by_slot):
    own, mate = read_meta(own_ref, ROWS), read_meta(mate_ref, ROWS)
    key = read_meta(early_ref, EARLY)
    keys, (mates, owns) = meet(
        key_ref[...], ids_of(key, EARLY, ROWS), [(mate_ref, ROWS, *mate[:2]), (own_ref, ROWS, *own[:2])]
    )
    line = [first_ref[i : i + 1, :] for i in range(6)]
    owns, mates = both(owns, line[0:2]), both(mates, line[2:4])
    keys = [jnp.concatenate([line[4 + i][:, :EARLY], keys[i]], axis=1) for i in range(2)]
    rows = []
    for part, slot in ((owns, own[2]), (mates, mate[2]), (keys, key[2])):
        rows += reply_to(*part, slot)
    rows += [tail_rows_ref[...], jnp.zeros((32, SLOTS), F32)]
    by_slot[...] = jnp.transpose(jnp.concatenate(rows, axis=0))
    reply = by_slot[pl.ds(0, DEVICES, stride=8), :]
    for order in range(1, 8):
        reply = reply + pltpu.roll(by_slot[pl.ds(order, DEVICES, stride=8), :], order, 1)
    out_ref[...] = reply + pltpu.roll(by_slot[MAIN:, :], 8, 1)


def answer_kernel(got_ref, route_ref, all_ref, high_ref):
    within = route_ref[4:5, :]
    replies = jnp.transpose(got_ref[...])
    row = iota((24, ROWS), 0)
    best = None
    for role in range(ROLES):
        rest = replies[role * 24 : role * 24 + 24]
        pieces = []
        for _ in range(3):
            pieces.append(rest.astype(BF).astype(F32))
            rest = rest - pieces[-1]
        sender = route_ref[role : role + 1, :]
        lines = dot(jnp.concatenate(pieces, axis=0).astype(BF), (iota((DEVICES, ROWS), 0) == sender).astype(BF))
        lines = jnp.where(sender >= 0, lines[0:24] + lines[24:48] + lines[48:72], -1.0)
        best = lines if best is None else jnp.maximum(best, lines)
    all_ref[...] = jnp.sum(jnp.where(row == within, best, 0.0), axis=0, keepdims=True).reshape(ROWS)
    high_ref[...] = jnp.sum(jnp.where(row == within + 12, best, 0.0), axis=0, keepdims=True).reshape(ROWS)


def call(kernel, out, args, scratch=(), flops=0, name=None, left=(), grant=48):
    moved = sum(a.size * a.dtype.itemsize for a in args)
    many = isinstance(out, list)
    shapes = [jax.ShapeDtypeStruct(*o) for o in (out if many else [out])]
    out_specs = [pl.BlockSpec(memory_space=pltpu.VMEM)] * len(shapes)
    return pl.pallas_call(
        kernel,
        out_shape=shapes if many else shapes[0],
        in_specs=[pl.BlockSpec(memory_space=pl.ANY if i in left else pltpu.VMEM) for i in range(len(args))],
        out_specs=out_specs if many else out_specs[0],
        scratch_shapes=list(scratch),
        compiler_params=pltpu.CompilerParams(vmem_limit_bytes=grant * 1024 * 1024),
        cost_estimate=pl.CostEstimate(flops=flops, bytes_accessed=moved, transcendentals=0),
        name=name,
    )(*args)


def body(embeddings, cluster_id, cluster_rank, dest_slot):
    send, route = call(
        pack_kernel,
        [((MAIN, ROWS + 128), BF), ((8, ROWS), jnp.int32)],
        (embeddings, cluster_id, cluster_rank, dest_slot),
        (
            pltpu.VMEM((ROWS, ROWS), BF),
            pltpu.VMEM((ROWS,), jnp.int32),
            pltpu.VMEM((ROWS,), jnp.int32),
            pltpu.VMEM((ROWS,), jnp.int32),
            pltpu.VMEM((ROWS, ROWS), BF),
            pltpu.VMEM((MAIN, 128), F32),
            pltpu.SemaphoreType.DMA((6,)),
        ),
        name="pack",
        left=(0, 1, 2, 3),
        grant=60,
    )
    got = lax.all_to_all(send, AXES, split_axis=0, concat_axis=0, tiled=True)
    own, first = call(
        unpack_kernel,
        [((ROWS + META, ROWS), BF), ((EARLY + META, ROWS), BF)],
        (got,),
        (pltpu.VMEM((MAIN, 128), F32), pltpu.VMEM((MAIN, 128), F32)),
        name="unpack",
    )
    mate = lax.ppermute(own, AXES, shift(-1))
    key1 = lax.ppermute(first, AXES, shift(2))
    tail = lax.ppermute(own[HALF:], AXES, shift(-2))
    key2 = lax.ppermute(own[EARLY:ROWS], AXES, shift(2))
    tile = 2 * ROWS**3
    local = call(local_kernel, ((8, ROWS), F32), (own,), flops=tile, name="local")
    near = call(mate_kernel, ((8, ROWS), F32), (own, mate, local), flops=tile, name="mate")
    lines, tail_rows = call(
        far_first_kernel,
        [((8, ROWS), F32), ((24, SLOTS), F32)],
        (key1, own, mate, tail, near),
        flops=tile,
        name="far_first",
    )
    reply = call(
        far_second_kernel,
        ((DEVICES, 128), F32),
        (key2, own, mate, key1, lines, tail_rows),
        (pltpu.VMEM((SLOTS, 128), F32),),
        flops=tile,
        name="far_second",
    )
    answer = lax.all_to_all(reply.reshape(DEVICES, 1, 128), AXES, split_axis=0, concat_axis=0, tiled=True)
    return call(answer_kernel, [((ROWS,), F32)] * 2, (answer.reshape(DEVICES, 128), route), name="answer")


def solution(mesh):
    rows = P(AXES)
    return jax.shard_map(
        body,
        mesh=mesh,
        in_specs=(P(AXES, None), rows, rows, rows),
        out_specs=(rows, rows),
        check_vma=False,
    )
```

```python
import jax
import jax.numpy as jnp
from jax import lax
from jax.experimental import pallas as pl
from jax.experimental.pallas import tpu as pltpu
from jax.sharding import PartitionSpec as P

AXES = ("seg", "pair")
DEVICES = 128
PLACES = [
    (3, 0, 1, 1), (0, 0, 1, 1), (3, 1, 1, 1), (0, 1, 1, 1), (3, 2, 1, 1), (0, 2, 1, 1), (3, 2, 2, 1), (0, 2, 2, 1),
    (3, 3, 2, 1), (0, 3, 2, 1), (3, 0, 2, 1), (0, 0, 2, 1), (3, 1, 2, 1), (0, 1, 2, 1), (3, 1, 3, 1), (0, 1, 3, 1),
    (3, 2, 3, 1), (0, 2, 3, 1), (3, 3, 3, 1), (0, 3, 3, 1), (3, 0, 3, 1), (0, 0, 3, 1), (3, 0, 0, 1), (0, 0, 0, 1),
    (3, 1, 0, 1), (0, 1, 0, 1), (3, 2, 0, 1), (0, 2, 0, 1), (3, 3, 0, 1), (0, 3, 0, 1), (3, 3, 1, 1), (0, 3, 1, 1),
    (0, 3, 1, 0), (1, 3, 1, 0), (0, 2, 1, 0), (1, 2, 1, 0), (0, 2, 0, 0), (1, 2, 0, 0), (0, 2, 3, 0), (1, 2, 3, 0),
    (0, 2, 2, 0), (1, 2, 2, 0), (0, 1, 2, 0), (1, 1, 2, 0), (0, 1, 1, 0), (1, 1, 1, 0), (0, 1, 0, 0), (1, 1, 0, 0),
    (0, 1, 3, 0), (1, 1, 3, 0), (0, 0, 3, 0), (1, 0, 3, 0), (0, 0, 2, 0), (1, 0, 2, 0), (0, 0, 1, 0), (1, 0, 1, 0),
    (0, 0, 0, 0), (1, 0, 0, 0), (0, 3, 0, 0), (1, 3, 0, 0), (0, 3, 3, 0), (1, 3, 3, 0), (0, 3, 2, 0), (1, 3, 2, 0),
    (1, 3, 2, 1), (2, 3, 2, 1), (1, 2, 2, 1), (2, 2, 2, 1), (1, 2, 1, 1), (2, 2, 1, 1), (1, 1, 1, 1), (2, 1, 1, 1),
    (1, 0, 1, 1), (2, 0, 1, 1), (1, 3, 1, 1), (2, 3, 1, 1), (1, 3, 0, 1), (2, 3, 0, 1), (1, 2, 0, 1), (2, 2, 0, 1),
    (1, 1, 0, 1), (2, 1, 0, 1), (1, 0, 0, 1), (2, 0, 0, 1), (1, 0, 3, 1), (2, 0, 3, 1), (1, 3, 3, 1), (2, 3, 3, 1),
    (1, 2, 3, 1), (2, 2, 3, 1), (1, 1, 3, 1), (2, 1, 3, 1), (1, 1, 2, 1), (2, 1, 2, 1), (1, 0, 2, 1), (2, 0, 2, 1),
    (2, 0, 2, 0), (3, 0, 2, 0), (2, 0, 3, 0), (3, 0, 3, 0), (2, 1, 3, 0), (3, 1, 3, 0), (2, 1, 0, 0), (3, 1, 0, 0),
    (2, 1, 1, 0), (3, 1, 1, 0), (2, 1, 2, 0), (3, 1, 2, 0), (2, 2, 2, 0), (3, 2, 2, 0), (2, 2, 3, 0), (3, 2, 3, 0),
    (2, 2, 0, 0), (3, 2, 0, 0), (2, 2, 1, 0), (3, 2, 1, 0), (2, 3, 1, 0), (3, 3, 1, 0), (2, 3, 2, 0), (3, 3, 2, 0),
    (2, 3, 3, 0), (3, 3, 3, 0), (2, 3, 0, 0), (3, 3, 0, 0), (2, 0, 0, 0), (3, 0, 0, 0), (2, 0, 1, 0), (3, 0, 1, 0),
]
ROWS = 768
HALF = 384
EARLY = 512
CAP = 9
SLOTS = DEVICES * CAP
MAIN = DEVICES * 8
META = 16
ROLES = 4
BF = jnp.bfloat16
F32 = jnp.float32
NT = (((1,), (1,)), ((), ()))


HOLDERS = [((((x & 1) * 4 + z) * 4 + y) << 2) + ((x >> 1) << 1) + core for x, y, z, core in PLACES]


def device_of(block):
    return HOLDERS[block % DEVICES]


def shift(step):
    return [(device_of(block + step), device_of(block)) for block in range(DEVICES)]


def iota(shape, dim):
    return lax.broadcasted_iota(jnp.int32, shape, dim)


def dot(a, b):
    return jnp.dot(a, b, preferred_element_type=F32)


def dot_nt(a, b):
    return lax.dot_general(a, b, NT, preferred_element_type=F32)


def split_slot(slot):
    block = ((slot >> 8) * 171) >> 9
    return block, slot - block * ROWS


def device_table():
    row, lane = iota((8, DEVICES), 0), iota((8, DEVICES), 1)
    step = jnp.where(row == 1, 1, jnp.where(row == 2, -2, jnp.where(row == 3, 2, 0)))
    block = (lane + step) & (DEVICES - 1)
    found = jnp.zeros_like(block)
    for index, device in enumerate(HOLDERS):
        found = jnp.where(block == index, device, found)
    return found.astype(F32).astype(BF)


def pack_kernel(emb_ref, cid_ref, rank_ref, slot_ref, out_ref, route_ref, raw, slots, cids, ranks, unit, extra, sems):
    ids = ((slot_ref, slots), (cid_ref, cids), (rank_ref, ranks))
    small = [pltpu.make_async_copy(*pair, sems.at[3 + i]) for i, pair in enumerate(ids)]
    copies = [
        pltpu.make_async_copy(emb_ref.at[pl.ds(part * 256, 256)], raw.at[pl.ds(part * 256, 256)], sems.at[part])
        for part in range(3)
    ]
    for copy in small + copies:
        copy.start()
    table = device_table()
    earlier = (iota((ROWS, ROWS), 0) < iota((ROWS, ROWS), 1)).astype(BF)
    for copy in small:
        copy.wait()
    slot, cid, rank = (ref[...].reshape(1, ROWS) for _, ref in ids)
    block, local = split_slot(slot)
    to_block = (iota((DEVICES, ROWS), 0) == block).astype(BF)
    within = jnp.sum(to_block.astype(F32) * dot(to_block, earlier), axis=0, keepdims=True).astype(jnp.int32)
    senders = dot(table, to_block).astype(jnp.int32)
    row = iota((8, ROWS), 0)
    dropped = (row == 3) & (local < HALF)
    route_ref[...] = jnp.where(row == 4, within, jnp.where(dropped, -1, senders))
    device = senders[0:1]
    to_device = (iota((DEVICES, ROWS), 0) == device).astype(BF)
    flat = jnp.where(within < 8, device * 8 + within, -1)
    field = iota((DEVICES, ROWS), 0) >> 4
    meta = jnp.where(field == 0, (local >> 8) + 1, jnp.where(field == 1, local & 255, jnp.where(field == 2, cid + 1, 0)))
    meta = jnp.where(field == 3, rank >> 8, jnp.where(field == 4, rank & 255, meta))
    meta = jnp.where((iota((DEVICES, ROWS), 0) & 15) == within, meta, 0).astype(F32).astype(BF)
    extra[...] = jnp.zeros_like(extra)
    extra[pl.ds(6, DEVICES, stride=8), :] = dot_nt(to_device, meta)
    ninth = jnp.where(within == 8, to_device, jnp.zeros_like(to_device))
    for part, copy in enumerate(copies):
        copy.wait()
        values = raw[part * 256 : (part + 1) * 256, :].astype(F32)
        scaling = lax.rsqrt(jnp.sum(values * values, axis=1, keepdims=True) + 1e-06)
        unit[part * 256 : (part + 1) * 256, :] = (values * scaling).astype(BF)
    for start in range(0, MAIN, 256):
        pick = (iota((256, ROWS), 0) + start == flat).astype(BF)
        out_ref[start : start + 256, :ROWS] = dot(pick, unit[...]).astype(BF)
    ninth_rows = dot(ninth, unit[...])
    for part in range(6):
        extra[pl.ds(part, DEVICES, stride=8), :] = ninth_rows[:, part * 128 : (part + 1) * 128]
    out_ref[:, ROWS:] = extra[...].astype(BF)


def unpack_kernel(got_ref, out_ref, first_ref, extra, spread):
    extra[...] = got_ref[:, ROWS:].astype(F32)
    ninth_rows = jnp.concatenate([extra[pl.ds(part, DEVICES, stride=8), :] for part in range(6)], axis=1).astype(BF)
    meta = extra[pl.ds(6, DEVICES, stride=8), :]
    for order in range(8):
        spread[pl.ds(order, DEVICES, stride=8), :] = meta
    lane, row = iota((MAIN, 128), 1), iota((MAIN, 128), 0)
    main = jnp.where((lane & 15) == (row & 7), spread[...], 0.0).astype(BF)
    last = jnp.where((iota((DEVICES, 128), 1) & 15) == 8, meta, 0.0).astype(BF)
    fields = ((iota((META, 128), 1) >> 4) == iota((META, 128), 0)).astype(BF)
    by_slot = jnp.concatenate([dot_nt(fields, main), dot_nt(fields, last)], axis=1)
    slot = ((by_slot[0:1] - 1.0) * 256.0 + by_slot[1:2]).astype(jnp.int32)
    cols = by_slot.astype(BF)
    for start in range(0, ROWS, 256):
        pick = (iota((256, SLOTS), 0) + start == slot).astype(BF)
        rows = dot(pick[:, :MAIN], got_ref[:, :ROWS]) + dot(pick[:, MAIN:], ninth_rows)
        out_ref[start : start + 256, :] = rows.astype(BF)
        placed = dot_nt(cols, pick)
        kept = jnp.concatenate([placed[2:5], jnp.zeros((13, 256), F32)], axis=0)
        out_ref[ROWS:, start : start + 256] = kept.astype(BF)
    out_ref[ROWS + 8 : ROWS + 9, :] = cols[0:1, :ROWS]
    out_ref[ROWS + 9 : ROWS + 10, :] = cols[1:2, :ROWS]
    out_ref[ROWS + 10 : ROWS + 11, :HALF] = cols[0:1, ROWS:]
    out_ref[ROWS + 11 : ROWS + 12, :HALF] = cols[1:2, ROWS:]
    first_ref[:EARLY, :] = out_ref[:EARLY, :]
    first_ref[EARLY:, :] = out_ref[ROWS:, :]


def read_meta(block_ref, rows):
    meta = block_ref[rows:, :].astype(F32)
    cid, rank = meta[0:1], meta[1:2] * 256.0 + meta[2:3]
    high = jnp.concatenate([meta[8:9], meta[10:11, :HALF]], axis=1)
    low = jnp.concatenate([meta[9:10], meta[11:12, :HALF]], axis=1)
    slot = ((high - 1.0) * 256.0 + low).astype(jnp.int32)
    return cid, rank, slot


def columns(cid, rank):
    both = jnp.concatenate([cid, rank, jnp.zeros((6, cid.shape[1]), F32)], axis=0)
    turned = jnp.transpose(both)
    return turned[:, 0:1], turned[:, 1:2]


def local_kernel(own_ref, out_ref):
    own_cid, own_rank, _ = read_meta(own_ref, ROWS)
    cid, rank = columns(own_cid, own_rank)
    best_all = jnp.full((8, ROWS), -1.0, F32)
    best_high = jnp.full((8, ROWS), -1.0, F32)
    for start in range(0, ROWS, HALF):
        cosine = dot_nt(own_ref[start : start + HALF, :], own_ref[:ROWS, :])
        c, r = cid[start : start + HALF], rank[start : start + HALF]
        near = jnp.where((c == own_cid) & (r != own_rank), cosine, -1.0)
        high = jnp.where(r < own_rank, near, -1.0)
        best_all = jnp.maximum(best_all, jnp.max(near.reshape(HALF // 8, 8, ROWS), axis=0))
        best_high = jnp.maximum(best_high, jnp.max(high.reshape(HALF // 8, 8, ROWS), axis=0))
    out_ref[0:1, :] = jnp.max(best_all, axis=0, keepdims=True)
    out_ref[1:2, :] = jnp.max(best_high, axis=0, keepdims=True)
    out_ref[2:, :] = jnp.full((6, ROWS), -1.0, F32)


def meet(key, ids, others):
    cid, rank = columns(*ids)
    rows = key.shape[0]
    key_all = jnp.full((rows, 128), -1.0, F32)
    key_high, found = key_all, []
    for ref, count, other_cid, other_rank in others:
        near = HALF if count == HALF else rows
        wide_all, wide_high, row_all, row_high = against(key[:near], cid[:near], rank[:near], ref, count, other_cid, other_rank)
        if near < rows:
            rest = jnp.full((rows - near, 128), -1.0, F32)
            wide_all, wide_high = jnp.concatenate([wide_all, rest], axis=0), jnp.concatenate([wide_high, rest], axis=0)
        key_all, key_high = jnp.maximum(key_all, wide_all), jnp.maximum(key_high, wide_high)
        found.append((row_all, row_high))
    return tuple(jnp.max(jnp.transpose(wide), axis=0, keepdims=True) for wide in (key_all, key_high)), found


def ids_of(ids, start, stop):
    return ids[0][:, start:stop], ids[1][:, start:stop]


def both(left, right):
    return tuple(jnp.maximum(a, b) for a, b in zip(left, right))


def against(key, key_cid, key_rank, other_ref, count, other_cid, other_rank):
    cosine = dot_nt(key, other_ref[:count, :])
    near = jnp.where(key_cid == other_cid, cosine, -1.0)
    before = other_rank < key_rank
    high = jnp.where(before, near, -1.0)
    low = jnp.where(before, -1.0, near)
    wide_all, wide_high = near[:, :128], high[:, :128]
    for lane in range(128, count, 128):
        wide_all = jnp.maximum(wide_all, near[:, lane : lane + 128])
        wide_high = jnp.maximum(wide_high, high[:, lane : lane + 128])
    return wide_all, wide_high, jnp.max(near, axis=0, keepdims=True), jnp.max(low, axis=0, keepdims=True)


def reply_rows(value, slot):
    groups = value.shape[1] // 128
    rows = [value[:, g * 128 : (g + 1) * 128] for g in range(groups)]
    rest = jnp.concatenate(rows + [jnp.zeros((8 - groups, 128), F32)], axis=0)
    pieces = []
    for _ in range(3):
        pieces.append(rest.astype(BF))
        rest = rest - pieces[-1].astype(F32)
    pieces = jnp.concatenate(pieces, axis=0).astype(F32)
    return pieces, jnp.where((slot >> 7) == iota((8, SLOTS), 0), 1.0, 0.0)


def reply_to(value_all, value_high, slot):
    pieces_all, group = reply_rows(value_all, slot)
    pieces_high, _ = reply_rows(value_high, slot)
    pieces = jnp.concatenate([pieces_all, pieces_high], axis=0).astype(BF)
    pick = (iota((128, SLOTS), 0) == (slot & 127)).astype(BF)
    lines = dot(pieces, pick)
    row = iota((8, SLOTS), 0)
    out = []
    for which in range(2):
        line = lines[which * 24 : which * 24 + 8] + lines[which * 24 + 8 : which * 24 + 16] + lines[which * 24 + 16 : which * 24 + 24]
        found = jnp.sum(line * group, axis=0, keepdims=True)
        out.append(jnp.where(row == 4 * which, found, 0.0))
    return out + [jnp.zeros((8, SLOTS), F32)]


def mate_kernel(own_ref, mate_ref, local_ref, out_ref):
    own, mate = read_meta(own_ref, ROWS), read_meta(mate_ref, ROWS)
    mine, theirs = [], None
    for half in range(2):
        rows = own_ref[half * HALF : (half + 1) * HALF, :]
        keys, (found,) = meet(rows, ids_of(own, half * HALF, half * HALF + HALF), [(mate_ref, ROWS, *mate[:2])])
        mine.append(keys)
        theirs = found if theirs is None else both(theirs, found)
    mine = [jnp.concatenate([mine[0][i], mine[1][i]], axis=1) for i in range(2)]
    mine = both(mine, (local_ref[0:1, :], local_ref[1:2, :]))
    out_ref[...] = jnp.concatenate([*mine, *theirs, jnp.full((4, ROWS), -1.0, F32)], axis=0)


def far_first_kernel(key_ref, own_ref, mate_ref, tail_ref, near_ref, out_ref):
    own, mate = read_meta(own_ref, ROWS), read_meta(mate_ref, ROWS)
    key, tail = read_meta(key_ref, EARLY), read_meta(tail_ref, HALF)
    keys, (tails, mates, owns) = meet(
        key_ref[:EARLY, :],
        ids_of(key, 0, EARLY),
        [(tail_ref, HALF, *ids_of(tail, HALF, ROWS)), (mate_ref, ROWS, *mate[:2]), (own_ref, ROWS, *own[:2])],
    )
    owns = both(owns, (near_ref[0:1, :], near_ref[1:2, :]))
    mates = both(mates, (near_ref[2:3, :], near_ref[3:4, :]))
    lines = [jnp.concatenate([keys[i], jnp.zeros((1, ROWS - EARLY), F32)], axis=1) for i in range(2)]
    lines += [jnp.concatenate([tails[i], jnp.zeros((1, HALF), F32)], axis=1) for i in range(2)]
    out_ref[...] = jnp.concatenate([*owns, *mates, *lines], axis=0)


def far_second_kernel(key_ref, own_ref, mate_ref, early_ref, tail_ref, first_ref, out_ref, by_slot):
    own, mate = read_meta(own_ref, ROWS), read_meta(mate_ref, ROWS)
    key, tail = read_meta(early_ref, EARLY), read_meta(tail_ref, HALF)
    keys, (mates, owns) = meet(
        key_ref[...], ids_of(key, EARLY, ROWS), [(mate_ref, ROWS, *mate[:2]), (own_ref, ROWS, *own[:2])]
    )
    line = [first_ref[i : i + 1, :] for i in range(8)]
    owns, mates = both(owns, line[0:2]), both(mates, line[2:4])
    keys = [jnp.concatenate([line[4 + i][:, :EARLY], keys[i]], axis=1) for i in range(2)]
    tails = [line[6 + i][:, :HALF] for i in range(2)]
    rows = []
    for part, slot in ((owns, own[2]), (mates, mate[2]), (keys, key[2]), (tails, tail[2] - HALF)):
        rows += reply_to(*part, slot)
    rows.append(jnp.zeros((32, SLOTS), F32))
    by_slot[...] = jnp.transpose(jnp.concatenate(rows, axis=0))
    reply = by_slot[pl.ds(0, DEVICES, stride=8), :]
    for order in range(1, 8):
        reply = reply + pltpu.roll(by_slot[pl.ds(order, DEVICES, stride=8), :], order, 1)
    out_ref[...] = reply + pltpu.roll(by_slot[MAIN:, :], 8, 1)


def answer_kernel(got_ref, route_ref, all_ref, high_ref):
    within = route_ref[4:5, :]
    replies = jnp.transpose(got_ref[...])
    row = iota((24, ROWS), 0)
    best = None
    for role in range(ROLES):
        rest = replies[role * 24 : role * 24 + 24]
        pieces = []
        for _ in range(3):
            pieces.append(rest.astype(BF).astype(F32))
            rest = rest - pieces[-1]
        sender = route_ref[role : role + 1, :]
        lines = dot(jnp.concatenate(pieces, axis=0).astype(BF), (iota((DEVICES, ROWS), 0) == sender).astype(BF))
        lines = jnp.where(sender >= 0, lines[0:24] + lines[24:48] + lines[48:72], -1.0)
        best = lines if best is None else jnp.maximum(best, lines)
    all_ref[...] = jnp.sum(jnp.where(row == within, best, 0.0), axis=0, keepdims=True).reshape(ROWS)
    high_ref[...] = jnp.sum(jnp.where(row == within + 12, best, 0.0), axis=0, keepdims=True).reshape(ROWS)


def call(kernel, out, args, scratch=(), flops=0, name=None, left=(), grant=48):
    moved = sum(a.size * a.dtype.itemsize for a in args)
    many = isinstance(out, list)
    shapes = [jax.ShapeDtypeStruct(*o) for o in (out if many else [out])]
    out_specs = [pl.BlockSpec(memory_space=pltpu.VMEM)] * len(shapes)
    return pl.pallas_call(
        kernel,
        out_shape=shapes if many else shapes[0],
        in_specs=[pl.BlockSpec(memory_space=pl.ANY if i in left else pltpu.VMEM) for i in range(len(args))],
        out_specs=out_specs if many else out_specs[0],
        scratch_shapes=list(scratch),
        compiler_params=pltpu.CompilerParams(vmem_limit_bytes=grant * 1024 * 1024),
        cost_estimate=pl.CostEstimate(flops=flops, bytes_accessed=moved, transcendentals=0),
        name=name,
    )(*args)


def body(embeddings, cluster_id, cluster_rank, dest_slot):
    send, route = call(
        pack_kernel,
        [((MAIN, ROWS + 128), BF), ((8, ROWS), jnp.int32)],
        (embeddings, cluster_id, cluster_rank, dest_slot),
        (
            pltpu.VMEM((ROWS, ROWS), BF),
            pltpu.VMEM((ROWS,), jnp.int32),
            pltpu.VMEM((ROWS,), jnp.int32),
            pltpu.VMEM((ROWS,), jnp.int32),
            pltpu.VMEM((ROWS, ROWS), BF),
            pltpu.VMEM((MAIN, 128), F32),
            pltpu.SemaphoreType.DMA((6,)),
        ),
        name="pack",
        left=(0, 1, 2, 3),
        grant=60,
    )
    got = lax.all_to_all(send, AXES, split_axis=0, concat_axis=0, tiled=True)
    own, first = call(
        unpack_kernel,
        [((ROWS + META, ROWS), BF), ((EARLY + META, ROWS), BF)],
        (got,),
        (pltpu.VMEM((MAIN, 128), F32), pltpu.VMEM((MAIN, 128), F32)),
        name="unpack",
    )
    mate = lax.ppermute(own, AXES, shift(-1))
    key1 = lax.ppermute(first, AXES, shift(2))
    tail = lax.ppermute(own[HALF:], AXES, shift(-2))
    key2 = lax.ppermute(own[EARLY:ROWS], AXES, shift(2))
    tile = 2 * ROWS**3
    local = call(local_kernel, ((8, ROWS), F32), (own,), flops=tile, name="local")
    near = call(mate_kernel, ((8, ROWS), F32), (own, mate, local), flops=tile, name="mate")
    lines = call(far_first_kernel, ((8, ROWS), F32), (key1, own, mate, tail, near), flops=tile, name="far_first")
    reply = call(
        far_second_kernel,
        ((DEVICES, 128), F32),
        (key2, own, mate, key1, tail, lines),
        (pltpu.VMEM((SLOTS, 128), F32),),
        flops=tile,
        name="far_second",
    )
    answer = lax.all_to_all(reply.reshape(DEVICES, 1, 128), AXES, split_axis=0, concat_axis=0, tiled=True)
    return call(answer_kernel, [((ROWS,), F32)] * 2, (answer.reshape(DEVICES, 128), route), name="answer")


def solution(mesh):
    rows = P(AXES)
    return jax.shard_map(
        body,
        mesh=mesh,
        in_specs=(P(AXES, None), rows, rows, rows),
        out_specs=(rows, rows),
        check_vma=False,
    )
```

```python
import jax
import jax.numpy as jnp
from jax import lax
from jax.experimental import pallas as pl
from jax.experimental.pallas import tpu as pltpu
from jax.sharding import PartitionSpec as P

AXES = ("seg", "pair")
DEVICES = 128
PLACES = [
    (3, 0, 1, 1), (0, 0, 1, 1), (3, 1, 1, 1), (0, 1, 1, 1), (3, 2, 1, 1), (0, 2, 1, 1), (3, 2, 2, 1), (0, 2, 2, 1),
    (3, 3, 2, 1), (0, 3, 2, 1), (3, 0, 2, 1), (0, 0, 2, 1), (3, 1, 2, 1), (0, 1, 2, 1), (3, 1, 3, 1), (0, 1, 3, 1),
    (3, 2, 3, 1), (0, 2, 3, 1), (3, 3, 3, 1), (0, 3, 3, 1), (3, 0, 3, 1), (0, 0, 3, 1), (3, 0, 0, 1), (0, 0, 0, 1),
    (3, 1, 0, 1), (0, 1, 0, 1), (3, 2, 0, 1), (0, 2, 0, 1), (3, 3, 0, 1), (0, 3, 0, 1), (3, 3, 1, 1), (0, 3, 1, 1),
    (0, 3, 1, 0), (1, 3, 1, 0), (0, 2, 1, 0), (1, 2, 1, 0), (0, 2, 0, 0), (1, 2, 0, 0), (0, 2, 3, 0), (1, 2, 3, 0),
    (0, 2, 2, 0), (1, 2, 2, 0), (0, 1, 2, 0), (1, 1, 2, 0), (0, 1, 1, 0), (1, 1, 1, 0), (0, 1, 0, 0), (1, 1, 0, 0),
    (0, 1, 3, 0), (1, 1, 3, 0), (0, 0, 3, 0), (1, 0, 3, 0), (0, 0, 2, 0), (1, 0, 2, 0), (0, 0, 1, 0), (1, 0, 1, 0),
    (0, 0, 0, 0), (1, 0, 0, 0), (0, 3, 0, 0), (1, 3, 0, 0), (0, 3, 3, 0), (1, 3, 3, 0), (0, 3, 2, 0), (1, 3, 2, 0),
    (1, 3, 2, 1), (2, 3, 2, 1), (1, 2, 2, 1), (2, 2, 2, 1), (1, 2, 1, 1), (2, 2, 1, 1), (1, 1, 1, 1), (2, 1, 1, 1),
    (1, 0, 1, 1), (2, 0, 1, 1), (1, 3, 1, 1), (2, 3, 1, 1), (1, 3, 0, 1), (2, 3, 0, 1), (1, 2, 0, 1), (2, 2, 0, 1),
    (1, 1, 0, 1), (2, 1, 0, 1), (1, 0, 0, 1), (2, 0, 0, 1), (1, 0, 3, 1), (2, 0, 3, 1), (1, 3, 3, 1), (2, 3, 3, 1),
    (1, 2, 3, 1), (2, 2, 3, 1), (1, 1, 3, 1), (2, 1, 3, 1), (1, 1, 2, 1), (2, 1, 2, 1), (1, 0, 2, 1), (2, 0, 2, 1),
    (2, 0, 2, 0), (3, 0, 2, 0), (2, 0, 3, 0), (3, 0, 3, 0), (2, 1, 3, 0), (3, 1, 3, 0), (2, 1, 0, 0), (3, 1, 0, 0),
    (2, 1, 1, 0), (3, 1, 1, 0), (2, 1, 2, 0), (3, 1, 2, 0), (2, 2, 2, 0), (3, 2, 2, 0), (2, 2, 3, 0), (3, 2, 3, 0),
    (2, 2, 0, 0), (3, 2, 0, 0), (2, 2, 1, 0), (3, 2, 1, 0), (2, 3, 1, 0), (3, 3, 1, 0), (2, 3, 2, 0), (3, 3, 2, 0),
    (2, 3, 3, 0), (3, 3, 3, 0), (2, 3, 0, 0), (3, 3, 0, 0), (2, 0, 0, 0), (3, 0, 0, 0), (2, 0, 1, 0), (3, 0, 1, 0),
]
ROWS = 768
HALF = 384
EARLY = 512
CAP = 9
SLOTS = DEVICES * CAP
MAIN = DEVICES * 8
META = 16
ROLES = 4
BF = jnp.bfloat16
F32 = jnp.float32
NT = (((1,), (1,)), ((), ()))


HOLDERS = [((((x & 1) * 4 + z) * 4 + y) << 2) + ((x >> 1) << 1) + core for x, y, z, core in PLACES]


def device_of(block):
    return HOLDERS[block % DEVICES]


def shift(step):
    return [(device_of(block + step), device_of(block)) for block in range(DEVICES)]


def iota(shape, dim):
    return lax.broadcasted_iota(jnp.int32, shape, dim)


def dot(a, b):
    return jnp.dot(a, b, preferred_element_type=F32)


def dot_nt(a, b):
    return lax.dot_general(a, b, NT, preferred_element_type=F32)


def split_slot(slot):
    block = ((slot >> 8) * 171) >> 9
    return block, slot - block * ROWS


def device_table():
    row, lane = iota((8, DEVICES), 0), iota((8, DEVICES), 1)
    step = jnp.where(row == 1, 1, jnp.where(row == 2, -2, jnp.where(row == 3, 2, 0)))
    block = (lane + step) & (DEVICES - 1)
    found = jnp.zeros_like(block)
    for index, device in enumerate(HOLDERS):
        found = jnp.where(block == index, device, found)
    return found.astype(F32).astype(BF)


def pack_kernel(emb_ref, cid_ref, rank_ref, slot_ref, out_ref, route_ref, raw, slots, cids, ranks, unit, extra, sems):
    ids = ((slot_ref, slots), (cid_ref, cids), (rank_ref, ranks))
    small = [pltpu.make_async_copy(*pair, sems.at[6 + i]) for i, pair in enumerate(ids)]
    copies = [
        pltpu.make_async_copy(emb_ref.at[pl.ds(part * 128, 128)], raw.at[pl.ds(part * 128, 128)], sems.at[part])
        for part in range(6)
    ]
    for copy in small + copies:
        copy.start()
    table = device_table()
    earlier = (iota((ROWS, ROWS), 0) < iota((ROWS, ROWS), 1)).astype(BF)
    for copy in small:
        copy.wait()
    slot, cid, rank = (ref[...].reshape(1, ROWS) for _, ref in ids)
    block, local = split_slot(slot)
    to_block = (iota((DEVICES, ROWS), 0) == block).astype(BF)
    within = jnp.sum(to_block.astype(F32) * dot(to_block, earlier), axis=0, keepdims=True).astype(jnp.int32)
    senders = dot(table, to_block).astype(jnp.int32)
    row = iota((8, ROWS), 0)
    dropped = (row == 3) & (local < HALF)
    route_ref[...] = jnp.where(row == 4, within, jnp.where(dropped, -1, senders))
    device = senders[0:1]
    to_device = (iota((DEVICES, ROWS), 0) == device).astype(BF)
    flat = jnp.where(within < 8, device * 8 + within, -1)
    for part, copy in enumerate(copies):
        copy.wait()
        values = raw[part * 128 : (part + 1) * 128, :].astype(F32)
        scaling = lax.rsqrt(jnp.sum(values * values, axis=1, keepdims=True) + 1e-06)
        unit[part * 128 : (part + 1) * 128, :] = (values * scaling).astype(BF)
    for start in range(0, MAIN, 256):
        pick = (iota((256, ROWS), 0) + start == flat).astype(BF)
        out_ref[start : start + 256, :ROWS] = dot(pick, unit[...]).astype(BF)
    ninth = jnp.where(within == 8, to_device, jnp.zeros_like(to_device))
    ninth_rows = dot(ninth, unit[...])
    field = iota((DEVICES, ROWS), 0) >> 4
    meta = jnp.where(field == 0, (local >> 8) + 1, jnp.where(field == 1, local & 255, jnp.where(field == 2, cid + 1, 0)))
    meta = jnp.where(field == 3, rank >> 8, jnp.where(field == 4, rank & 255, meta))
    meta = jnp.where((iota((DEVICES, ROWS), 0) & 15) == within, meta, 0).astype(F32).astype(BF)
    extra[...] = jnp.zeros_like(extra)
    for part in range(6):
        extra[pl.ds(part, DEVICES, stride=8), :] = ninth_rows[:, part * 128 : (part + 1) * 128]
    extra[pl.ds(6, DEVICES, stride=8), :] = dot_nt(to_device, meta)
    out_ref[:, ROWS:] = extra[...].astype(BF)


def unpack_kernel(got_ref, out_ref, first_ref, extra, spread):
    extra[...] = got_ref[:, ROWS:].astype(F32)
    ninth_rows = jnp.concatenate([extra[pl.ds(part, DEVICES, stride=8), :] for part in range(6)], axis=1).astype(BF)
    meta = extra[pl.ds(6, DEVICES, stride=8), :]
    for order in range(8):
        spread[pl.ds(order, DEVICES, stride=8), :] = meta
    lane, row = iota((MAIN, 128), 1), iota((MAIN, 128), 0)
    main = jnp.where((lane & 15) == (row & 7), spread[...], 0.0).astype(BF)
    last = jnp.where((iota((DEVICES, 128), 1) & 15) == 8, meta, 0.0).astype(BF)
    fields = ((iota((META, 128), 1) >> 4) == iota((META, 128), 0)).astype(BF)
    by_slot = jnp.concatenate([dot_nt(fields, main), dot_nt(fields, last)], axis=1)
    slot = ((by_slot[0:1] - 1.0) * 256.0 + by_slot[1:2]).astype(jnp.int32)
    cols = by_slot.astype(BF)
    for start in range(0, ROWS, 256):
        pick = (iota((256, SLOTS), 0) + start == slot).astype(BF)
        rows = dot(pick[:, :MAIN], got_ref[:, :ROWS]) + dot(pick[:, MAIN:], ninth_rows)
        out_ref[start : start + 256, :] = rows.astype(BF)
        placed = dot_nt(cols, pick)
        kept = jnp.concatenate([placed[2:5], jnp.zeros((13, 256), F32)], axis=0)
        out_ref[ROWS:, start : start + 256] = kept.astype(BF)
    out_ref[ROWS + 8 : ROWS + 9, :] = cols[0:1, :ROWS]
    out_ref[ROWS + 9 : ROWS + 10, :] = cols[1:2, :ROWS]
    out_ref[ROWS + 10 : ROWS + 11, :HALF] = cols[0:1, ROWS:]
    out_ref[ROWS + 11 : ROWS + 12, :HALF] = cols[1:2, ROWS:]
    first_ref[:EARLY, :] = out_ref[:EARLY, :]
    first_ref[EARLY:, :] = out_ref[ROWS:, :]


def read_meta(block_ref, rows):
    meta = block_ref[rows:, :].astype(F32)
    cid, rank = meta[0:1], meta[1:2] * 256.0 + meta[2:3]
    high = jnp.concatenate([meta[8:9], meta[10:11, :HALF]], axis=1)
    low = jnp.concatenate([meta[9:10], meta[11:12, :HALF]], axis=1)
    slot = ((high - 1.0) * 256.0 + low).astype(jnp.int32)
    return cid, rank, slot


def columns(cid, rank):
    both = jnp.concatenate([cid, rank, jnp.zeros((6, cid.shape[1]), F32)], axis=0)
    turned = jnp.transpose(both)
    return turned[:, 0:1], turned[:, 1:2]


def local_kernel(own_ref, out_ref):
    own_cid, own_rank, _ = read_meta(own_ref, ROWS)
    cid, rank = columns(own_cid, own_rank)
    best_all = jnp.full((8, ROWS), -1.0, F32)
    best_high = jnp.full((8, ROWS), -1.0, F32)
    for start in range(0, ROWS, HALF):
        cosine = dot_nt(own_ref[start : start + HALF, :], own_ref[:ROWS, :])
        c, r = cid[start : start + HALF], rank[start : start + HALF]
        near = jnp.where((c == own_cid) & (r != own_rank), cosine, -1.0)
        high = jnp.where(r < own_rank, near, -1.0)
        best_all = jnp.maximum(best_all, jnp.max(near.reshape(HALF // 8, 8, ROWS), axis=0))
        best_high = jnp.maximum(best_high, jnp.max(high.reshape(HALF // 8, 8, ROWS), axis=0))
    out_ref[0:1, :] = jnp.max(best_all, axis=0, keepdims=True)
    out_ref[1:2, :] = jnp.max(best_high, axis=0, keepdims=True)
    out_ref[2:, :] = jnp.full((6, ROWS), -1.0, F32)


def meet(key, ids, others):
    cid, rank = columns(*ids)
    rows = key.shape[0]
    key_all = jnp.full((rows, 128), -1.0, F32)
    key_high, found = key_all, []
    for ref, count, other_cid, other_rank in others:
        near = HALF if count == HALF else rows
        wide_all, wide_high, row_all, row_high = against(key[:near], cid[:near], rank[:near], ref, count, other_cid, other_rank)
        if near < rows:
            rest = jnp.full((rows - near, 128), -1.0, F32)
            wide_all, wide_high = jnp.concatenate([wide_all, rest], axis=0), jnp.concatenate([wide_high, rest], axis=0)
        key_all, key_high = jnp.maximum(key_all, wide_all), jnp.maximum(key_high, wide_high)
        found.append((row_all, row_high))
    return tuple(jnp.max(jnp.transpose(wide), axis=0, keepdims=True) for wide in (key_all, key_high)), found


def ids_of(ids, start, stop):
    return ids[0][:, start:stop], ids[1][:, start:stop]


def both(left, right):
    return tuple(jnp.maximum(a, b) for a, b in zip(left, right))


def against(key, key_cid, key_rank, other_ref, count, other_cid, other_rank):
    cosine = dot_nt(key, other_ref[:count, :])
    near = jnp.where(key_cid == other_cid, cosine, -1.0)
    before = other_rank < key_rank
    high = jnp.where(before, near, -1.0)
    low = jnp.where(before, -1.0, near)
    wide_all, wide_high = near[:, :128], high[:, :128]
    for lane in range(128, count, 128):
        wide_all = jnp.maximum(wide_all, near[:, lane : lane + 128])
        wide_high = jnp.maximum(wide_high, high[:, lane : lane + 128])
    return wide_all, wide_high, jnp.max(near, axis=0, keepdims=True), jnp.max(low, axis=0, keepdims=True)


def reply_rows(value, slot):
    groups = value.shape[1] // 128
    rows = [value[:, g * 128 : (g + 1) * 128] for g in range(groups)]
    rest = jnp.concatenate(rows + [jnp.zeros((8 - groups, 128), F32)], axis=0)
    pieces = []
    for _ in range(3):
        pieces.append(rest.astype(BF))
        rest = rest - pieces[-1].astype(F32)
    pieces = jnp.concatenate(pieces, axis=0).astype(F32)
    return pieces, jnp.where((slot >> 7) == iota((8, SLOTS), 0), 1.0, 0.0)


def reply_to(value_all, value_high, slot):
    pieces_all, group = reply_rows(value_all, slot)
    pieces_high, _ = reply_rows(value_high, slot)
    pieces = jnp.concatenate([pieces_all, pieces_high], axis=0).astype(BF)
    pick = (iota((128, SLOTS), 0) == (slot & 127)).astype(BF)
    lines = dot(pieces, pick)
    row = iota((8, SLOTS), 0)
    out = []
    for which in range(2):
        line = lines[which * 24 : which * 24 + 8] + lines[which * 24 + 8 : which * 24 + 16] + lines[which * 24 + 16 : which * 24 + 24]
        found = jnp.sum(line * group, axis=0, keepdims=True)
        out.append(jnp.where(row == 4 * which, found, 0.0))
    return out + [jnp.zeros((8, SLOTS), F32)]


def mate_kernel(own_ref, mate_ref, local_ref, out_ref):
    own, mate = read_meta(own_ref, ROWS), read_meta(mate_ref, ROWS)
    mine, theirs = [], None
    for half in range(2):
        rows = own_ref[half * HALF : (half + 1) * HALF, :]
        keys, (found,) = meet(rows, ids_of(own, half * HALF, half * HALF + HALF), [(mate_ref, ROWS, *mate[:2])])
        mine.append(keys)
        theirs = found if theirs is None else both(theirs, found)
    mine = [jnp.concatenate([mine[0][i], mine[1][i]], axis=1) for i in range(2)]
    mine = both(mine, (local_ref[0:1, :], local_ref[1:2, :]))
    out_ref[...] = jnp.concatenate([*mine, *theirs, jnp.full((4, ROWS), -1.0, F32)], axis=0)


def far_first_kernel(key_ref, own_ref, mate_ref, tail_ref, near_ref, out_ref):
    own, mate = read_meta(own_ref, ROWS), read_meta(mate_ref, ROWS)
    key, tail = read_meta(key_ref, EARLY), read_meta(tail_ref, HALF)
    keys, (tails, mates, owns) = meet(
        key_ref[:EARLY, :],
        ids_of(key, 0, EARLY),
        [(tail_ref, HALF, *ids_of(tail, HALF, ROWS)), (mate_ref, ROWS, *mate[:2]), (own_ref, ROWS, *own[:2])],
    )
    owns = both(owns, (near_ref[0:1, :], near_ref[1:2, :]))
    mates = both(mates, (near_ref[2:3, :], near_ref[3:4, :]))
    lines = [jnp.concatenate([keys[i], jnp.zeros((1, ROWS - EARLY), F32)], axis=1) for i in range(2)]
    lines += [jnp.concatenate([tails[i], jnp.zeros((1, HALF), F32)], axis=1) for i in range(2)]
    out_ref[...] = jnp.concatenate([*owns, *mates, *lines], axis=0)


def far_second_kernel(key_ref, own_ref, mate_ref, early_ref, tail_ref, first_ref, out_ref, by_slot):
    own, mate = read_meta(own_ref, ROWS), read_meta(mate_ref, ROWS)
    key, tail = read_meta(early_ref, EARLY), read_meta(tail_ref, HALF)
    keys, (mates, owns) = meet(
        key_ref[...], ids_of(key, EARLY, ROWS), [(mate_ref, ROWS, *mate[:2]), (own_ref, ROWS, *own[:2])]
    )
    line = [first_ref[i : i + 1, :] for i in range(8)]
    owns, mates = both(owns, line[0:2]), both(mates, line[2:4])
    keys = [jnp.concatenate([line[4 + i][:, :EARLY], keys[i]], axis=1) for i in range(2)]
    tails = [line[6 + i][:, :HALF] for i in range(2)]
    rows = []
    for part, slot in ((owns, own[2]), (mates, mate[2]), (keys, key[2]), (tails, tail[2] - HALF)):
        rows += reply_to(*part, slot)
    rows.append(jnp.zeros((32, SLOTS), F32))
    by_slot[...] = jnp.transpose(jnp.concatenate(rows, axis=0))
    reply = by_slot[pl.ds(0, DEVICES, stride=8), :]
    for order in range(1, 8):
        reply = reply + pltpu.roll(by_slot[pl.ds(order, DEVICES, stride=8), :], order, 1)
    out_ref[...] = reply + pltpu.roll(by_slot[MAIN:, :], 8, 1)


def answer_kernel(got_ref, route_ref, all_ref, high_ref):
    within = route_ref[4:5, :]
    replies = jnp.transpose(got_ref[...])
    row = iota((24, ROWS), 0)
    best = None
    for role in range(ROLES):
        rest = replies[role * 24 : role * 24 + 24]
        pieces = []
        for _ in range(3):
            pieces.append(rest.astype(BF).astype(F32))
            rest = rest - pieces[-1]
        sender = route_ref[role : role + 1, :]
        lines = dot(jnp.concatenate(pieces, axis=0).astype(BF), (iota((DEVICES, ROWS), 0) == sender).astype(BF))
        lines = jnp.where(sender >= 0, lines[0:24] + lines[24:48] + lines[48:72], -1.0)
        best = lines if best is None else jnp.maximum(best, lines)
    all_ref[...] = jnp.sum(jnp.where(row == within, best, 0.0), axis=0, keepdims=True).reshape(ROWS)
    high_ref[...] = jnp.sum(jnp.where(row == within + 12, best, 0.0), axis=0, keepdims=True).reshape(ROWS)


def call(kernel, out, args, scratch=(), flops=0, name=None, left=(), grant=48):
    moved = sum(a.size * a.dtype.itemsize for a in args)
    many = isinstance(out, list)
    shapes = [jax.ShapeDtypeStruct(*o) for o in (out if many else [out])]
    out_specs = [pl.BlockSpec(memory_space=pltpu.VMEM)] * len(shapes)
    return pl.pallas_call(
        kernel,
        out_shape=shapes if many else shapes[0],
        in_specs=[pl.BlockSpec(memory_space=pl.ANY if i in left else pltpu.VMEM) for i in range(len(args))],
        out_specs=out_specs if many else out_specs[0],
        scratch_shapes=list(scratch),
        compiler_params=pltpu.CompilerParams(vmem_limit_bytes=grant * 1024 * 1024),
        cost_estimate=pl.CostEstimate(flops=flops, bytes_accessed=moved, transcendentals=0),
        name=name,
    )(*args)


def body(embeddings, cluster_id, cluster_rank, dest_slot):
    send, route = call(
        pack_kernel,
        [((MAIN, ROWS + 128), BF), ((8, ROWS), jnp.int32)],
        (embeddings, cluster_id, cluster_rank, dest_slot),
        (
            pltpu.VMEM((ROWS, ROWS), BF),
            pltpu.VMEM((ROWS,), jnp.int32),
            pltpu.VMEM((ROWS,), jnp.int32),
            pltpu.VMEM((ROWS,), jnp.int32),
            pltpu.VMEM((ROWS, ROWS), BF),
            pltpu.VMEM((MAIN, 128), F32),
            pltpu.SemaphoreType.DMA((9,)),
        ),
        name="pack",
        left=(0, 1, 2, 3),
        grant=60,
    )
    got = lax.all_to_all(send, AXES, split_axis=0, concat_axis=0, tiled=True)
    own, first = call(
        unpack_kernel,
        [((ROWS + META, ROWS), BF), ((EARLY + META, ROWS), BF)],
        (got,),
        (pltpu.VMEM((MAIN, 128), F32), pltpu.VMEM((MAIN, 128), F32)),
        name="unpack",
    )
    mate = lax.ppermute(own, AXES, shift(-1))
    key1 = lax.ppermute(first, AXES, shift(2))
    tail = lax.ppermute(own[HALF:], AXES, shift(-2))
    key2 = lax.ppermute(own[EARLY:ROWS], AXES, shift(2))
    tile = 2 * ROWS**3
    local = call(local_kernel, ((8, ROWS), F32), (own,), flops=tile, name="local")
    near = call(mate_kernel, ((8, ROWS), F32), (own, mate, local), flops=tile, name="mate")
    lines = call(far_first_kernel, ((8, ROWS), F32), (key1, own, mate, tail, near), flops=tile, name="far_first")
    reply = call(
        far_second_kernel,
        ((DEVICES, 128), F32),
        (key2, own, mate, key1, tail, lines),
        (pltpu.VMEM((SLOTS, 128), F32),),
        flops=tile,
        name="far_second",
    )
    answer = lax.all_to_all(reply.reshape(DEVICES, 1, 128), AXES, split_axis=0, concat_axis=0, tiled=True)
    return call(answer_kernel, [((ROWS,), F32)] * 2, (answer.reshape(DEVICES, 128), route), name="answer")


def solution(mesh):
    rows = P(AXES)
    return jax.shard_map(
        body,
        mesh=mesh,
        in_specs=(P(AXES, None), rows, rows, rows),
        out_specs=(rows, rows),
        check_vma=False,
    )
```

```python
import jax
import jax.numpy as jnp
from jax import lax
from jax.experimental import pallas as pl
from jax.experimental.pallas import tpu as pltpu
from jax.sharding import PartitionSpec as P

AXES = ("seg", "pair")
DEVICES = 128
PLACES = [
    (3, 0, 1, 0), (2, 0, 1, 0), (3, 0, 0, 0), (2, 0, 0, 0), (3, 3, 0, 0), (2, 3, 0, 0), (3, 3, 3, 0), (2, 3, 3, 0),
    (3, 3, 2, 0), (2, 3, 2, 0), (3, 3, 1, 0), (2, 3, 1, 0), (3, 2, 1, 0), (2, 2, 1, 0), (3, 2, 0, 0), (2, 2, 0, 0),
    (3, 2, 3, 0), (2, 2, 3, 0), (3, 2, 2, 0), (2, 2, 2, 0), (3, 1, 2, 0), (2, 1, 2, 0), (3, 1, 1, 0), (2, 1, 1, 0),
    (3, 1, 0, 0), (2, 1, 0, 0), (3, 1, 3, 0), (2, 1, 3, 0), (3, 0, 3, 0), (2, 0, 3, 0), (3, 0, 2, 0), (2, 0, 2, 0),
    (2, 0, 2, 1), (1, 0, 2, 1), (2, 1, 2, 1), (1, 1, 2, 1), (2, 1, 3, 1), (1, 1, 3, 1), (2, 2, 3, 1), (1, 2, 3, 1),
    (2, 3, 3, 1), (1, 3, 3, 1), (2, 0, 3, 1), (1, 0, 3, 1), (2, 0, 0, 1), (1, 0, 0, 1), (2, 1, 0, 1), (1, 1, 0, 1),
    (2, 2, 0, 1), (1, 2, 0, 1), (2, 3, 0, 1), (1, 3, 0, 1), (2, 3, 1, 1), (1, 3, 1, 1), (2, 0, 1, 1), (1, 0, 1, 1),
    (2, 1, 1, 1), (1, 1, 1, 1), (2, 2, 1, 1), (1, 2, 1, 1), (2, 2, 2, 1), (1, 2, 2, 1), (2, 3, 2, 1), (1, 3, 2, 1),
    (1, 3, 2, 0), (0, 3, 2, 0), (1, 3, 3, 0), (0, 3, 3, 0), (1, 3, 0, 0), (0, 3, 0, 0), (1, 0, 0, 0), (0, 0, 0, 0),
    (1, 0, 1, 0), (0, 0, 1, 0), (1, 0, 2, 0), (0, 0, 2, 0), (1, 0, 3, 0), (0, 0, 3, 0), (1, 1, 3, 0), (0, 1, 3, 0),
    (1, 1, 0, 0), (0, 1, 0, 0), (1, 1, 1, 0), (0, 1, 1, 0), (1, 1, 2, 0), (0, 1, 2, 0), (1, 2, 2, 0), (0, 2, 2, 0),
    (1, 2, 3, 0), (0, 2, 3, 0), (1, 2, 0, 0), (0, 2, 0, 0), (1, 2, 1, 0), (0, 2, 1, 0), (1, 3, 1, 0), (0, 3, 1, 0),
    (0, 3, 1, 1), (3, 3, 1, 1), (0, 3, 0, 1), (3, 3, 0, 1), (0, 2, 0, 1), (3, 2, 0, 1), (0, 1, 0, 1), (3, 1, 0, 1),
    (0, 0, 0, 1), (3, 0, 0, 1), (0, 0, 3, 1), (3, 0, 3, 1), (0, 3, 3, 1), (3, 3, 3, 1), (0, 2, 3, 1), (3, 2, 3, 1),
    (0, 1, 3, 1), (3, 1, 3, 1), (0, 1, 2, 1), (3, 1, 2, 1), (0, 0, 2, 1), (3, 0, 2, 1), (0, 3, 2, 1), (3, 3, 2, 1),
    (0, 2, 2, 1), (3, 2, 2, 1), (0, 2, 1, 1), (3, 2, 1, 1), (0, 1, 1, 1), (3, 1, 1, 1), (0, 0, 1, 1), (3, 0, 1, 1),
]
ROWS = 768
HALF = 384
EARLY = 512
CAP = 9
SLOTS = DEVICES * CAP
MAIN = DEVICES * 8
META = 16
ROLES = 4
BF = jnp.bfloat16
F32 = jnp.float32
NT = (((1,), (1,)), ((), ()))


HOLDERS = [((((x & 1) * 4 + z) * 4 + y) << 2) + ((x >> 1) << 1) + core for x, y, z, core in PLACES]


def device_of(block):
    return HOLDERS[block % DEVICES]


def shift(step):
    return [(device_of(block + step), device_of(block)) for block in range(DEVICES)]


def iota(shape, dim):
    return lax.broadcasted_iota(jnp.int32, shape, dim)


def dot(a, b):
    return jnp.dot(a, b, preferred_element_type=F32)


def dot_nt(a, b):
    return lax.dot_general(a, b, NT, preferred_element_type=F32)


def split_slot(slot):
    block = ((slot >> 8) * 171) >> 9
    return block, slot - block * ROWS


def device_table():
    row, lane = iota((8, DEVICES), 0), iota((8, DEVICES), 1)
    step = jnp.where(row == 1, 1, jnp.where(row == 2, -2, jnp.where(row == 3, 2, 0)))
    block = (lane + step) & (DEVICES - 1)
    found = jnp.zeros_like(block)
    for index, device in enumerate(HOLDERS):
        found = jnp.where(block == index, device, found)
    return found.astype(F32).astype(BF)


def pack_kernel(emb_ref, cid_ref, rank_ref, slot_ref, out_ref, route_ref, raw, slots, cids, ranks, unit, extra, sems):
    ids = ((slot_ref, slots), (cid_ref, cids), (rank_ref, ranks))
    small = [pltpu.make_async_copy(*pair, sems.at[3 + i]) for i, pair in enumerate(ids)]
    copies = [
        pltpu.make_async_copy(emb_ref.at[pl.ds(part * 256, 256)], raw.at[pl.ds(part * 256, 256)], sems.at[part])
        for part in range(3)
    ]
    for copy in small + copies:
        copy.start()
    table = device_table()
    earlier = (iota((ROWS, ROWS), 0) < iota((ROWS, ROWS), 1)).astype(BF)
    for copy in small:
        copy.wait()
    slot, cid, rank = (ref[...].reshape(1, ROWS) for _, ref in ids)
    block, local = split_slot(slot)
    to_block = (iota((DEVICES, ROWS), 0) == block).astype(BF)
    within = jnp.sum(to_block.astype(F32) * dot(to_block, earlier), axis=0, keepdims=True).astype(jnp.int32)
    senders = dot(table, to_block).astype(jnp.int32)
    row = iota((8, ROWS), 0)
    dropped = (row == 3) & (local < HALF)
    route_ref[...] = jnp.where(row == 4, within, jnp.where(dropped, -1, senders))
    device = senders[0:1]
    to_device = (iota((DEVICES, ROWS), 0) == device).astype(BF)
    flat = jnp.where(within < 8, device * 8 + within, -1)
    for part, copy in enumerate(copies):
        copy.wait()
        values = raw[part * 256 : (part + 1) * 256, :].astype(F32)
        scaling = lax.rsqrt(jnp.sum(values * values, axis=1, keepdims=True) + 1e-06)
        unit[part * 256 : (part + 1) * 256, :] = (values * scaling).astype(BF)
    for start in range(0, MAIN, 256):
        pick = (iota((256, ROWS), 0) + start == flat).astype(BF)
        out_ref[start : start + 256, :ROWS] = dot(pick, unit[...]).astype(BF)
    ninth = jnp.where(within == 8, to_device, jnp.zeros_like(to_device))
    ninth_rows = dot(ninth, unit[...])
    field = iota((DEVICES, ROWS), 0) >> 4
    meta = jnp.where(field == 0, (local >> 8) + 1, jnp.where(field == 1, local & 255, jnp.where(field == 2, cid + 1, 0)))
    meta = jnp.where(field == 3, rank >> 8, jnp.where(field == 4, rank & 255, meta))
    meta = jnp.where((iota((DEVICES, ROWS), 0) & 15) == within, meta, 0).astype(F32).astype(BF)
    extra[...] = jnp.zeros_like(extra)
    for part in range(6):
        extra[pl.ds(part, DEVICES, stride=8), :] = ninth_rows[:, part * 128 : (part + 1) * 128]
    extra[pl.ds(6, DEVICES, stride=8), :] = dot_nt(to_device, meta)
    out_ref[:, ROWS:] = extra[...].astype(BF)


def unpack_kernel(got_ref, out_ref, first_ref, extra, spread):
    extra[...] = got_ref[:, ROWS:].astype(F32)
    ninth_rows = jnp.concatenate([extra[pl.ds(part, DEVICES, stride=8), :] for part in range(6)], axis=1).astype(BF)
    meta = extra[pl.ds(6, DEVICES, stride=8), :]
    for order in range(8):
        spread[pl.ds(order, DEVICES, stride=8), :] = meta
    lane, row = iota((MAIN, 128), 1), iota((MAIN, 128), 0)
    main = jnp.where((lane & 15) == (row & 7), spread[...], 0.0).astype(BF)
    last = jnp.where((iota((DEVICES, 128), 1) & 15) == 8, meta, 0.0).astype(BF)
    fields = ((iota((META, 128), 1) >> 4) == iota((META, 128), 0)).astype(BF)
    by_slot = jnp.concatenate([dot_nt(fields, main), dot_nt(fields, last)], axis=1)
    slot = ((by_slot[0:1] - 1.0) * 256.0 + by_slot[1:2]).astype(jnp.int32)
    cols = by_slot.astype(BF)
    for start in range(0, ROWS, 256):
        pick = (iota((256, SLOTS), 0) + start == slot).astype(BF)
        rows = dot(pick[:, :MAIN], got_ref[:, :ROWS]) + dot(pick[:, MAIN:], ninth_rows)
        out_ref[start : start + 256, :] = rows.astype(BF)
        placed = dot_nt(cols, pick)
        kept = jnp.concatenate([placed[2:5], jnp.zeros((13, 256), F32)], axis=0)
        out_ref[ROWS:, start : start + 256] = kept.astype(BF)
    out_ref[ROWS + 8 : ROWS + 9, :] = cols[0:1, :ROWS]
    out_ref[ROWS + 9 : ROWS + 10, :] = cols[1:2, :ROWS]
    out_ref[ROWS + 10 : ROWS + 11, :HALF] = cols[0:1, ROWS:]
    out_ref[ROWS + 11 : ROWS + 12, :HALF] = cols[1:2, ROWS:]
    first_ref[:EARLY, :] = out_ref[:EARLY, :]
    first_ref[EARLY:, :] = out_ref[ROWS:, :]


def read_meta(block_ref, rows):
    meta = block_ref[rows:, :].astype(F32)
    cid, rank = meta[0:1], meta[1:2] * 256.0 + meta[2:3]
    high = jnp.concatenate([meta[8:9], meta[10:11, :HALF]], axis=1)
    low = jnp.concatenate([meta[9:10], meta[11:12, :HALF]], axis=1)
    slot = ((high - 1.0) * 256.0 + low).astype(jnp.int32)
    return cid, rank, slot


def columns(cid, rank):
    both = jnp.concatenate([cid, rank, jnp.zeros((6, cid.shape[1]), F32)], axis=0)
    turned = jnp.transpose(both)
    return turned[:, 0:1], turned[:, 1:2]


def local_kernel(own_ref, out_ref):
    own_cid, own_rank, _ = read_meta(own_ref, ROWS)
    cid, rank = columns(own_cid, own_rank)
    best_all = jnp.full((8, ROWS), -1.0, F32)
    best_high = jnp.full((8, ROWS), -1.0, F32)
    for start in range(0, ROWS, HALF):
        cosine = dot_nt(own_ref[start : start + HALF, :], own_ref[:ROWS, :])
        c, r = cid[start : start + HALF], rank[start : start + HALF]
        near = jnp.where((c == own_cid) & (r != own_rank), cosine, -1.0)
        high = jnp.where(r < own_rank, near, -1.0)
        best_all = jnp.maximum(best_all, jnp.max(near.reshape(HALF // 8, 8, ROWS), axis=0))
        best_high = jnp.maximum(best_high, jnp.max(high.reshape(HALF // 8, 8, ROWS), axis=0))
    out_ref[0:1, :] = jnp.max(best_all, axis=0, keepdims=True)
    out_ref[1:2, :] = jnp.max(best_high, axis=0, keepdims=True)
    out_ref[2:, :] = jnp.full((6, ROWS), -1.0, F32)


def meet(key, ids, others):
    cid, rank = columns(*ids)
    rows = key.shape[0]
    key_all = jnp.full((rows, 128), -1.0, F32)
    key_high, found = key_all, []
    for ref, count, other_cid, other_rank in others:
        near = HALF if count == HALF else rows
        wide_all, wide_high, row_all, row_high = against(key[:near], cid[:near], rank[:near], ref, count, other_cid, other_rank)
        if near < rows:
            rest = jnp.full((rows - near, 128), -1.0, F32)
            wide_all, wide_high = jnp.concatenate([wide_all, rest], axis=0), jnp.concatenate([wide_high, rest], axis=0)
        key_all, key_high = jnp.maximum(key_all, wide_all), jnp.maximum(key_high, wide_high)
        found.append((row_all, row_high))
    return tuple(jnp.max(jnp.transpose(wide), axis=0, keepdims=True) for wide in (key_all, key_high)), found


def ids_of(ids, start, stop):
    return ids[0][:, start:stop], ids[1][:, start:stop]


def both(left, right):
    return tuple(jnp.maximum(a, b) for a, b in zip(left, right))


def against(key, key_cid, key_rank, other_ref, count, other_cid, other_rank):
    cosine = dot_nt(key, other_ref[:count, :])
    near = jnp.where(key_cid == other_cid, cosine, -1.0)
    before = other_rank < key_rank
    high = jnp.where(before, near, -1.0)
    low = jnp.where(before, -1.0, near)
    wide_all, wide_high = near[:, :128], high[:, :128]
    for lane in range(128, count, 128):
        wide_all = jnp.maximum(wide_all, near[:, lane : lane + 128])
        wide_high = jnp.maximum(wide_high, high[:, lane : lane + 128])
    return wide_all, wide_high, jnp.max(near, axis=0, keepdims=True), jnp.max(low, axis=0, keepdims=True)


def reply_rows(value, slot):
    groups = value.shape[1] // 128
    rows = [value[:, g * 128 : (g + 1) * 128] for g in range(groups)]
    rest = jnp.concatenate(rows + [jnp.zeros((8 - groups, 128), F32)], axis=0)
    pieces = []
    for _ in range(3):
        pieces.append(rest.astype(BF))
        rest = rest - pieces[-1].astype(F32)
    pieces = jnp.concatenate(pieces, axis=0).astype(F32)
    return pieces, jnp.where((slot >> 7) == iota((8, SLOTS), 0), 1.0, 0.0)


def reply_to(value_all, value_high, slot):
    pieces_all, group = reply_rows(value_all, slot)
    pieces_high, _ = reply_rows(value_high, slot)
    pieces = jnp.concatenate([pieces_all, pieces_high], axis=0).astype(BF)
    pick = (iota((128, SLOTS), 0) == (slot & 127)).astype(BF)
    lines = dot(pieces, pick)
    row = iota((8, SLOTS), 0)
    out = []
    for which in range(2):
        line = lines[which * 24 : which * 24 + 8] + lines[which * 24 + 8 : which * 24 + 16] + lines[which * 24 + 16 : which * 24 + 24]
        found = jnp.sum(line * group, axis=0, keepdims=True)
        out.append(jnp.where(row == 4 * which, found, 0.0))
    return out + [jnp.zeros((8, SLOTS), F32)]


def mate_kernel(own_ref, mate_ref, local_ref, out_ref):
    own, mate = read_meta(own_ref, ROWS), read_meta(mate_ref, ROWS)
    mine, theirs = [], None
    for half in range(2):
        rows = own_ref[half * HALF : (half + 1) * HALF, :]
        keys, (found,) = meet(rows, ids_of(own, half * HALF, half * HALF + HALF), [(mate_ref, ROWS, *mate[:2])])
        mine.append(keys)
        theirs = found if theirs is None else both(theirs, found)
    mine = [jnp.concatenate([mine[0][i], mine[1][i]], axis=1) for i in range(2)]
    mine = both(mine, (local_ref[0:1, :], local_ref[1:2, :]))
    out_ref[...] = jnp.concatenate([*mine, *theirs, jnp.full((4, ROWS), -1.0, F32)], axis=0)


def far_first_kernel(key_ref, own_ref, mate_ref, tail_ref, near_ref, out_ref):
    own, mate = read_meta(own_ref, ROWS), read_meta(mate_ref, ROWS)
    key, tail = read_meta(key_ref, EARLY), read_meta(tail_ref, HALF)
    keys, (tails, mates, owns) = meet(
        key_ref[:EARLY, :],
        ids_of(key, 0, EARLY),
        [(tail_ref, HALF, *ids_of(tail, HALF, ROWS)), (mate_ref, ROWS, *mate[:2]), (own_ref, ROWS, *own[:2])],
    )
    owns = both(owns, (near_ref[0:1, :], near_ref[1:2, :]))
    mates = both(mates, (near_ref[2:3, :], near_ref[3:4, :]))
    lines = [jnp.concatenate([keys[i], jnp.zeros((1, ROWS - EARLY), F32)], axis=1) for i in range(2)]
    lines += [jnp.concatenate([tails[i], jnp.zeros((1, HALF), F32)], axis=1) for i in range(2)]
    out_ref[...] = jnp.concatenate([*owns, *mates, *lines], axis=0)


def far_second_kernel(key_ref, own_ref, mate_ref, early_ref, tail_ref, first_ref, out_ref, by_slot):
    own, mate = read_meta(own_ref, ROWS), read_meta(mate_ref, ROWS)
    key, tail = read_meta(early_ref, EARLY), read_meta(tail_ref, HALF)
    keys, (mates, owns) = meet(
        key_ref[...], ids_of(key, EARLY, ROWS), [(mate_ref, ROWS, *mate[:2]), (own_ref, ROWS, *own[:2])]
    )
    line = [first_ref[i : i + 1, :] for i in range(8)]
    owns, mates = both(owns, line[0:2]), both(mates, line[2:4])
    keys = [jnp.concatenate([line[4 + i][:, :EARLY], keys[i]], axis=1) for i in range(2)]
    tails = [line[6 + i][:, :HALF] for i in range(2)]
    rows = []
    for part, slot in ((owns, own[2]), (mates, mate[2]), (keys, key[2]), (tails, tail[2] - HALF)):
        rows += reply_to(*part, slot)
    rows.append(jnp.zeros((32, SLOTS), F32))
    by_slot[...] = jnp.transpose(jnp.concatenate(rows, axis=0))
    reply = by_slot[pl.ds(0, DEVICES, stride=8), :]
    for order in range(1, 8):
        reply = reply + pltpu.roll(by_slot[pl.ds(order, DEVICES, stride=8), :], order, 1)
    out_ref[...] = reply + pltpu.roll(by_slot[MAIN:, :], 8, 1)


def answer_kernel(got_ref, route_ref, all_ref, high_ref):
    within = route_ref[4:5, :]
    replies = jnp.transpose(got_ref[...])
    row = iota((24, ROWS), 0)
    best = None
    for role in range(ROLES):
        rest = replies[role * 24 : role * 24 + 24]
        pieces = []
        for _ in range(3):
            pieces.append(rest.astype(BF).astype(F32))
            rest = rest - pieces[-1]
        sender = route_ref[role : role + 1, :]
        lines = dot(jnp.concatenate(pieces, axis=0).astype(BF), (iota((DEVICES, ROWS), 0) == sender).astype(BF))
        lines = jnp.where(sender >= 0, lines[0:24] + lines[24:48] + lines[48:72], -1.0)
        best = lines if best is None else jnp.maximum(best, lines)
    all_ref[...] = jnp.sum(jnp.where(row == within, best, 0.0), axis=0, keepdims=True).reshape(ROWS)
    high_ref[...] = jnp.sum(jnp.where(row == within + 12, best, 0.0), axis=0, keepdims=True).reshape(ROWS)


def call(kernel, out, args, scratch=(), flops=0, name=None, left=(), grant=48):
    moved = sum(a.size * a.dtype.itemsize for a in args)
    many = isinstance(out, list)
    shapes = [jax.ShapeDtypeStruct(*o) for o in (out if many else [out])]
    out_specs = [pl.BlockSpec(memory_space=pltpu.VMEM)] * len(shapes)
    return pl.pallas_call(
        kernel,
        out_shape=shapes if many else shapes[0],
        in_specs=[pl.BlockSpec(memory_space=pl.ANY if i in left else pltpu.VMEM) for i in range(len(args))],
        out_specs=out_specs if many else out_specs[0],
        scratch_shapes=list(scratch),
        compiler_params=pltpu.CompilerParams(vmem_limit_bytes=grant * 1024 * 1024),
        cost_estimate=pl.CostEstimate(flops=flops, bytes_accessed=moved, transcendentals=0),
        name=name,
    )(*args)


def body(embeddings, cluster_id, cluster_rank, dest_slot):
    send, route = call(
        pack_kernel,
        [((MAIN, ROWS + 128), BF), ((8, ROWS), jnp.int32)],
        (embeddings, cluster_id, cluster_rank, dest_slot),
        (
            pltpu.VMEM((ROWS, ROWS), BF),
            pltpu.VMEM((ROWS,), jnp.int32),
            pltpu.VMEM((ROWS,), jnp.int32),
            pltpu.VMEM((ROWS,), jnp.int32),
            pltpu.VMEM((ROWS, ROWS), BF),
            pltpu.VMEM((MAIN, 128), F32),
            pltpu.SemaphoreType.DMA((6,)),
        ),
        name="pack",
        left=(0, 1, 2, 3),
        grant=60,
    )
    got = lax.all_to_all(send, AXES, split_axis=0, concat_axis=0, tiled=True)
    own, first = call(
        unpack_kernel,
        [((ROWS + META, ROWS), BF), ((EARLY + META, ROWS), BF)],
        (got,),
        (pltpu.VMEM((MAIN, 128), F32), pltpu.VMEM((MAIN, 128), F32)),
        name="unpack",
    )
    mate = lax.ppermute(own, AXES, shift(-1))
    key1 = lax.ppermute(first, AXES, shift(2))
    tail = lax.ppermute(own[HALF:], AXES, shift(-2))
    key2 = lax.ppermute(own[EARLY:ROWS], AXES, shift(2))
    tile = 2 * ROWS**3
    local = call(local_kernel, ((8, ROWS), F32), (own,), flops=tile, name="local")
    near = call(mate_kernel, ((8, ROWS), F32), (own, mate, local), flops=tile, name="mate")
    lines = call(far_first_kernel, ((8, ROWS), F32), (key1, own, mate, tail, near), flops=tile, name="far_first")
    reply = call(
        far_second_kernel,
        ((DEVICES, 128), F32),
        (key2, own, mate, key1, tail, lines),
        (pltpu.VMEM((SLOTS, 128), F32),),
        flops=tile,
        name="far_second",
    )
    answer = lax.all_to_all(reply.reshape(DEVICES, 1, 128), AXES, split_axis=0, concat_axis=0, tiled=True)
    return call(answer_kernel, [((ROWS,), F32)] * 2, (answer.reshape(DEVICES, 128), route), name="answer")


def solution(mesh):
    rows = P(AXES)
    return jax.shard_map(
        body,
        mesh=mesh,
        in_specs=(P(AXES, None), rows, rows, rows),
        out_specs=(rows, rows),
        check_vma=False,
    )
```
